128 devices in a mesh: dp: 8 (over x, core), fsdp: 16 (over z, y).
Axes of the slice: x: 4, y: 4, z: 4, core: 2. Of those that a mesh axis runs over, the one named last changes fastest.
Arguments:
- replica_grads: bfloat16 [8, 2048, 16384], P('dp', 'fsdp'), may hold values from -240 to 240
- owners: int32 [8, 16], P('dp'), may hold values from 0 to 31, as said below
- left_factor: float32 [8, 32, 512, 512], P('dp', 'fsdp'), may hold values from -30 to 30
- right_factor: float32 [8, 32, 512, 512], P('dp', 'fsdp'), may hold values from -30 to 30
- left_basis: float32 [8, 32, 512, 512], P('dp', 'fsdp'), may hold values from -0.25 to 0.25
- right_basis: float32 [8, 32, 512, 512], P('dp', 'fsdp'), may hold values from -0.25 to 0.25
- first_moment: float32 [8, 32, 512, 512], P('dp', 'fsdp'), may hold values from -2 to 2
- second_moment: float32 [8, 32, 512, 512], P('dp', 'fsdp'), may hold values from 0.1 to 2
Outputs:
- update: bfloat16 [2048, 16384], P('fsdp', 'dp')
- new_left: float32 [8, 32, 512, 512], P('dp', 'fsdp')
- new_right: float32 [8, 32, 512, 512], P('dp', 'fsdp')
- new_first: float32 [8, 32, 512, 512], P('dp', 'fsdp')
- new_second: float32 [8, 32, 512, 512], P('dp', 'fsdp')
The draws below stay inside these ranges and needn't reach their ends.
Inputs may be any that keep to these rules, and one draw needn't show every extreme that they name: owners[d, b] = o * 2 + s names slot s of owner o along fsdp within replica group d; the entries of one row are distinct, and in every row some owner has all 2 of its slots named.
All inputs are finite; a program needn't handle non-finite values.
Results may differ from the reference program's by a relative error of at most 0.012.
Values may be sent and summed in bfloat16 or wider, within the bound.
No kernel may reach another device: no remote copies, remote signals or barrier semaphores. Data moves between devices by JAX's collectives and lax.ppermute only.
A program may use at most 128 MiB of HBM per device.

```python
import math
import jax
import jax.numpy as jnp
from jax import lax

D = 2048
BLOCK = 512
COLB = 4
SLOTS = 2
COLS = 16384
NS = 32
N_DP = 8
N_FSDP = 16


def draw_owners(key, part):
    key = jax.random.fold_in(key, 11)
    slot_total = N_FSDP * SLOTS
    block_count = D // BLOCK * COLB

    def one_group(group_key):
        first_key, second_key = jax.random.split(group_key)
        shuffled = jax.random.permutation(first_key, slot_total).astype(jnp.int32)
        full_owner = shuffled[0] // SLOTS
        position = jnp.arange(slot_total, dtype=jnp.int32)
        is_full = (shuffled // SLOTS == full_owner).astype(jnp.int32)
        order = jnp.argsort(is_full * slot_total + position, stable=True)
        remaining = shuffled[order]
        head_slots = full_owner * SLOTS + jnp.arange(SLOTS, dtype=jnp.int32)
        chosen = jnp.concatenate([head_slots, remaining[:block_count - SLOTS]])
        mixing = jax.random.permutation(second_key, block_count)
        return chosen[mixing].astype(jnp.int32)
    return jax.vmap(one_group)(jax.random.split(key, N_DP))


def draw_replica_grads(key, part):
    key = jax.random.fold_in(key, 5)
    noise_key = jax.random.fold_in(key, 0)
    column_key = jax.random.fold_in(key, 2)
    row_place = jnp.arange(D, dtype=jnp.float32) / D
    column_place = jnp.arange(COLS, dtype=jnp.float32) / COLS
    column_rough = jax.random.uniform(column_key, (COLS,), jnp.float32, 0.5, 1.0)
    base = jax.random.normal(noise_key, (N_DP, D, COLS), jnp.float32)
    row_scale = jnp.power(3.0, row_place)
    column_scale = jnp.power(3.0, column_place) * column_rough
    values = base * row_scale[None, :, None] * column_scale[None, None, :]
    return values.astype(jnp.bfloat16)


def steps_of(key, shape, pieces, smallest, top_value):
    level = 1.0
    for dim, parts in pieces:
        draws = jax.random.uniform(jax.random.fold_in(jax.random.fold_in(key, 6), dim), (parts,), jnp.float32, smallest / len(pieces), top_value / len(pieces))
        level = level * jnp.repeat(jnp.exp(draws), shape[dim] // parts).reshape((-1,) + (1,) * (len(shape) - 1 - dim))
    return level


def noise(key, shape, scale, reach, cuts=(), kind=jnp.bfloat16):
    drawn = scale * jax.random.normal(key, shape, jnp.float32)
    if cuts:
        drawn = drawn * steps_of(key, shape, cuts, -0.22, 0.18)
    return jnp.clip(drawn, -reach, reach).astype(kind)


def setup_inputs(seed: int = 0) -> dict:
    splits = jax.random.split(jax.random.key(seed), 9)
    replica_grads = draw_replica_grads(jax.random.fold_in(splits[8], 71), 0)
    owners = draw_owners(jax.random.fold_in(splits[8], 71), 0)
    left_factor = noise(splits[2], (N_DP, NS, BLOCK, BLOCK), 5.0, 30.0, ((0, 8), (1, 16)), jnp.float32)
    right_factor = noise(splits[3], (N_DP, NS, BLOCK, BLOCK), 5.0, 30.0, ((0, 8), (1, 16)), jnp.float32)
    left_basis = noise(splits[4], (N_DP, NS, BLOCK, BLOCK), BLOCK ** -0.5, 0.25, ((0, 8), (1, 16)), jnp.float32)
    right_basis = noise(splits[5], (N_DP, NS, BLOCK, BLOCK), BLOCK ** -0.5, 0.25, ((0, 8), (1, 16)), jnp.float32)
    first_moment = noise(splits[6], (N_DP, NS, BLOCK, BLOCK), 0.3, 2.0, ((0, 8), (1, 16)), jnp.float32)
    second_moment = jnp.clip(jnp.exp(math.log(2.0) - 2.9957323 * jax.random.uniform(splits[7], (N_DP, NS, BLOCK, BLOCK), jnp.float32) ** steps_of(splits[7], (N_DP, NS, BLOCK, BLOCK), ((0, 8), (1, 16)), -0.2, 0.2)), 0.1, 2.0)
    return dict(replica_grads=replica_grads, owners=owners, left_factor=left_factor, right_factor=right_factor, left_basis=left_basis, right_basis=right_basis, first_moment=first_moment, second_moment=second_moment)


full_precision = lax.Precision.HIGHEST

def soap_blocks(blocks, left_old, right_old, left_basis, right_basis, first_old, second_old):
    left_grad = jnp.einsum('sij,skj->sik', blocks, blocks, precision=full_precision)
    right_grad = jnp.einsum('sji,sjk->sik', blocks, blocks, precision=full_precision)
    left_new = 0.9 * left_old + 0.1 * left_grad
    right_new = 0.9 * right_old + 0.1 * right_grad
    half_rot = jnp.einsum('sji,sjk->sik', left_basis, blocks, precision=full_precision)
    rotated = jnp.einsum('sij,sjk->sik', half_rot, right_basis, precision=full_precision)
    first_new = 0.9 * first_old + 0.1 * blocks
    first_half = jnp.einsum('sji,sjk->sik', left_basis, first_new, precision=full_precision)
    first_rot = jnp.einsum('sij,sjk->sik', first_half, right_basis, precision=full_precision)
    second_new = 0.95 * second_old + 0.05 * rotated * rotated
    direction = first_rot / (jnp.sqrt(second_new) + 1e-08)
    back_half = jnp.einsum('sij,sjk->sik', left_basis, direction, precision=full_precision)
    block_update = jnp.einsum('sij,skj->sik', back_half, right_basis, precision=full_precision)
    return (block_update.astype(jnp.bfloat16), left_new, right_new, first_new, second_new)

def reference(replica_grads, owners, left_factor, right_factor, left_basis, right_basis, first_moment, second_moment):
    grad_sum = lax.optimization_barrier(jnp.sum(replica_grads.astype(jnp.float32), axis=0))
    mean_square = jnp.sum(grad_sum * grad_sum) / (D * COLS)
    clip_factor = jnp.minimum(1.0, 1.0 / jnp.sqrt(mean_square + 1e-06))
    grouped = grad_sum.reshape(D // BLOCK, BLOCK, N_DP, COLB, BLOCK).transpose(2, 0, 3, 1, 4)
    grouped = grouped.reshape(N_DP, D // BLOCK * COLB, BLOCK, BLOCK) * clip_factor

    def update_group(inputs):
        blocks, slot_table, left_all, right_all, lbasis_all, rbasis_all, first_all, second_all = inputs
        picked = [state[slot_table] for state in (left_all, right_all, lbasis_all, rbasis_all, first_all, second_all)]
        block_update, left_new, right_new, first_new, second_new = soap_blocks(blocks, *picked)
        return (block_update, left_all.at[slot_table].set(left_new), right_all.at[slot_table].set(right_new), first_all.at[slot_table].set(first_new), second_all.at[slot_table].set(second_new))
    block_update, new_left, new_right, new_first, new_second = lax.map(update_group, (grouped, owners, left_factor, right_factor, left_basis, right_basis, first_moment, second_moment))
    update = block_update.reshape(N_DP, D // BLOCK, COLB, BLOCK, BLOCK).transpose(1, 3, 0, 2, 4).reshape(D, COLS)
    return (update, new_left, new_right, new_first, new_second)
```

```python
import jax
import jax.numpy as jnp
from jax import lax
from jax.experimental import pallas as pl
from jax.experimental.pallas import tpu as pltpu
from jax.sharding import PartitionSpec as P

f32 = jnp.float32
bf16 = jnp.bfloat16
SMEM = pltpu.MemorySpace.SMEM
VMEM = pltpu.MemorySpace.VMEM
HBM = pltpu.MemorySpace.HBM
LANES = 128


def in_hbm(*arrays):
    return [pltpu.with_memory_space_constraint(a, HBM) for a in arrays]


def split3(value):
    head, rest = split(value)
    mid, tail = split(value - head.astype(f32))
    return head, mid, tail


def split(value):
    head = value.astype(bf16)
    return head, (value - head.astype(f32)).astype(bf16)


def mm(a, b, dims=((1,), (0,))):
    return lax.dot_general(a, b, (dims, ((), ())), preferred_element_type=f32)


def mm3(a, b, dims=((1,), (0,))):
    return mm(a[0], b[0], dims) + (mm(a[0], b[1], dims) + mm(a[1], b[0], dims))


def prepare_body(left_ref, right_ref, first_ref, lt_h, lt_l, l_h, r_h, r_l, rot_ref):
    left = left_ref[0]
    left_t = left.T
    left_t_split = split(left_t)
    right_split = split(right_ref[0])
    lt_h[0], lt_l[0] = left_t_split
    l_h[0] = left.astype(bf16)
    r_h[0], r_l[0] = right_split
    half = mm3(left_t_split, split(first_ref[0]))
    rot_ref[0] = 0.9 * mm3(split(half), right_split)


def prepare(left_basis, right_basis, first_moment):
    slots, n, _ = left_basis.shape
    block = pl.BlockSpec((1, n, n), lambda s: (s, 0, 0))
    half = HBM((slots, n, n), bf16)
    return pl.pallas_call(
        prepare_body,
        grid=(slots,),
        in_specs=[block] * 3,
        out_specs=[block] * 6,
        out_shape=[half] * 5 + [HBM((slots, n, n), f32)],
        compiler_params=pltpu.CompilerParams(vmem_limit_bytes=32 << 20),
        cost_estimate=pl.CostEstimate(
            flops=slots * 12 * n**3, bytes_accessed=slots * 26 * n * n, transcendentals=0
        ),
        name="prepare",
    )(*in_hbm(left_basis, right_basis, first_moment))


def local(body, arrays, out_shape, name, limit=8 << 20):
    return pl.pallas_call(
        body,
        in_specs=[pl.BlockSpec(memory_space=SMEM)]
        + [pl.BlockSpec(memory_space=VMEM)] * (len(arrays) - 1),
        out_specs=jax.tree.map(lambda _: pl.BlockSpec(memory_space=VMEM), out_shape),
        out_shape=out_shape,
        compiler_params=pltpu.CompilerParams(vmem_limit_bytes=limit),
        name=name,
    )(*arrays)


def dispatch_body(table, *refs):
    *srcs, dst, square = refs
    n = dst.shape[2]
    bands = len(srcs)
    width = srcs[0].shape[1] - LANES
    cols = width // n
    z = table[0, bands * cols]
    total = jnp.zeros(square.shape, f32)
    for j, src in enumerate(srcs):
        band = lax.rem(z + bands - j, bands)
        for c in range(cols):
            dst[table[0, band * cols + c]] = src[:, c * n : (c + 1) * n]
        terms = src[:, width:].astype(f32)
        for t in range(3):
            total = total + terms[8 * t : 8 * t + 8]
    square[...] = total


def collect_body(table, src, *dsts):
    n = src.shape[2]
    bands = len(dsts)
    cols = dsts[0].shape[1] // n
    z = table[0, bands * cols]
    for j, dst in enumerate(dsts):
        band = lax.rem(z + j, bands)
        for c in range(cols):
            dst[:, c * n : (c + 1) * n] = src[table[0, band * cols + c]]


def put_body(table, *refs):
    *srcs, dst = refs
    bands = len(srcs)
    z = table[0, table.shape[1] - 1]
    for j, src in enumerate(srcs):
        dst[lax.rem(z + bands - j, bands)] = src[...]


def plus_body(table, *refs):
    total = refs[0][...]
    for ref in refs[1:-1]:
        total = total + ref[...]
    refs[-1][...] = total


def slabs(place, src, core, dst, sems, steps, chips, width):
    return [
        pltpu.make_async_copy(
            src.at[
                :,
                pl.ds(
                    pl.multiple_of((2 * lax.rem(place[0] + j, chips) + core) * width, width),
                    width,
                ),
            ],
            dst.at[i],
            sems.at[i],
        )
        for i, j in enumerate(steps)
    ]


def pick(place, grads, steps, width):
    rows, columns = grads.shape
    chips = columns // width // 2

    def body(place, src, dst, sems):
        copies = slabs(place, src, 1 - place[1], dst, sems, steps, chips, width)
        for c in copies:
            c.start()
        for c in copies:
            c.wait()

    return pl.pallas_call(
        body,
        in_specs=[pl.BlockSpec(memory_space=SMEM), pl.BlockSpec(memory_space=HBM)],
        out_specs=pl.BlockSpec(memory_space=VMEM),
        out_shape=jax.ShapeDtypeStruct((len(steps), rows, width), bf16),
        scratch_shapes=[pltpu.SemaphoreType.DMA((len(steps),))],
        compiler_params=pltpu.CompilerParams(vmem_limit_bytes=4 << 20),
        name="pick",
    )(place, *in_hbm(grads))


def pair(body, place, grads, other, steps, width, outs, name):
    rows, columns = grads.shape
    chips = columns // width // 2
    low = rows // 2

    def run(place, src, far, *refs):
        *outs, near, sems = refs
        copies = slabs(place, src, place[1], near, sems, steps, chips, width)
        for c in copies:
            c.start()

        def total(i, a):
            if a == 0:
                copies[i].wait()
            part = slice(a * low, (a + 1) * low)
            return near[i, part].astype(f32) + far[i, part].astype(f32)

        body(total, low, *outs)

    return pl.pallas_call(
        run,
        in_specs=[
            pl.BlockSpec(memory_space=SMEM),
            pl.BlockSpec(memory_space=HBM),
            pl.BlockSpec(memory_space=VMEM),
        ],
        out_specs=[pl.BlockSpec(memory_space=VMEM)] * len(outs),
        out_shape=[jax.ShapeDtypeStruct(shape, kind) for shape, kind in outs],
        scratch_shapes=[
            pltpu.VMEM((len(steps), rows, width), bf16),
            pltpu.SemaphoreType.DMA((len(steps),)),
        ],
        compiler_params=pltpu.CompilerParams(vmem_limit_bytes=8 << 20),
        name=name,
    )(place, *in_hbm(grads), other)


def far_body(total, low, to_right, to_left):
    to_right[...] = total(0, 0).astype(bf16)
    to_left[...] = total(0, 1).astype(bf16)


def near_body(total, low, to_right, to_left, keep_right, keep_left, own):
    keep_right[...] = total(0, 0)
    to_right[...] = total(0, 1).astype(bf16)
    to_left[...] = total(1, 0).astype(bf16)
    keep_left[...] = total(1, 1)
    for a in range(2):
        own[a * low : (a + 1) * low] = total(2, a)


def relay(place, kept, arrived):
    def body(place, kept, arrived, out):
        out[...] = (kept[...] + arrived[...].astype(f32)).astype(bf16)

    out = jax.ShapeDtypeStruct(kept.shape, bf16)
    return local(body, (place, kept, arrived), out, "relay")


def finish(place, own, left_direct, right_direct, left_sum, right_sum, bands):
    rows, width = own.shape
    low = rows // 2
    piece = rows // bands

    def body(place, own, left_direct, right_direct, left_sum, right_sum, *outs):
        total = jnp.zeros((8, LANES), f32)
        for q in range(bands):
            near, far = (left_sum, right_direct) if q * piece < low else (left_direct, right_sum)
            part = slice(q * piece % low, q * piece % low + piece)
            value = own[q * piece : (q + 1) * piece] + (
                near[part].astype(f32) + far[part].astype(f32)
            )
            step = lax.rem(q - place[2] + bands, bands)
            rounded = value.astype(bf16)
            for j in range(bands):

                @pl.when(step == j)
                def _():
                    outs[j][:, :width] = rounded

            by_row = jnp.sum((value * value).reshape(piece // 8, 8, width), axis=0)
            for c in range(width // LANES):
                total = total + by_row[:, c * LANES : (c + 1) * LANES]
        terms = [t.astype(f32) for t in split3(total)]
        terms.append(jnp.zeros((piece - 24, LANES), f32))
        terms = jnp.concatenate(terms, axis=0).astype(bf16)
        for out in outs:
            out[:, width:] = terms

    arrays = [place, own, left_direct, right_direct, left_sum, right_sum]
    out = [jax.ShapeDtypeStruct((piece, width + LANES), bf16)] * bands
    return local(body, arrays, out, "finish", 12 << 20)


def sum_over_replicas(place, grads, bands):
    size = lax.axis_size("dp")
    rows, columns = grads.shape
    width = columns // size
    half = (rows // 2, width)
    swap = [(d, d ^ 1) for d in range(size)]
    up = [(d, (d + 2) % size) for d in range(size)]
    down = [(d, (d - 2) % size) for d in range(size)]
    other = lax.ppermute(pick(place, grads, (2,), width), "dp", swap)
    others = lax.ppermute(pick(place, grads, (1, 3, 0), width), "dp", swap)
    to_right, to_left = pair(
        far_body, place, grads, other, (2,), width, [(half, bf16)] * 2, "pair_far"
    )
    left_far = lax.ppermute(to_right, "dp", up)
    right_far = lax.ppermute(to_left, "dp", down)
    outs = [(half, bf16)] * 2 + [(half, f32)] * 2 + [((rows, width), f32)]
    to_right, to_left, keep_right, keep_left, own = pair(
        near_body, place, grads, others, (1, 3, 0), width, outs, "pair_near"
    )
    left_direct = lax.ppermute(to_right, "dp", up)
    right_direct = lax.ppermute(to_left, "dp", down)
    left_sum = lax.ppermute(relay(place, keep_right, left_far), "dp", up)
    right_sum = lax.ppermute(relay(place, keep_left, right_far), "dp", down)
    return own, left_direct, right_direct, left_sum, right_sum


def exchange(arrays, steps):
    order = sorted(range(1, len(arrays)), key=lambda j: -min(j, len(arrays) - j))
    got = {0: arrays[0]}
    for j in order:
        got[j] = lax.ppermute(arrays[j], *steps[j - 1])
    return [got[j] for j in range(len(arrays))]


def add_up(place, value, steps):
    arrived = [lax.ppermute(value, axis, perm) for axis, perm in steps]
    return local(plus_body, [place, value] + arrived, jax.ShapeDtypeStruct(value.shape, f32), "plus")


def assemble(pieces_ref, slot, bands):
    senders = pieces_ref.shape[0]
    per = senders // bands
    return jnp.concatenate(
        [pieces_ref[z * per + y, slot] for y in range(per) for z in range(bands)], axis=0
    )


def is_named(table, slot):
    named = table[0, 0] == slot
    for b in range(1, table.shape[1]):
        named = jnp.logical_or(named, table[0, b] == slot)
    return named


def clip_of(square, entries):
    total = jnp.sum(jnp.sum(square[...], axis=0, keepdims=True), axis=1, keepdims=True)
    return jnp.minimum(1.0, 1.0 / jnp.sqrt(total / entries + 1e-06))


def direction_body(
    bands, entries, table, me, square, pieces, second, *refs
):
    states, (out, second_out), scratch = refs[:6], refs[6:8], refs[8:]
    *bufs, old, new, sems, out_sems = scratch
    slots = second.shape[0]
    sources = (*states[:2], *states[3:5], states[5], second, states[2])
    targets = (*bufs[:2], *bufs[3:5], bufs[5], old, bufs[2])
    copies = [
        [
            pltpu.make_async_copy(src.at[s], dst.at[s], sems.at[s, i])
            for i, (src, dst) in enumerate(zip(sources, targets))
        ]
        for s in range(slots)
    ]
    for group in copies:
        for c in group:
            c.start()
    lt_h, lt_l, l_h, r_h, r_l, rot = bufs
    scale = clip_of(square, entries)
    senders, rows, n = pieces.shape[0], pieces.shape[2], pieces.shape[3]
    per = senders // bands
    for s in range(slots):
        wait = [c.wait for c in copies[s]]
        block = assemble(pieces, s, bands)
        wait[0]()
        wait[1]()
        half = mm(lt_h[s], block) + mm(lt_l[s], block)
        wait[2]()
        wait[3]()
        rotated = mm3(split(half), (r_h[s], r_l[s])) * scale
        wait[4]()
        wait[5]()
        value = 0.95 * old[s] + 0.05 * rotated * rotated
        step = (rot[s] + 0.1 * rotated) / (jnp.sqrt(value) + 1e-08)
        named = is_named(table, me[0] * slots + s)
        new[s] = jnp.where(named, value, old[s])
        pltpu.make_async_copy(new.at[s], second_out.at[s], out_sems.at[s]).start()
        wait[6]()
        back = mm(l_h[s], step.astype(bf16))
        update = mm(back.astype(bf16), r_h[s], ((1,), (1,))).astype(bf16)
        for y in range(per):
            for z in range(bands):
                row = (y * bands + z) * rows
                out[z * per + y, s] = update[row : row + rows]
    for s in range(slots):
        pltpu.make_async_copy(new.at[s], second_out.at[s], out_sems.at[s]).wait()


def direction(table, me, square, pieces, prepared, second, bands, entries):
    slots, n, _ = second.shape
    scalar = pl.BlockSpec(memory_space=SMEM)
    whole = pl.BlockSpec(memory_space=VMEM)
    far = pl.BlockSpec(memory_space=HBM)

    def body(*refs):
        direction_body(bands, entries, *refs)

    return pl.pallas_call(
        body,
        in_specs=[scalar] * 2 + [whole] * 2 + [far] * 7,
        out_specs=[whole, far],
        out_shape=[
            jax.ShapeDtypeStruct(pieces.shape, bf16),
            HBM(second.shape, f32),
        ],
        scratch_shapes=[pltpu.VMEM((slots, n, n), bf16)] * 5
        + [pltpu.VMEM((slots, n, n), f32)] * 3
        + [pltpu.SemaphoreType.DMA((slots, 7)), pltpu.SemaphoreType.DMA((slots,))],
        compiler_params=pltpu.CompilerParams(vmem_limit_bytes=32 << 20),
        name="direction",
    )(table, me, square, pieces, *in_hbm(second, *prepared))


def factors_body(bands, entries, table, me, clip, pieces, left, right, first, left_out, right_out, first_out):
    slot = me[0] * pl.num_programs(0) + pl.program_id(0)
    scale = clip_of(clip, entries)
    s = assemble(pieces, pl.program_id(0), bands)
    named = is_named(table, slot)
    square = 0.1 * scale * scale
    left_out[0] = jnp.where(named, 0.9 * left[0] + square * mm(s, s, ((1,), (1,))), left[0])
    right_out[0] = jnp.where(named, 0.9 * right[0] + square * mm(s.T, s), right[0])
    first_out[0] = jnp.where(named, 0.9 * first[0] + (0.1 * scale) * s.astype(f32), first[0])


def factors(table, me, clip, pieces, left, right, first, bands, entries):
    slots, n, _ = left.shape
    block = pl.BlockSpec((1, n, n), lambda s: (s, 0, 0))
    scalar = pl.BlockSpec(memory_space=SMEM)
    whole = pl.BlockSpec(memory_space=VMEM)

    def body(*refs):
        factors_body(bands, entries, *refs)

    return pl.pallas_call(
        body,
        grid=(slots,),
        in_specs=[scalar] * 2 + [whole] * 2 + [block] * 3,
        out_specs=[block] * 3,
        out_shape=[HBM(left.shape, f32)] * 3,
        compiler_params=pltpu.CompilerParams(vmem_limit_bytes=32 << 20),
        cost_estimate=pl.CostEstimate(
            flops=slots * 4 * n**3, bytes_accessed=slots * 26 * n * n, transcendentals=0
        ),
        name="factors",
    )(table, me, clip, pieces, *in_hbm(left, right, first))


def per_device(
    replica_grads,
    owners,
    left_factor,
    right_factor,
    left_basis,
    right_basis,
    first_moment,
    second_moment,
):
    rows_dev = replica_grads.shape[1]
    shards = lax.axis_size("fsdp")
    slots, n = left_factor.shape[1:3]
    per_band = n // rows_dev
    bands = shards // per_band
    dp = lax.axis_size("dp")
    dp_me = lax.axis_index("dp").astype(jnp.int32)
    me = lax.axis_index("fsdp").astype(jnp.int32)
    place = jnp.stack([dp_me // 2, dp_me % 2, me // per_band])
    table = jnp.concatenate([owners, (me // per_band).reshape(1, 1)], axis=1)
    me = me.reshape(1)
    core = [("dp", [(d, d ^ 1) for d in range(dp)])]
    along_x = [("dp", [(d, (d + 2 * h) % dp) for d in range(dp)]) for h in range(1, dp // 2)]
    along_y = [
        ("fsdp", [(i, i // per_band * per_band + (i + h) % per_band) for i in range(shards)])
        for h in range(1, per_band)
    ]
    along_z = [
        ("fsdp", [(i, (i + h * per_band) % shards) for i in range(shards)])
        for h in range(1, bands)
    ]
    prepared = prepare(left_basis[0], right_basis[0], first_moment[0])
    parts = sum_over_replicas(place, replica_grads[0], bands)
    parts, prepared = lax.optimization_barrier((parts, prepared))
    sums = finish(place, *parts, bands)
    rows = sums[0].shape[0]
    width = sums[0].shape[1] - LANES
    cols = width // n
    entries = rows_dev * shards * replica_grads.shape[2]
    spread = exchange(sums, along_z)
    out = [
        jax.ShapeDtypeStruct((shards * slots, rows, n), bf16),
        jax.ShapeDtypeStruct((8, LANES), f32),
    ]
    sent, square = local(dispatch_body, [table, *spread], out, "dispatch")
    pieces = lax.all_to_all(
        sent.reshape(shards, slots, rows, n), "fsdp", split_axis=0, concat_axis=0, tiled=True
    )
    for steps in (core, along_x, along_y):
        square = add_up(place, square, steps)
    update, second_new = direction(
        owners, me, square, pieces, prepared, second_moment[0], bands, entries
    )
    back = lax.all_to_all(update, "fsdp", split_axis=0, concat_axis=0, tiled=True)
    new = factors(
        owners, me, square, pieces, left_factor[0], right_factor[0], first_moment[0], bands, entries
    )
    back, new = lax.optimization_barrier((back, new))
    left_new, right_new, first_new = new
    out = [jax.ShapeDtypeStruct((rows, width), bf16)] * bands
    mine = local(collect_body, [table, back.reshape(shards * slots, rows, n)], out, "collect")
    out = jax.ShapeDtypeStruct((bands, rows, width), bf16)
    result = local(put_body, [table, *exchange(mine, along_z)], out, "put").reshape(rows_dev, width)
    return (result, left_new[None], right_new[None], first_new[None], second_new[None])


def solution(mesh):
    state = P("dp", "fsdp", None, None)
    return jax.shard_map(
        per_device,
        mesh=mesh,
        in_specs=(P("dp", "fsdp", None), P("dp", None)) + (state,) * 6,
        out_specs=(P("fsdp", "dp"),) + (state,) * 4,
        check_vma=False,
    )
```

```python
import jax
import jax.numpy as jnp
from jax import lax
from jax.experimental import pallas as pl
from jax.experimental.pallas import tpu as pltpu
from jax.sharding import PartitionSpec as P

f32 = jnp.float32
bf16 = jnp.bfloat16
SMEM = pltpu.MemorySpace.SMEM
VMEM = pltpu.MemorySpace.VMEM
HBM = pltpu.MemorySpace.HBM
LANES = 128


def in_hbm(*arrays):
    return [pltpu.with_memory_space_constraint(a, HBM) for a in arrays]


def split3(value):
    head, rest = split(value)
    mid, tail = split(value - head.astype(f32))
    return head, mid, tail


def split(value):
    head = value.astype(bf16)
    return head, (value - head.astype(f32)).astype(bf16)


def mm(a, b, dims=((1,), (0,))):
    return lax.dot_general(a, b, (dims, ((), ())), preferred_element_type=f32)


def tiles(count, size=32):
    return [slice(r, r + size) for r in range(0, count, size)]


def prepare_body(left_ref, right_ref, first_ref, lt_ref, l_ref, r_ref, rot_ref, half, product):
    n = left_ref.shape[1]
    for rows in tiles(n, LANES):
        head, tail = split(left_ref[0, rows].T)
        lt_ref[0, :n, rows] = head
        lt_ref[0, n:, rows] = tail
    for rows in tiles(n):
        l_ref[0, rows] = left_ref[0, rows].astype(bf16)
        head, tail = split(right_ref[0, rows])
        r_ref[0, rows, :n] = head
        r_ref[0, rows, n:] = tail
        half[rows] = first_ref[0, rows].astype(bf16)
    product[...] = mm(lt_ref[0], half[...])
    for rows, more in zip(tiles(n), tiles(2 * n)[n // 32 :]):
        half[rows] = (product[rows] + product[more]).astype(bf16)
    right = r_ref[0]
    rot_ref[0] = 0.9 * (mm(half[...], right[:, :n]) + mm(half[...], right[:, n:]))


def prepare(left_basis, right_basis, first_moment):
    slots, n, _ = left_basis.shape
    block = pl.BlockSpec((1, n, n), lambda s: (s, 0, 0))
    return pl.pallas_call(
        prepare_body,
        grid=(slots,),
        in_specs=[block] * 3,
        out_specs=[
            pl.BlockSpec((1, 2 * n, n), lambda s: (s, 0, 0)),
            block,
            pl.BlockSpec((1, n, 2 * n), lambda s: (s, 0, 0)),
            block,
        ],
        out_shape=[
            HBM((slots, 2 * n, n), bf16),
            HBM((slots, n, n), bf16),
            HBM((slots, n, 2 * n), bf16),
            HBM((slots, n, n), f32),
        ],
        scratch_shapes=[pltpu.VMEM((n, n), bf16), pltpu.VMEM((2 * n, n), f32)],
        compiler_params=pltpu.CompilerParams(vmem_limit_bytes=24 << 20),
        cost_estimate=pl.CostEstimate(
            flops=slots * 8 * n**3, bytes_accessed=slots * 26 * n * n, transcendentals=0
        ),
        name="prepare",
    )(*in_hbm(left_basis, right_basis, first_moment))


def local(body, arrays, out_shape, name, limit=8 << 20):
    return pl.pallas_call(
        body,
        in_specs=[pl.BlockSpec(memory_space=SMEM)]
        + [pl.BlockSpec(memory_space=VMEM)] * (len(arrays) - 1),
        out_specs=jax.tree.map(
            lambda _: pl.BlockSpec(memory_space=VMEM), out_shape, is_leaf=lambda o: hasattr(o, "shape")
        ),
        out_shape=out_shape,
        compiler_params=pltpu.CompilerParams(vmem_limit_bytes=limit),
        name=name,
    )(*arrays)


def dispatch_body(table, *refs):
    *squares, dst = refs[4:]
    srcs = refs[:4]
    n = dst.shape[2]
    rows, width = srcs[0].shape
    bands = len(srcs)
    cols = width // n
    slots = (dst.shape[1] - 8) // rows
    z = table[0, bands * cols]
    for j, src in enumerate(srcs):
        band = lax.rem(z + bands - j, bands)
        for c in range(cols):
            slot = table[0, band * cols + c]
            row = pl.multiple_of(lax.rem(slot, slots) * rows, rows)
            dst[slot // slots, pl.ds(row, rows)] = src[:, c * n : (c + 1) * n]
    total = squares[0][...]
    for square in squares[1:]:
        total = total + square[...]
    terms = [t.astype(f32) for t in split3(total)]
    terms.append(jnp.zeros((8, n - 3 * LANES), f32))
    terms = jnp.concatenate(terms, axis=1).astype(bf16)
    for o in range(dst.shape[0]):
        dst[o, slots * rows :] = terms


def collect_body(table, src, *dsts):
    n = src.shape[2]
    bands = len(dsts)
    cols = dsts[0].shape[1] // n
    z = table[0, bands * cols]
    for j, dst in enumerate(dsts):
        band = lax.rem(z + j, bands)
        for c in range(cols):
            dst[:, c * n : (c + 1) * n] = src[table[0, band * cols + c]]


def put_body(table, *refs):
    *srcs, dst = refs
    bands = len(srcs)
    z = table[0, table.shape[1] - 1]
    for j, src in enumerate(srcs):
        dst[lax.rem(z + bands - j, bands)] = src[...]


def plus_body(place, a, b, out):
    out[...] = a[...] + b[...]


def load(place, grads, width):
    rows, columns = grads.shape
    chips = columns // width // 2
    groups = ((2,), (1, 3, 0))

    def body(place, src, *refs):
        *dsts, sems = refs
        copies = []
        for i, dst in enumerate(dsts):
            core = 1 - place[1] if i < 2 else place[1]
            for k, j in enumerate(groups[i % 2]):
                slab = 2 * lax.rem(place[0] + j, chips) + core
                columns = pl.ds(pl.multiple_of(slab * width, width), width)
                copies.append(
                    pltpu.make_async_copy(src.at[:, columns], dst.at[k], sems.at[len(copies)])
                )
        for c in copies:
            c.start()
        for c in copies:
            c.wait()

    return pl.pallas_call(
        body,
        in_specs=[pl.BlockSpec(memory_space=SMEM), pl.BlockSpec(memory_space=HBM)],
        out_specs=[pl.BlockSpec(memory_space=VMEM)] * 4,
        out_shape=[VMEM((len(g), rows, width), bf16) for g in groups * 2],
        scratch_shapes=[pltpu.SemaphoreType.DMA((2 * chips,))],
        compiler_params=pltpu.CompilerParams(vmem_limit_bytes=2 << 20),
        name="load",
    )(place, *in_hbm(grads))


def pair(body, place, near, far, outs, name):
    low = near.shape[1] // 2

    def run(place, near, far, *outs):
        def total(i, a):
            part = slice(a * low, (a + 1) * low)
            return near[i, part].astype(f32) + far[i, part].astype(f32)

        body(total, low, *outs)

    out = [jax.ShapeDtypeStruct(shape, kind) for shape, kind in outs]
    return local(run, [place, near, far], out, name)


def far_body(total, low, to_right, to_left):
    to_right[...] = total(0, 0).astype(bf16)
    to_left[...] = total(0, 1).astype(bf16)


def near_body(total, low, to_right, to_left, keep_right, keep_left, own):
    keep_right[...] = total(0, 0)
    to_right[...] = total(0, 1).astype(bf16)
    to_left[...] = total(1, 0).astype(bf16)
    keep_left[...] = total(1, 1)
    for a in range(2):
        own[a * low : (a + 1) * low] = total(2, a)


def relay(place, kept, arrived):
    def body(place, kept, arrived, out):
        out[...] = (kept[...] + arrived[...].astype(f32)).astype(bf16)

    out = jax.ShapeDtypeStruct(kept.shape, bf16)
    return local(body, (place, kept, arrived), out, "relay")


def finish(place, own, left_direct, right_direct, left_sum, right_sum, bands):
    rows, width = own.shape
    low = rows // 2
    piece = rows // bands

    def body(place, own, left_direct, right_direct, left_sum, right_sum, *refs):
        *outs, square = refs
        total = jnp.zeros((8, LANES), f32)
        for q in range(bands):
            near, far = (left_sum, right_direct) if q * piece < low else (left_direct, right_sum)
            part = slice(q * piece % low, q * piece % low + piece)
            value = own[q * piece : (q + 1) * piece] + (
                near[part].astype(f32) + far[part].astype(f32)
            )
            step = lax.rem(q - place[2] + bands, bands)
            rounded = value.astype(bf16)
            for j in range(bands):

                @pl.when(step == j)
                def _():
                    outs[j][...] = rounded

            by_row = jnp.sum((value * value).reshape(piece // 8, 8, width), axis=0)
            for c in range(width // LANES):
                total = total + by_row[:, c * LANES : (c + 1) * LANES]
        square[...] = total

    arrays = [place, own, left_direct, right_direct, left_sum, right_sum]
    out = [jax.ShapeDtypeStruct((piece, width), bf16)] * bands
    out.append(jax.ShapeDtypeStruct((8, LANES), f32))
    return local(body, arrays, out, "finish", 12 << 20)


def sum_over_replicas(place, grads, bands):
    size = lax.axis_size("dp")
    rows, columns = grads.shape
    width = columns // size
    half = (rows // 2, width)
    swap = [(d, d ^ 1) for d in range(size)]
    up = [(d, (d + 2) % size) for d in range(size)]
    down = [(d, (d - 2) % size) for d in range(size)]
    far_there, near_there, far_here, near_here = load(place, grads, width)
    other = lax.ppermute(far_there, "dp", swap)
    other, near_there = lax.optimization_barrier((other, near_there))
    others = lax.ppermute(near_there, "dp", swap)
    to_right, to_left = pair(far_body, place, far_here, other, [(half, bf16)] * 2, "pair_far")
    left_far = lax.ppermute(to_right, "dp", up)
    right_far = lax.ppermute(to_left, "dp", down)
    outs = [(half, bf16)] * 2 + [(half, f32)] * 2 + [((rows, width), f32)]
    to_right, to_left, keep_right, keep_left, own = pair(
        near_body, place, near_here, others, outs, "pair_near"
    )
    left_direct = lax.ppermute(to_right, "dp", up)
    right_direct = lax.ppermute(to_left, "dp", down)
    left_sum = lax.ppermute(relay(place, keep_right, left_far), "dp", up)
    right_sum = lax.ppermute(relay(place, keep_left, right_far), "dp", down)
    return own, left_direct, right_direct, left_sum, right_sum


def exchange(arrays, steps):
    order = sorted(range(1, len(arrays)), key=lambda j: -min(j, len(arrays) - j))
    got = {0: arrays[0]}
    for j in order:
        got[j] = lax.ppermute(arrays[j], *steps[j - 1])
    return [got[j] for j in range(len(arrays))]


def assemble(pieces, slot, rows, bands):
    per = pieces.shape[0] // bands
    part = pl.ds(slot * rows, rows)
    return jnp.concatenate(
        [pieces[z * per + y, part] for y in range(per) for z in range(bands)], axis=0
    )


def is_named(table, slot):
    named = table[0, 0] == slot
    for b in range(1, table.shape[1]):
        named = jnp.logical_or(named, table[0, b] == slot)
    return named


def clip_of(pieces, entries):
    total = jnp.zeros((8, pieces.shape[2]), f32)
    for sender in range(pieces.shape[0]):
        total = total + pieces[sender, pieces.shape[1] - 8 :].astype(f32)
    total = jnp.sum(jnp.sum(total, axis=0, keepdims=True), axis=1, keepdims=True)
    return jnp.minimum(1.0, 1.0 / jnp.sqrt(total / entries + 1e-06))


def direction_body(bands, entries, table, me, pieces, second, *refs):
    lt_src, l_src, r_src, rot_src, out, second_out = refs[:6]
    lt, left, right, rot, old, new, half, product, step, sems, out_sems = refs[6:]
    slots, n, _ = second.shape
    sources, targets = (lt_src, r_src, rot_src, second, l_src), (lt, right, rot, old, left)
    copies = [
        [
            pltpu.make_async_copy(src.at[s], dst.at[s], sems.at[s, i])
            for i, (src, dst) in enumerate(zip(sources, targets))
        ]
        for s in range(slots)
    ]
    for group in copies:
        for c in group:
            c.start()
    scale = clip_of(pieces, entries)
    senders = pieces.shape[0]
    rows = n // senders
    per = senders // bands
    for s in range(slots):
        block = assemble(pieces, s, rows, bands)
        copies[s][0].wait()
        product[...] = mm(lt[s], block)
        for r, more in zip(tiles(n), tiles(2 * n)[n // 32 :]):
            half[r] = (product[r] + product[more]).astype(bf16)
        copies[s][1].wait()
        product[:n] = mm(half[...], right[s, :, :n])
        product[n:] = mm(half[...], right[s, :, n:])
        copies[s][2].wait()
        copies[s][3].wait()
        named = is_named(table, me[0] * slots + s)
        for r, more in zip(tiles(n), tiles(2 * n)[n // 32 :]):
            rotated = (product[r] + product[more]) * scale
            before = old[s, r]
            value = 0.95 * before + 0.05 * rotated * rotated
            new[s, r] = jnp.where(named, value, before)
            turned = rot[s, r] + 0.1 * rotated
            step[r] = (turned / (jnp.sqrt(value) + 1e-08)).astype(bf16)
        pltpu.make_async_copy(new.at[s], second_out.at[s], out_sems.at[s]).start()
        copies[s][4].wait()
        half[...] = mm(left[s], step[...]).astype(bf16)
        update = mm(half[...], right[s, :, :n], ((1,), (1,))).astype(bf16)
        for y in range(per):
            for z in range(bands):
                row = (y * bands + z) * rows
                out[z * per + y, s] = update[row : row + rows]
    for s in range(slots):
        pltpu.make_async_copy(new.at[s], second_out.at[s], out_sems.at[s]).wait()


def direction(table, me, pieces, prepared, second, bands, entries):
    slots, n, _ = second.shape
    senders = pieces.shape[0]
    scalar = pl.BlockSpec(memory_space=SMEM)
    whole = pl.BlockSpec(memory_space=VMEM)
    far = pl.BlockSpec(memory_space=HBM)

    def body(*refs):
        direction_body(bands, entries, *refs)

    return pl.pallas_call(
        body,
        in_specs=[scalar] * 2 + [whole] + [far] * 5,
        out_specs=[whole, far],
        out_shape=[
            jax.ShapeDtypeStruct((senders, slots, n // senders, n), bf16),
            HBM(second.shape, f32),
        ],
        scratch_shapes=[
            pltpu.VMEM((slots, 2 * n, n), bf16),
            pltpu.VMEM((slots, n, n), bf16),
            pltpu.VMEM((slots, n, 2 * n), bf16),
            pltpu.VMEM((slots, n, n), f32),
            pltpu.VMEM((slots, n, n), f32),
            pltpu.VMEM((slots, n, n), f32),
            pltpu.VMEM((n, n), bf16),
            pltpu.VMEM((2 * n, n), f32),
            pltpu.VMEM((n, n), bf16),
            pltpu.SemaphoreType.DMA((slots, 5)),
            pltpu.SemaphoreType.DMA((slots,)),
        ],
        compiler_params=pltpu.CompilerParams(vmem_limit_bytes=32 << 20),
        name="direction",
    )(table, me, pieces, *in_hbm(second, *prepared))


def factors_body(bands, entries, table, me, pieces, left, right, first, left_out, right_out, first_out):
    slot = me[0] * pl.num_programs(0) + pl.program_id(0)
    scale = clip_of(pieces, entries)
    s = assemble(pieces, pl.program_id(0), left.shape[1] // pieces.shape[0], bands)
    named = is_named(table, slot)
    square = 0.1 * scale * scale
    left_out[0] = jnp.where(named, 0.9 * left[0] + square * mm(s, s, ((1,), (1,))), left[0])
    right_out[0] = jnp.where(named, 0.9 * right[0] + square * mm(s.T, s), right[0])
    first_out[0] = jnp.where(named, 0.9 * first[0] + (0.1 * scale) * s.astype(f32), first[0])


def factors(table, me, pieces, left, right, first, bands, entries):
    slots, n, _ = left.shape
    block = pl.BlockSpec((1, n, n), lambda s: (s, 0, 0))
    scalar = pl.BlockSpec(memory_space=SMEM)
    whole = pl.BlockSpec(memory_space=VMEM)

    def body(*refs):
        factors_body(bands, entries, *refs)

    return pl.pallas_call(
        body,
        grid=(slots,),
        in_specs=[scalar] * 2 + [whole] + [block] * 3,
        out_specs=[block] * 3,
        out_shape=[HBM(left.shape, f32)] * 3,
        compiler_params=pltpu.CompilerParams(vmem_limit_bytes=32 << 20),
        cost_estimate=pl.CostEstimate(
            flops=slots * 4 * n**3, bytes_accessed=slots * 26 * n * n, transcendentals=0
        ),
        name="factors",
    )(table, me, pieces, *in_hbm(left, right, first))


def per_device(
    replica_grads,
    owners,
    left_factor,
    right_factor,
    left_basis,
    right_basis,
    first_moment,
    second_moment,
):
    rows_dev = replica_grads.shape[1]
    shards = lax.axis_size("fsdp")
    slots, n = left_factor.shape[1:3]
    per_band = n // rows_dev
    bands = shards // per_band
    dp = lax.axis_size("dp")
    dp_me = lax.axis_index("dp").astype(jnp.int32)
    me = lax.axis_index("fsdp").astype(jnp.int32)
    place = jnp.stack([dp_me // 2, dp_me % 2, me // per_band])
    table = jnp.concatenate([owners, (me // per_band).reshape(1, 1)], axis=1)
    me = me.reshape(1)
    core = ("dp", [(d, d ^ 1) for d in range(dp)])
    along_x = [("dp", [(d, (d + 2 * h) % dp) for d in range(dp)]) for h in range(1, dp // 2)]
    along_z = [
        ("fsdp", [(i, (i + h * per_band) % shards) for i in range(shards)])
        for h in range(1, bands)
    ]
    parts = sum_over_replicas(place, replica_grads[0], bands)
    prepared = prepare(left_basis[0], right_basis[0], first_moment[0])
    parts, prepared = lax.optimization_barrier((parts, prepared))
    *sums, square = finish(place, *parts, bands)
    rows, width = sums[0].shape
    cols = width // n
    entries = rows_dev * shards * replica_grads.shape[2]
    spread = exchange(sums, along_z)
    out = jax.ShapeDtypeStruct((8, LANES), f32)
    square = local(plus_body, [place, square, lax.ppermute(square, *core)], out, "plus")
    squares = [square] + [lax.ppermute(square, *step) for step in along_x]
    out = jax.ShapeDtypeStruct((shards, slots * rows + 8, n), bf16)
    sent = local(dispatch_body, [table, *spread, *squares], out, "dispatch")
    pieces = lax.all_to_all(sent, "fsdp", split_axis=0, concat_axis=0, tiled=True)
    update, second_new = direction(
        owners, me, pieces, prepared, second_moment[0], bands, entries
    )
    back = lax.all_to_all(update, "fsdp", split_axis=0, concat_axis=0, tiled=True)
    back, pieces = lax.optimization_barrier((back, pieces))
    new = factors(
        owners, me, pieces, left_factor[0], right_factor[0], first_moment[0], bands, entries
    )
    left_new, right_new, first_new = new
    out = [jax.ShapeDtypeStruct((rows, width), bf16)] * bands
    mine = local(collect_body, [table, back.reshape(shards * slots, rows, n)], out, "collect")
    out = jax.ShapeDtypeStruct((bands, rows, width), bf16)
    result = local(put_body, [table, *exchange(mine, along_z)], out, "put").reshape(rows_dev, width)
    return (result, left_new[None], right_new[None], first_new[None], second_new[None])


def solution(mesh):
    state = P("dp", "fsdp", None, None)
    return jax.shard_map(
        per_device,
        mesh=mesh,
        in_specs=(P("dp", "fsdp", None), P("dp", None)) + (state,) * 6,
        out_specs=(P("fsdp", "dp"),) + (state,) * 4,
        check_vma=False,
    )
```

```python
import jax
import jax.numpy as jnp
from jax import lax
from jax.experimental import pallas as pl
from jax.experimental.pallas import tpu as pltpu
from jax.sharding import PartitionSpec as P

f32 = jnp.float32
bf16 = jnp.bfloat16
SMEM = pltpu.MemorySpace.SMEM
VMEM = pltpu.MemorySpace.VMEM
HBM = pltpu.MemorySpace.HBM
LANES = 128


def in_hbm(*arrays):
    return [pltpu.with_memory_space_constraint(a, HBM) for a in arrays]


def split3(value):
    head, rest = split(value)
    mid, tail = split(value - head.astype(f32))
    return head, mid, tail


def split(value):
    head = value.astype(bf16)
    return head, (value - head.astype(f32)).astype(bf16)


def mm(a, b, dims=((1,), (0,))):
    return lax.dot_general(a, b, (dims, ((), ())), preferred_element_type=f32)


def tiles(count, size=32):
    return [slice(r, r + size) for r in range(0, count, size)]


def prepare_body(left_ref, right_ref, first_ref, lt_ref, l_ref, r_ref, rot_ref, half, product):
    n = left_ref.shape[1]
    for rows in tiles(n, LANES):
        head, tail = split(left_ref[0, rows].T)
        lt_ref[0, :n, rows] = head
        lt_ref[0, n:, rows] = tail
    for rows in tiles(n):
        l_ref[0, rows] = left_ref[0, rows].astype(bf16)
        head, tail = split(right_ref[0, rows])
        r_ref[0, rows, :n] = head
        r_ref[0, rows, n:] = tail
        half[rows] = first_ref[0, rows].astype(bf16)
    product[...] = mm(lt_ref[0], half[...])
    for rows, more in zip(tiles(n), tiles(2 * n)[n // 32 :]):
        half[rows] = (product[rows] + product[more]).astype(bf16)
    right = r_ref[0]
    rot_ref[0] = 0.9 * (mm(half[...], right[:, :n]) + mm(half[...], right[:, n:]))


def prepare(left_basis, right_basis, first_moment):
    slots, n, _ = left_basis.shape
    block = pl.BlockSpec((1, n, n), lambda s: (s, 0, 0))
    return pl.pallas_call(
        prepare_body,
        grid=(slots,),
        in_specs=[block] * 3,
        out_specs=[
            pl.BlockSpec((1, 2 * n, n), lambda s: (s, 0, 0)),
            block,
            pl.BlockSpec((1, n, 2 * n), lambda s: (s, 0, 0)),
            block,
        ],
        out_shape=[
            HBM((slots, 2 * n, n), bf16),
            HBM((slots, n, n), bf16),
            HBM((slots, n, 2 * n), bf16),
            HBM((slots, n, n), f32),
        ],
        scratch_shapes=[pltpu.VMEM((n, n), bf16), pltpu.VMEM((2 * n, n), f32)],
        compiler_params=pltpu.CompilerParams(vmem_limit_bytes=24 << 20),
        cost_estimate=pl.CostEstimate(
            flops=slots * 8 * n**3, bytes_accessed=slots * 26 * n * n, transcendentals=0
        ),
        name="prepare",
    )(*in_hbm(left_basis, right_basis, first_moment))


def local(body, arrays, out_shape, name, limit=8 << 20):
    return pl.pallas_call(
        body,
        in_specs=[pl.BlockSpec(memory_space=SMEM)]
        + [pl.BlockSpec(memory_space=VMEM)] * (len(arrays) - 1),
        out_specs=jax.tree.map(
            lambda _: pl.BlockSpec(memory_space=VMEM), out_shape, is_leaf=lambda o: hasattr(o, "shape")
        ),
        out_shape=out_shape,
        compiler_params=pltpu.CompilerParams(vmem_limit_bytes=limit),
        name=name,
    )(*arrays)


def dispatch_body(table, *refs):
    *srcs, squares, dst = refs
    n = dst.shape[2]
    rows, width = srcs[0].shape
    bands = len(srcs)
    cols = width // n
    slots = (dst.shape[1] - 8) // rows
    z = table[0, bands * cols]
    for j, src in enumerate(srcs):
        band = lax.rem(z + bands - j, bands)
        for c in range(cols):
            slot = table[0, band * cols + c]
            row = pl.multiple_of(lax.rem(slot, slots) * rows, rows)
            dst[slot // slots, pl.ds(row, rows)] = src[:, c * n : (c + 1) * n]
    total = squares[0]
    for i in range(1, squares.shape[0]):
        total = total + squares[i]
    terms = [t.astype(f32) for t in split3(total)]
    terms.append(jnp.zeros((8, n - 3 * LANES), f32))
    terms = jnp.concatenate(terms, axis=1).astype(bf16)
    for o in range(dst.shape[0]):
        dst[o, slots * rows :] = terms


def collect_body(table, src, *dsts):
    n = src.shape[2]
    bands = len(dsts)
    cols = dsts[0].shape[1] // n
    z = table[0, bands * cols]
    for j, dst in enumerate(dsts):
        band = lax.rem(z + j, bands)
        for c in range(cols):
            dst[:, c * n : (c + 1) * n] = src[table[0, band * cols + c]]


def put(table, arrays):
    bands = len(arrays)
    rows, width = arrays[0].shape

    def body(table, *refs):
        *srcs, dst, sems = refs
        z = table[0, table.shape[1] - 1]
        copies = [
            pltpu.make_async_copy(src, dst.at[lax.rem(z + bands - j, bands)], sems.at[j])
            for j, src in enumerate(srcs)
        ]
        for c in copies:
            c.start()
        for c in copies:
            c.wait()

    return pl.pallas_call(
        body,
        in_specs=[pl.BlockSpec(memory_space=SMEM)] + [pl.BlockSpec(memory_space=VMEM)] * bands,
        out_specs=pl.BlockSpec(memory_space=HBM),
        out_shape=HBM((bands, rows, width), bf16),
        scratch_shapes=[pltpu.SemaphoreType.DMA((bands,))],
        compiler_params=pltpu.CompilerParams(vmem_limit_bytes=2 << 20),
        name="put",
    )(table, *arrays)


def load(place, grads, width):
    rows, columns = grads.shape
    chips = columns // width // 2
    groups = ((2,), (1, 3, 0))

    def body(place, src, *refs):
        *dsts, sems = refs
        copies = []
        for i, dst in enumerate(dsts):
            core = 1 - place[1] if i < 2 else place[1]
            for k, j in enumerate(groups[i % 2]):
                slab = 2 * lax.rem(place[0] + j, chips) + core
                columns = pl.ds(pl.multiple_of(slab * width, width), width)
                copies.append(
                    pltpu.make_async_copy(src.at[:, columns], dst.at[k], sems.at[len(copies)])
                )
        for c in copies:
            c.start()
        for c in copies:
            c.wait()

    return pl.pallas_call(
        body,
        in_specs=[pl.BlockSpec(memory_space=SMEM), pl.BlockSpec(memory_space=HBM)],
        out_specs=[pl.BlockSpec(memory_space=VMEM)] * 4,
        out_shape=[VMEM((len(g), rows, width), bf16) for g in groups * 2],
        scratch_shapes=[pltpu.SemaphoreType.DMA((2 * chips,))],
        compiler_params=pltpu.CompilerParams(vmem_limit_bytes=2 << 20),
        name="load",
    )(place, *in_hbm(grads))


def pair(body, place, near, far, outs, name):
    low = near.shape[1] // 2

    def run(place, near, far, *outs):
        def total(i, a):
            part = slice(a * low, (a + 1) * low)
            return near[i, part].astype(f32) + far[i, part].astype(f32)

        body(total, low, *outs)

    out = [jax.ShapeDtypeStruct(shape, kind) for shape, kind in outs]
    return local(run, [place, near, far], out, name)


def far_body(total, low, to_right, to_left):
    to_right[...] = total(0, 0).astype(bf16)
    to_left[...] = total(0, 1).astype(bf16)


def near_body(total, low, to_right, to_left, keep_right, keep_left, own):
    keep_right[...] = total(0, 0)
    to_right[...] = total(0, 1).astype(bf16)
    to_left[...] = total(1, 0).astype(bf16)
    keep_left[...] = total(1, 1)
    for a in range(2):
        own[a * low : (a + 1) * low] = total(2, a)


def relay(place, kept, arrived):
    def body(place, kept, arrived, out):
        out[...] = (kept[...] + arrived[...].astype(f32)).astype(bf16)

    out = jax.ShapeDtypeStruct(kept.shape, bf16)
    return local(body, (place, kept, arrived), out, "relay")


def finish(place, own, left_direct, right_direct, left_sum, right_sum, bands, copies):
    rows, width = own.shape
    low = rows // 2
    piece = rows // bands

    def body(place, own, left_direct, right_direct, left_sum, right_sum, *refs):
        *outs, squares = refs
        total = jnp.zeros((8, LANES), f32)
        for q in range(bands):
            near, far = (left_sum, right_direct) if q * piece < low else (left_direct, right_sum)
            part = slice(q * piece % low, q * piece % low + piece)
            value = own[q * piece : (q + 1) * piece] + (
                near[part].astype(f32) + far[part].astype(f32)
            )
            step = lax.rem(q - place[2] + bands, bands)
            rounded = value.astype(bf16)
            for j in range(bands):

                @pl.when(step == j)
                def _():
                    outs[j][...] = rounded

            by_row = jnp.sum((value * value).reshape(piece // 8, 8, width), axis=0)
            for c in range(width // LANES):
                total = total + by_row[:, c * LANES : (c + 1) * LANES]
        for i in range(squares.shape[0]):
            squares[i] = total

    arrays = [place, own, left_direct, right_direct, left_sum, right_sum]
    out = [jax.ShapeDtypeStruct((piece, width), bf16)] * bands
    out.append(jax.ShapeDtypeStruct((copies, 8, LANES), f32))
    return local(body, arrays, out, "finish", 12 << 20)


def sum_over_replicas(place, grads, bands):
    size = lax.axis_size("dp")
    rows, columns = grads.shape
    width = columns // size
    half = (rows // 2, width)
    swap = [(d, d ^ 1) for d in range(size)]
    up = [(d, (d + 2) % size) for d in range(size)]
    down = [(d, (d - 2) % size) for d in range(size)]
    far_there, near_there, far_here, near_here = load(place, grads, width)
    other = lax.ppermute(far_there, "dp", swap)
    other, near_there = lax.optimization_barrier((other, near_there))
    others = lax.ppermute(near_there, "dp", swap)
    to_right, to_left = pair(far_body, place, far_here, other, [(half, bf16)] * 2, "pair_far")
    left_far = lax.ppermute(to_right, "dp", up)
    right_far = lax.ppermute(to_left, "dp", down)
    outs = [(half, bf16)] * 2 + [(half, f32)] * 2 + [((rows, width), f32)]
    to_right, to_left, keep_right, keep_left, own = pair(
        near_body, place, near_here, others, outs, "pair_near"
    )
    left_direct = lax.ppermute(to_right, "dp", up)
    right_direct = lax.ppermute(to_left, "dp", down)
    left_sum = lax.ppermute(relay(place, keep_right, left_far), "dp", up)
    right_sum = lax.ppermute(relay(place, keep_left, right_far), "dp", down)
    return own, left_direct, right_direct, left_sum, right_sum


def exchange(arrays, steps):
    order = sorted(range(1, len(arrays)), key=lambda j: -min(j, len(arrays) - j))
    got = {0: arrays[0]}
    for j in order:
        got[j] = lax.ppermute(arrays[j], *steps[j - 1])
    return [got[j] for j in range(len(arrays))]


def assemble(pieces, slot, rows, bands):
    per = pieces.shape[0] // bands
    part = pl.ds(slot * rows, rows)
    return jnp.concatenate(
        [pieces[z * per + y, part] for y in range(per) for z in range(bands)], axis=0
    )


def is_named(table, slot):
    named = table[0, 0] == slot
    for b in range(1, table.shape[1]):
        named = jnp.logical_or(named, table[0, b] == slot)
    return named


def clip_of(pieces, entries):
    total = jnp.zeros((8, pieces.shape[2]), f32)
    for sender in range(pieces.shape[0]):
        total = total + pieces[sender, pieces.shape[1] - 8 :].astype(f32)
    total = jnp.sum(jnp.sum(total, axis=0, keepdims=True), axis=1, keepdims=True)
    return jnp.minimum(1.0, 1.0 / jnp.sqrt(total / entries + 1e-06))


def direction_body(bands, entries, table, me, pieces, second, *refs):
    lt_src, l_src, r_src, rot_src, out, second_out = refs[:6]
    lt, left, right, rot, old, new, half, product, step, sems, out_sems = refs[6:]
    slots, n, _ = second.shape
    sources, targets = (lt_src, r_src, rot_src, second, l_src), (lt, right, rot, old, left)
    copies = [
        [
            pltpu.make_async_copy(src.at[s], dst.at[s], sems.at[s, i])
            for i, (src, dst) in enumerate(zip(sources, targets))
        ]
        for s in range(slots)
    ]
    for group in copies:
        for c in group:
            c.start()
    scale = clip_of(pieces, entries)
    senders = pieces.shape[0]
    rows = n // senders
    per = senders // bands
    for s in range(slots):
        block = assemble(pieces, s, rows, bands)
        copies[s][0].wait()
        product[...] = mm(lt[s], block)
        for r, more in zip(tiles(n), tiles(2 * n)[n // 32 :]):
            half[r] = (product[r] + product[more]).astype(bf16)
        copies[s][1].wait()
        product[:n] = mm(half[...], right[s, :, :n])
        product[n:] = mm(half[...], right[s, :, n:])
        copies[s][2].wait()
        copies[s][3].wait()
        named = is_named(table, me[0] * slots + s)
        for r, more in zip(tiles(n), tiles(2 * n)[n // 32 :]):
            rotated = (product[r] + product[more]) * scale
            before = old[s, r]
            value = 0.95 * before + 0.05 * rotated * rotated
            new[s, r] = jnp.where(named, value, before)
            turned = rot[s, r] + 0.1 * rotated
            step[r] = (turned / (jnp.sqrt(value) + 1e-08)).astype(bf16)
        pltpu.make_async_copy(new.at[s], second_out.at[s], out_sems.at[s]).start()
        copies[s][4].wait()
        half[...] = mm(left[s], step[...]).astype(bf16)
        update = mm(half[...], right[s, :, :n], ((1,), (1,))).astype(bf16)
        for y in range(per):
            for z in range(bands):
                row = (y * bands + z) * rows
                out[z * per + y, s] = update[row : row + rows]
    for s in range(slots):
        pltpu.make_async_copy(new.at[s], second_out.at[s], out_sems.at[s]).wait()


def direction(table, me, pieces, prepared, second, bands, entries):
    slots, n, _ = second.shape
    senders = pieces.shape[0]
    scalar = pl.BlockSpec(memory_space=SMEM)
    whole = pl.BlockSpec(memory_space=VMEM)
    far = pl.BlockSpec(memory_space=HBM)

    def body(*refs):
        direction_body(bands, entries, *refs)

    return pl.pallas_call(
        body,
        in_specs=[scalar] * 2 + [whole] + [far] * 5,
        out_specs=[whole, far],
        out_shape=[
            jax.ShapeDtypeStruct((senders, slots, n // senders, n), bf16),
            HBM(second.shape, f32),
        ],
        scratch_shapes=[
            pltpu.VMEM((slots, 2 * n, n), bf16),
            pltpu.VMEM((slots, n, n), bf16),
            pltpu.VMEM((slots, n, 2 * n), bf16),
            pltpu.VMEM((slots, n, n), f32),
            pltpu.VMEM((slots, n, n), f32),
            pltpu.VMEM((slots, n, n), f32),
            pltpu.VMEM((n, n), bf16),
            pltpu.VMEM((2 * n, n), f32),
            pltpu.VMEM((n, n), bf16),
            pltpu.SemaphoreType.DMA((slots, 5)),
            pltpu.SemaphoreType.DMA((slots,)),
        ],
        compiler_params=pltpu.CompilerParams(vmem_limit_bytes=32 << 20),
        name="direction",
    )(table, me, pieces, *in_hbm(second, *prepared))


def factors_body(bands, entries, table, me, pieces, left, right, first, left_out, right_out, first_out):
    slot = me[0] * pl.num_programs(0) + pl.program_id(0)
    scale = clip_of(pieces, entries)
    s = assemble(pieces, pl.program_id(0), left.shape[1] // pieces.shape[0], bands)
    named = is_named(table, slot)
    square = 0.1 * scale * scale
    left_out[0] = jnp.where(named, 0.9 * left[0] + square * mm(s, s, ((1,), (1,))), left[0])
    right_out[0] = jnp.where(named, 0.9 * right[0] + square * mm(s.T, s), right[0])
    first_out[0] = jnp.where(named, 0.9 * first[0] + (0.1 * scale) * s.astype(f32), first[0])


def factors(table, me, pieces, left, right, first, bands, entries):
    slots, n, _ = left.shape
    block = pl.BlockSpec((1, n, n), lambda s: (s, 0, 0))
    scalar = pl.BlockSpec(memory_space=SMEM)
    whole = pl.BlockSpec(memory_space=VMEM)

    def body(*refs):
        factors_body(bands, entries, *refs)

    return pl.pallas_call(
        body,
        grid=(slots,),
        in_specs=[scalar] * 2 + [whole] + [block] * 3,
        out_specs=[block] * 3,
        out_shape=[HBM(left.shape, f32)] * 3,
        compiler_params=pltpu.CompilerParams(vmem_limit_bytes=32 << 20),
        cost_estimate=pl.CostEstimate(
            flops=slots * 4 * n**3, bytes_accessed=slots * 26 * n * n, transcendentals=0
        ),
        name="factors",
    )(table, me, pieces, *in_hbm(left, right, first))


def per_device(
    replica_grads,
    owners,
    left_factor,
    right_factor,
    left_basis,
    right_basis,
    first_moment,
    second_moment,
):
    rows_dev = replica_grads.shape[1]
    shards = lax.axis_size("fsdp")
    slots, n = left_factor.shape[1:3]
    per_band = n // rows_dev
    bands = shards // per_band
    dp = lax.axis_size("dp")
    dp_me = lax.axis_index("dp").astype(jnp.int32)
    me = lax.axis_index("fsdp").astype(jnp.int32)
    place = jnp.stack([dp_me // 2, dp_me % 2, me // per_band])
    table = jnp.concatenate([owners, (me // per_band).reshape(1, 1)], axis=1)
    me = me.reshape(1)
    along_z = [
        ("fsdp", [(i, (i + h * per_band) % shards) for i in range(shards)])
        for h in range(1, bands)
    ]
    parts = sum_over_replicas(place, replica_grads[0], bands)
    prepared = prepare(left_basis[0], right_basis[0], first_moment[0])
    parts, prepared = lax.optimization_barrier((parts, prepared))
    *sums, squares = finish(place, *parts, bands, dp)
    rows, width = sums[0].shape
    cols = width // n
    entries = rows_dev * shards * replica_grads.shape[2]
    spread = exchange(sums, along_z)
    squares = lax.all_to_all(squares, "dp", split_axis=0, concat_axis=0, tiled=True)
    out = jax.ShapeDtypeStruct((shards, slots * rows + 8, n), bf16)
    sent = local(dispatch_body, [table, *spread, squares], out, "dispatch")
    pieces = lax.all_to_all(sent, "fsdp", split_axis=0, concat_axis=0, tiled=True)
    update, second_new = direction(
        owners, me, pieces, prepared, second_moment[0], bands, entries
    )
    back = lax.all_to_all(update, "fsdp", split_axis=0, concat_axis=0, tiled=True)
    back, pieces = lax.optimization_barrier((back, pieces))
    new = factors(
        owners, me, pieces, left_factor[0], right_factor[0], first_moment[0], bands, entries
    )
    left_new, right_new, first_new = new
    out = [jax.ShapeDtypeStruct((rows, width), bf16)] * bands
    mine = local(collect_body, [table, back.reshape(shards * slots, rows, n)], out, "collect")
    result = put(table, exchange(mine, along_z)).reshape(rows_dev, width)
    return (result, left_new[None], right_new[None], first_new[None], second_new[None])


def solution(mesh):
    state = P("dp", "fsdp", None, None)
    return jax.shard_map(
        per_device,
        mesh=mesh,
        in_specs=(P("dp", "fsdp", None), P("dp", None)) + (state,) * 6,
        out_specs=(P("fsdp", "dp"),) + (state,) * 4,
        check_vma=False,
    )
```

```python
import jax
import jax.numpy as jnp
from jax import lax
from jax.experimental import pallas as pl
from jax.experimental.pallas import tpu as pltpu
from jax.sharding import PartitionSpec as P

f32 = jnp.float32
bf16 = jnp.bfloat16
SMEM = pltpu.MemorySpace.SMEM
VMEM = pltpu.MemorySpace.VMEM
HBM = pltpu.MemorySpace.HBM
LANES = 128


def in_hbm(*arrays):
    return [pltpu.with_memory_space_constraint(a, HBM) for a in arrays]


def split3(value):
    head, rest = split(value)
    mid, tail = split(value - head.astype(f32))
    return head, mid, tail


def split(value):
    head = value.astype(bf16)
    return head, (value - head.astype(f32)).astype(bf16)


def mm(a, b, dims=((1,), (0,))):
    return lax.dot_general(a, b, (dims, ((), ())), preferred_element_type=f32)


def tiles(count, size=32):
    return [slice(r, r + size) for r in range(0, count, size)]


def prepare_body(
    left_src, right_src, first_src, lt_dst, l_dst, r_dst, rot_dst, *scratch
):
    left, right, first, lt, low, head, rot, lt_both, half, tail, product, sems, out_sems = scratch
    slots, n, _ = left.shape
    pairs = ((left_src, left), (first_src, first), (right_src, right))
    copies = [
        [
            pltpu.make_async_copy(src.at[s], dst.at[s], sems.at[s, i])
            for i, (src, dst) in enumerate(pairs)
        ]
        for s in range(slots)
    ]
    for group in copies:
        for c in group:
            c.start()
    pairs = ((lt, lt_dst), (low, l_dst), (head, r_dst), (rot, rot_dst))
    outs = [
        [
            pltpu.make_async_copy(src.at[s], dst.at[s], out_sems.at[s, i])
            for i, (src, dst) in enumerate(pairs)
        ]
        for s in range(slots)
    ]
    for s in range(slots):
        copies[s][0].wait()
        for rows in tiles(n, LANES):
            above, below = split(left[s, rows].T)
            lt[s, :, rows] = above
            lt_both[:n, rows] = above
            lt_both[n:, rows] = below
        outs[s][0].start()
        for rows in tiles(n):
            low[s, rows] = left[s, rows].astype(bf16)
        outs[s][1].start()
        copies[s][1].wait()
        for rows in tiles(n):
            half[rows] = first[s, rows].astype(bf16)
        product[...] = mm(lt_both[...], half[...])
        copies[s][2].wait()
        for rows, more in zip(tiles(n), tiles(2 * n)[n // 32 :]):
            half[rows] = (product[rows] + product[more]).astype(bf16)
            head[s, rows], tail[rows] = split(right[s, rows])
        outs[s][2].start()
        rot[s] = 0.9 * (mm(half[...], head[s]) + mm(half[...], tail[...]))
        outs[s][3].start()
    for group in outs:
        for c in group:
            c.wait()


def prepare(left_basis, right_basis, first_moment):
    slots, n, _ = left_basis.shape
    far = pl.BlockSpec(memory_space=HBM)
    return pl.pallas_call(
        prepare_body,
        in_specs=[far] * 3,
        out_specs=[far] * 4,
        out_shape=[HBM((slots, n, n), bf16)] * 3 + [HBM((slots, n, n), f32)],
        scratch_shapes=[pltpu.VMEM((slots, n, n), f32)] * 3
        + [pltpu.VMEM((slots, n, n), bf16)] * 3
        + [
            pltpu.VMEM((slots, n, n), f32),
            pltpu.VMEM((2 * n, n), bf16),
            pltpu.VMEM((n, n), bf16),
            pltpu.VMEM((n, n), bf16),
            pltpu.VMEM((2 * n, n), f32),
            pltpu.SemaphoreType.DMA((slots, 3)),
            pltpu.SemaphoreType.DMA((slots, 4)),
        ],
        compiler_params=pltpu.CompilerParams(vmem_limit_bytes=24 << 20),
        cost_estimate=pl.CostEstimate(
            flops=slots * 8 * n**3, bytes_accessed=slots * 22 * n * n, transcendentals=0
        ),
        name="prepare",
    )(*in_hbm(left_basis, right_basis, first_moment))


def local(body, arrays, out_shape, name, limit=8 << 20, cost=None):
    return pl.pallas_call(
        body,
        in_specs=[pl.BlockSpec(memory_space=SMEM)]
        + [pl.BlockSpec(memory_space=VMEM)] * (len(arrays) - 1),
        out_specs=jax.tree.map(
            lambda _: pl.BlockSpec(memory_space=VMEM), out_shape, is_leaf=lambda o: hasattr(o, "shape")
        ),
        out_shape=out_shape,
        compiler_params=pltpu.CompilerParams(vmem_limit_bytes=limit),
        cost_estimate=cost,
        name=name,
    )(*arrays)


def dispatch_body(table, *refs):
    *srcs, dst, square = refs
    n = dst.shape[2]
    bands = len(srcs)
    width = srcs[0].shape[1] - LANES
    cols = width // n
    z = table[0, bands * cols]
    total = jnp.zeros(square.shape, f32)
    for j, src in enumerate(srcs):
        band = lax.rem(z + bands - j, bands)
        for c in range(cols):
            dst[table[0, band * cols + c]] = src[:, c * n : (c + 1) * n]
        terms = src[:, width:].astype(f32)
        for t in range(3):
            total = total + terms[8 * t : 8 * t + 8]
    square[...] = total


def collect_body(table, src, *dsts):
    n = src.shape[2]
    bands = len(dsts)
    cols = dsts[0].shape[1] // n
    z = table[0, bands * cols]
    for j, dst in enumerate(dsts):
        band = lax.rem(z + j, bands)
        for c in range(cols):
            dst[:, c * n : (c + 1) * n] = src[table[0, band * cols + c]]


def put_body(table, *refs):
    *srcs, dst = refs
    bands = len(srcs)
    z = table[0, table.shape[1] - 1]
    for j, src in enumerate(srcs):
        dst[lax.rem(z + bands - j, bands)] = src[...]


def plus_body(place, *refs):
    total = refs[0][...]
    for ref in refs[1:-1]:
        total = total + ref[...]
    refs[-1][...] = total


def load(place, grads, width):
    rows, columns = grads.shape
    chips = columns // width // 2
    groups = ((2,), (1, 3, 0))

    def body(place, src, *refs):
        *dsts, sems = refs
        copies = []
        for i, dst in enumerate(dsts):
            core = 1 - place[1] if i < 2 else place[1]
            for k, j in enumerate(groups[i % 2]):
                slab = 2 * lax.rem(place[0] + j, chips) + core
                columns = pl.ds(pl.multiple_of(slab * width, width), width)
                copies.append(
                    pltpu.make_async_copy(src.at[:, columns], dst.at[k], sems.at[len(copies)])
                )
        for c in copies:
            c.start()
        for c in copies:
            c.wait()

    return pl.pallas_call(
        body,
        in_specs=[pl.BlockSpec(memory_space=SMEM), pl.BlockSpec(memory_space=HBM)],
        out_specs=[pl.BlockSpec(memory_space=VMEM)] * 4,
        out_shape=[VMEM((len(g), rows, width), bf16) for g in groups * 2],
        scratch_shapes=[pltpu.SemaphoreType.DMA((2 * chips,))],
        compiler_params=pltpu.CompilerParams(vmem_limit_bytes=2 << 20),
        name="load",
    )(place, *in_hbm(grads))


def pair(body, place, near, far, outs, name):
    low = near.shape[1] // 2

    def run(place, near, far, *outs):
        def total(i, a):
            part = slice(a * low, (a + 1) * low)
            return near[i, part].astype(f32) + far[i, part].astype(f32)

        body(total, low, *outs)

    out = [jax.ShapeDtypeStruct(shape, kind) for shape, kind in outs]
    return local(run, [place, near, far], out, name)


def far_body(total, low, to_right, to_left):
    to_right[...] = total(0, 0).astype(bf16)
    to_left[...] = total(0, 1).astype(bf16)


def near_body(total, low, to_right, to_left, keep_right, keep_left, own):
    keep_right[...] = total(0, 0)
    to_right[...] = total(0, 1).astype(bf16)
    to_left[...] = total(1, 0).astype(bf16)
    keep_left[...] = total(1, 1)
    for a in range(2):
        own[a * low : (a + 1) * low] = total(2, a)


def relay(place, kept, arrived):
    def body(place, kept, arrived, out):
        out[...] = (kept[...] + arrived[...].astype(f32)).astype(bf16)

    out = jax.ShapeDtypeStruct(kept.shape, bf16)
    return local(body, (place, kept, arrived), out, "relay")


def direct_body(place, own, left_direct, right_direct, out):
    low = left_direct.shape[0]
    out[:low] = own[:low] + right_direct[...].astype(f32)
    out[low:] = own[low:] + left_direct[...].astype(f32)


def finish(place, own, left_sum, right_sum, bands):
    rows, width = own.shape
    low = rows // 2
    piece = rows // bands

    def body(place, own, left_sum, right_sum, *outs):
        total = jnp.zeros((8, LANES), f32)
        for q in range(bands):
            relayed = left_sum if q * piece < low else right_sum
            part = slice(q * piece % low, q * piece % low + piece)
            value = own[q * piece : (q + 1) * piece] + relayed[part].astype(f32)
            step = lax.rem(q - place[2] + bands, bands)
            rounded = value.astype(bf16)
            for j in range(bands):

                @pl.when(step == j)
                def _():
                    outs[j][:, :width] = rounded

            by_row = jnp.sum((value * value).reshape(piece // 8, 8, width), axis=0)
            for c in range(width // LANES):
                total = total + by_row[:, c * LANES : (c + 1) * LANES]
        terms = [t.astype(f32) for t in split3(total)]
        terms.append(jnp.zeros((piece - 24, LANES), f32))
        terms = jnp.concatenate(terms, axis=0).astype(bf16)
        for out in outs:
            out[:, width:] = terms

    arrays = [place, own, left_sum, right_sum]
    out = [jax.ShapeDtypeStruct((piece, width + LANES), bf16)] * bands
    return local(body, arrays, out, "finish", 12 << 20)


def sum_over_replicas(place, grads, bands):
    size = lax.axis_size("dp")
    rows, columns = grads.shape
    width = columns // size
    half = (rows // 2, width)
    swap = [(d, d ^ 1) for d in range(size)]
    up = [(d, (d + 2) % size) for d in range(size)]
    down = [(d, (d - 2) % size) for d in range(size)]
    far_there, near_there, far_here, near_here = load(place, grads, width)
    other = lax.ppermute(far_there, "dp", swap)
    other, near_there = lax.optimization_barrier((other, near_there))
    others = lax.ppermute(near_there, "dp", swap)
    to_right, to_left = pair(far_body, place, far_here, other, [(half, bf16)] * 2, "pair_far")
    left_far = lax.ppermute(to_right, "dp", up)
    right_far = lax.ppermute(to_left, "dp", down)
    outs = [(half, bf16)] * 2 + [(half, f32)] * 2 + [((rows, width), f32)]
    to_right, to_left, keep_right, keep_left, own = pair(
        near_body, place, near_here, others, outs, "pair_near"
    )
    left_direct = lax.ppermute(to_right, "dp", up)
    right_direct = lax.ppermute(to_left, "dp", down)
    left_sum = lax.ppermute(relay(place, keep_right, left_far), "dp", up)
    right_sum = lax.ppermute(relay(place, keep_left, right_far), "dp", down)
    out = jax.ShapeDtypeStruct((rows, width), f32)
    own = local(direct_body, [place, own, left_direct, right_direct], out, "direct", cost=pl.CostEstimate(flops=2 * rows * width, bytes_accessed=12 * rows * width, transcendentals=0))
    return own, left_sum, right_sum


def exchange(arrays, steps):
    order = sorted(range(1, len(arrays)), key=lambda j: -min(j, len(arrays) - j))
    got = {0: arrays[0]}
    for j in order:
        got[j] = lax.ppermute(arrays[j], *steps[j - 1])
    return [got[j] for j in range(len(arrays))]


def assemble(pieces, slot, bands):
    per = pieces.shape[0] // bands
    return jnp.concatenate(
        [pieces[z * per + y, slot] for y in range(per) for z in range(bands)], axis=0
    )


def is_named(table, slot):
    named = table[0, 0] == slot
    for b in range(1, table.shape[1]):
        named = jnp.logical_or(named, table[0, b] == slot)
    return named


def clip_of(squares, entries):
    total = squares[0][...]
    for square in squares[1:]:
        total = total + square[...]
    total = jnp.sum(jnp.sum(total, axis=0, keepdims=True), axis=1, keepdims=True)
    return jnp.minimum(1.0, 1.0 / jnp.sqrt(total / entries + 1e-06))


def rotate(pieces, prepared, second, bands):
    slots, n, _ = second.shape

    def body(pieces, lt_src, l_src, r_src, rot_src, old_src, *refs):
        out, left, right, rot, old, lt, half, sems = refs
        pairs = ((lt_src, lt), (r_src, right), (rot_src, rot), (old_src, old), (l_src, left))
        copies = [
            pltpu.make_async_copy(src.at[s], dst.at[s], sems.at[s, i])
            for s in range(slots)
            for i, (src, dst) in enumerate(pairs)
        ]
        for c in copies:
            c.start()
        for s in range(slots):
            group = copies[s * len(pairs) : (s + 1) * len(pairs)]
            block = assemble(pieces, s, bands)
            group[0].wait()
            half[...] = mm(lt[s], block).astype(bf16)
            group[1].wait()
            out[s] = mm(half[...], right[s])
            for c in group[2:]:
                c.wait()

    whole = pl.BlockSpec(memory_space=VMEM)
    far = pl.BlockSpec(memory_space=HBM)
    return pl.pallas_call(
        body,
        in_specs=[whole] + [far] * 5,
        out_specs=[whole] * 5,
        out_shape=[
            VMEM((slots, n, n), f32),
            VMEM((slots, n, n), bf16),
            VMEM((slots, n, n), bf16),
            VMEM((slots, n, n), f32),
            VMEM((slots, n, n), f32),
        ],
        scratch_shapes=[
            pltpu.VMEM((slots, n, n), bf16),
            pltpu.VMEM((n, n), bf16),
            pltpu.SemaphoreType.DMA((slots, 5)),
        ],
        compiler_params=pltpu.CompilerParams(vmem_limit_bytes=12 << 20),
        name="rotate",
    )(pieces, *in_hbm(*prepared, second))


def direction(table, me, squares, rotated, bands, senders, entries):
    slots, n, _ = rotated[0].shape
    rows = n // senders
    per = senders // bands

    def body(table, me, *refs):
        squares, rest = refs[: len(refs) - 11], refs[len(refs) - 11 :]
        product, left, right, rot, old, out, second_out, new, step, half, sems = rest
        scale = clip_of(squares, entries)
        for s in range(slots):
            named = is_named(table, me[0] * slots + s)
            for r in tiles(n):
                turned = product[s, r] * scale
                before = old[s, r]
                value = 0.95 * before + 0.05 * turned * turned
                new[s, r] = jnp.where(named, value, before)
                ahead = rot[s, r] + 0.1 * turned
                step[r] = (ahead / (jnp.sqrt(value) + 1e-08)).astype(bf16)
            pltpu.make_async_copy(new.at[s], second_out.at[s], sems.at[s]).start()
            half[...] = mm(left[s], step[...]).astype(bf16)
            update = mm(half[...], right[s], ((1,), (1,))).astype(bf16)
            for y in range(per):
                for z in range(bands):
                    row = (y * bands + z) * rows
                    out[z * per + y, s] = update[row : row + rows]
        for s in range(slots):
            pltpu.make_async_copy(new.at[s], second_out.at[s], sems.at[s]).wait()

    scalar = pl.BlockSpec(memory_space=SMEM)
    whole = pl.BlockSpec(memory_space=VMEM)
    return pl.pallas_call(
        body,
        in_specs=[scalar] * 2 + [whole] * (len(squares) + 5),
        out_specs=[whole, pl.BlockSpec(memory_space=HBM)],
        out_shape=[
            jax.ShapeDtypeStruct((senders, slots, rows, n), bf16),
            HBM((slots, n, n), f32),
        ],
        scratch_shapes=[
            pltpu.VMEM((slots, n, n), f32),
            pltpu.VMEM((n, n), bf16),
            pltpu.VMEM((n, n), bf16),
            pltpu.SemaphoreType.DMA((slots,)),
        ],
        compiler_params=pltpu.CompilerParams(vmem_limit_bytes=16 << 20),
        name="direction",
    )(table, me, *squares, *rotated)


def factors_body(bands, entries, table, me, *refs):
    *squares, pieces = refs[:-14]
    sources, outs, (news, olds), sems = refs[-14:-11], refs[-11:-8], (refs[-8:-5], refs[-5:-2]), refs[-2:]
    slots, n, _ = news[0].shape
    copies = [
        [
            pltpu.make_async_copy(src.at[s], dst.at[s], sems[0].at[s, i])
            for i, (src, dst) in enumerate(zip(sources, olds))
        ]
        for s in range(slots)
    ]
    for group in copies:
        for c in group:
            c.start()
    scale = clip_of(squares, entries)
    square = 0.1 * scale * scale
    done = []
    for s in range(slots):
        named = is_named(table, me[0] * slots + s)
        block = assemble(pieces, s, bands)
        for i in range(3):
            if i == 0:
                more = square * mm(block, block, ((1,), (1,)))
            elif i == 1:
                more = square * mm(block.T, block)
            else:
                more = (0.1 * scale) * block.astype(f32)
            copies[s][i].wait()
            old = olds[i][s]
            news[i][s] = jnp.where(named, 0.9 * old + more, old)
            done.append(pltpu.make_async_copy(news[i].at[s], outs[i].at[s], sems[1].at[s, i]))
            done[-1].start()
    for c in done:
        c.wait()


def factors(table, me, squares, pieces, left, right, first, bands, entries):
    slots, n, _ = left.shape
    scalar = pl.BlockSpec(memory_space=SMEM)
    whole = pl.BlockSpec(memory_space=VMEM)
    far = pl.BlockSpec(memory_space=HBM)

    def body(*refs):
        factors_body(bands, entries, *refs)

    return pl.pallas_call(
        body,
        in_specs=[scalar] * 2 + [whole] * (len(squares) + 1) + [far] * 3,
        out_specs=[far] * 3,
        out_shape=[HBM(left.shape, f32)] * 3,
        scratch_shapes=[pltpu.VMEM((slots, n, n), f32)] * 6
        + [pltpu.SemaphoreType.DMA((slots, 3))] * 2,
        compiler_params=pltpu.CompilerParams(vmem_limit_bytes=24 << 20),
        cost_estimate=pl.CostEstimate(
            flops=slots * 4 * n**3, bytes_accessed=slots * 26 * n * n, transcendentals=0
        ),
        name="factors",
    )(table, me, *squares, pieces, *in_hbm(left, right, first))


def per_device(
    replica_grads,
    owners,
    left_factor,
    right_factor,
    left_basis,
    right_basis,
    first_moment,
    second_moment,
):
    rows_dev = replica_grads.shape[1]
    shards = lax.axis_size("fsdp")
    slots, n = left_factor.shape[1:3]
    per_band = n // rows_dev
    bands = shards // per_band
    dp = lax.axis_size("dp")
    dp_me = lax.axis_index("dp").astype(jnp.int32)
    me = lax.axis_index("fsdp").astype(jnp.int32)
    place = jnp.stack([dp_me // 2, dp_me % 2, me // per_band])
    table = jnp.concatenate([owners, (me // per_band).reshape(1, 1)], axis=1)
    me = me.reshape(1)
    core = [("dp", [(d, d ^ 1) for d in range(dp)])]
    along_x = [("dp", [(d, (d + 2 * h) % dp) for d in range(dp)]) for h in range(1, dp // 2)]
    along_y = [
        ("fsdp", [(i, i // per_band * per_band + (i + h) % per_band) for i in range(shards)])
        for h in range(1, per_band)
    ]
    along_z = [
        ("fsdp", [(i, (i + h * per_band) % shards) for i in range(shards)])
        for h in range(1, bands)
    ]
    parts = sum_over_replicas(place, replica_grads[0], bands)
    prepared = prepare(left_basis[0], right_basis[0], first_moment[0])
    parts, prepared = lax.optimization_barrier((parts, prepared))
    sums = finish(place, *parts, bands)
    rows, width = sums[0].shape[0], sums[0].shape[1] - LANES
    cols = width // n
    entries = rows_dev * shards * replica_grads.shape[2]
    spread = exchange(sums, along_z)
    one = jax.ShapeDtypeStruct((8, LANES), f32)
    out = [jax.ShapeDtypeStruct((shards * slots, rows, n), bf16), one]
    sent, square = local(dispatch_body, [table, *spread], out, "dispatch")
    sent = sent.reshape(shards, slots, rows, n)
    pieces = lax.all_to_all(sent, "fsdp", split_axis=0, concat_axis=0, tiled=True)
    for steps in (core, along_x):
        arrived = [lax.ppermute(square, *step) for step in steps]
        square = local(plus_body, [place, square, *arrived], one, "plus")
    squares = [square] + [lax.ppermute(square, *step) for step in along_y]
    rotated = rotate(pieces, prepared, second_moment[0], bands)
    update, second_new = direction(owners, me, squares, rotated, bands, shards, entries)
    back = lax.all_to_all(update, "fsdp", split_axis=0, concat_axis=0, tiled=True)
    back, pieces = lax.optimization_barrier((back, pieces))
    new = factors(
        owners, me, squares, pieces, left_factor[0], right_factor[0], first_moment[0], bands, entries
    )
    left_new, right_new, first_new = new
    out = [jax.ShapeDtypeStruct((rows, width), bf16)] * bands
    mine = local(collect_body, [table, back.reshape(shards * slots, rows, n)], out, "collect")
    out = jax.ShapeDtypeStruct((bands, rows, width), bf16)
    result = local(put_body, [table, *exchange(mine, along_z)], out, "put").reshape(rows_dev, width)
    return (result, left_new[None], right_new[None], first_new[None], second_new[None])


def solution(mesh):
    state = P("dp", "fsdp", None, None)
    return jax.shard_map(
        per_device,
        mesh=mesh,
        in_specs=(P("dp", "fsdp", None), P("dp", None)) + (state,) * 6,
        out_specs=(P("fsdp", "dp"),) + (state,) * 4,
        check_vma=False,
    )
```

```python
import jax
import jax.numpy as jnp
from jax import lax
from jax.experimental import pallas as pl
from jax.experimental.pallas import tpu as pltpu
from jax.sharding import PartitionSpec as P

f32 = jnp.float32
bf16 = jnp.bfloat16
SMEM = pltpu.MemorySpace.SMEM
VMEM = pltpu.MemorySpace.VMEM
HBM = pltpu.MemorySpace.HBM
LANES = 128


def in_hbm(*arrays):
    return [pltpu.with_memory_space_constraint(a, HBM) for a in arrays]


def split3(value):
    head, rest = split(value)
    mid, tail = split(value - head.astype(f32))
    return head, mid, tail


def split(value):
    head = value.astype(bf16)
    return head, (value - head.astype(f32)).astype(bf16)


def mm(a, b, dims=((1,), (0,))):
    return lax.dot_general(a, b, (dims, ((), ())), preferred_element_type=f32)


def tiles(count, size=32):
    return [slice(r, r + size) for r in range(0, count, size)]


def prepare_body(
    left_src, right_src, first_src, lt_dst, l_dst, r_dst, rot_dst, *scratch
):
    left, right, first, lt, low, head, rot, lt_both, half, tail, product, sems, out_sems = scratch
    slots, n, _ = left.shape
    pairs = ((left_src, left), (first_src, first), (right_src, right))
    copies = [
        [
            pltpu.make_async_copy(src.at[s], dst.at[s], sems.at[s, i])
            for i, (src, dst) in enumerate(pairs)
        ]
        for s in range(slots)
    ]
    for group in copies:
        for c in group:
            c.start()
    pairs = ((lt, lt_dst), (low, l_dst), (head, r_dst), (rot, rot_dst))
    outs = [
        [
            pltpu.make_async_copy(src.at[s], dst.at[s], out_sems.at[s, i])
            for i, (src, dst) in enumerate(pairs)
        ]
        for s in range(slots)
    ]
    for s in range(slots):
        copies[s][0].wait()
        for rows in tiles(n, LANES):
            above, below = split(left[s, rows].T)
            lt[s, :, rows] = above
            lt_both[:n, rows] = above
            lt_both[n:, rows] = below
        outs[s][0].start()
        for rows in tiles(n):
            low[s, rows] = left[s, rows].astype(bf16)
        outs[s][1].start()
        copies[s][1].wait()
        for rows in tiles(n):
            half[rows] = first[s, rows].astype(bf16)
        product[...] = mm(lt_both[...], half[...])
        copies[s][2].wait()
        for rows, more in zip(tiles(n), tiles(2 * n)[n // 32 :]):
            half[rows] = (product[rows] + product[more]).astype(bf16)
            head[s, rows], tail[rows] = split(right[s, rows])
        outs[s][2].start()
        rot[s] = 0.9 * (mm(half[...], head[s]) + mm(half[...], tail[...]))
        outs[s][3].start()
    for group in outs:
        for c in group:
            c.wait()


def prepare(left_basis, right_basis, first_moment):
    slots, n, _ = left_basis.shape
    far = pl.BlockSpec(memory_space=HBM)
    return pl.pallas_call(
        prepare_body,
        in_specs=[far] * 3,
        out_specs=[far] * 4,
        out_shape=[HBM((slots, n, n), bf16)] * 3 + [HBM((slots, n, n), f32)],
        scratch_shapes=[pltpu.VMEM((slots, n, n), f32)] * 3
        + [pltpu.VMEM((slots, n, n), bf16)] * 3
        + [
            pltpu.VMEM((slots, n, n), f32),
            pltpu.VMEM((2 * n, n), bf16),
            pltpu.VMEM((n, n), bf16),
            pltpu.VMEM((n, n), bf16),
            pltpu.VMEM((2 * n, n), f32),
            pltpu.SemaphoreType.DMA((slots, 3)),
            pltpu.SemaphoreType.DMA((slots, 4)),
        ],
        compiler_params=pltpu.CompilerParams(vmem_limit_bytes=24 << 20),
        cost_estimate=pl.CostEstimate(
            flops=slots * 8 * n**3, bytes_accessed=slots * 22 * n * n, transcendentals=0
        ),
        name="prepare",
    )(*in_hbm(left_basis, right_basis, first_moment))


def local(body, arrays, out_shape, name, limit=8 << 20, cost=None):
    return pl.pallas_call(
        body,
        in_specs=[pl.BlockSpec(memory_space=SMEM)]
        + [pl.BlockSpec(memory_space=VMEM)] * (len(arrays) - 1),
        out_specs=jax.tree.map(
            lambda _: pl.BlockSpec(memory_space=VMEM), out_shape, is_leaf=lambda o: hasattr(o, "shape")
        ),
        out_shape=out_shape,
        compiler_params=pltpu.CompilerParams(vmem_limit_bytes=limit),
        cost_estimate=cost,
        name=name,
    )(*arrays)


def dispatch_body(table, *refs):
    *srcs, dst, square = refs
    n = dst.shape[2]
    bands = len(srcs)
    width = srcs[0].shape[1] - LANES
    cols = width // n
    z = table[0, bands * cols]
    total = jnp.zeros(square.shape, f32)
    for j, src in enumerate(srcs):
        band = lax.rem(z + bands - j, bands)
        for c in range(cols):
            dst[table[0, band * cols + c]] = src[:, c * n : (c + 1) * n]
        terms = src[:, width:].astype(f32)
        for t in range(3):
            total = total + terms[8 * t : 8 * t + 8]
    square[...] = total


def collect_body(table, src, *dsts):
    n = src.shape[2]
    bands = len(dsts)
    cols = dsts[0].shape[1] // n
    z = table[0, bands * cols]
    for j, dst in enumerate(dsts):
        band = lax.rem(z + j, bands)
        for c in range(cols):
            dst[:, c * n : (c + 1) * n] = src[table[0, band * cols + c]]


def put_body(table, *refs):
    *srcs, dst = refs
    bands = len(srcs)
    z = table[0, table.shape[1] - 1]
    for j, src in enumerate(srcs):
        dst[lax.rem(z + bands - j, bands)] = src[...]


def plus_body(place, *refs):
    total = refs[0][...]
    for ref in refs[1:-1]:
        total = total + ref[...]
    refs[-1][...] = total


def load(place, grads, width):
    rows, columns = grads.shape
    chips = columns // width // 2
    groups = ((2,), (1, 3, 0))

    def body(place, src, *refs):
        *dsts, sems = refs
        copies = []
        for i, dst in enumerate(dsts):
            core = 1 - place[1] if i < 2 else place[1]
            for k, j in enumerate(groups[i % 2]):
                slab = 2 * lax.rem(place[0] + j, chips) + core
                columns = pl.ds(pl.multiple_of(slab * width, width), width)
                copies.append(
                    pltpu.make_async_copy(src.at[:, columns], dst.at[k], sems.at[len(copies)])
                )
        for c in copies:
            c.start()
        for c in copies:
            c.wait()

    return pl.pallas_call(
        body,
        in_specs=[pl.BlockSpec(memory_space=SMEM), pl.BlockSpec(memory_space=HBM)],
        out_specs=[pl.BlockSpec(memory_space=VMEM)] * 4,
        out_shape=[VMEM((len(g), rows, width), bf16) for g in groups * 2],
        scratch_shapes=[pltpu.SemaphoreType.DMA((2 * chips,))],
        compiler_params=pltpu.CompilerParams(vmem_limit_bytes=2 << 20),
        name="load",
    )(place, *in_hbm(grads))


def pair(body, place, near, far, outs, name):
    low = near.shape[1] // 2

    def run(place, near, far, *outs):
        def total(i, a):
            part = slice(a * low, (a + 1) * low)
            return near[i, part].astype(f32) + far[i, part].astype(f32)

        body(total, low, *outs)

    out = [jax.ShapeDtypeStruct(shape, kind) for shape, kind in outs]
    return local(run, [place, near, far], out, name)


def far_body(total, low, to_right, to_left):
    to_right[...] = total(0, 0).astype(bf16)
    to_left[...] = total(0, 1).astype(bf16)


def near_body(total, low, to_right, to_left, keep_right, keep_left, own):
    keep_right[...] = total(0, 0)
    to_right[...] = total(0, 1).astype(bf16)
    to_left[...] = total(1, 0).astype(bf16)
    keep_left[...] = total(1, 1)
    for a in range(2):
        own[a * low : (a + 1) * low] = total(2, a)


def relay(place, kept, arrived):
    def body(place, kept, arrived, out):
        out[...] = (kept[...] + arrived[...].astype(f32)).astype(bf16)

    out = jax.ShapeDtypeStruct(kept.shape, bf16)
    return local(body, (place, kept, arrived), out, "relay")


def direct_body(place, own, left_direct, right_direct, out):
    low = left_direct.shape[0]
    out[:low] = own[:low] + right_direct[...].astype(f32)
    out[low:] = own[low:] + left_direct[...].astype(f32)


def finish(place, own, left_sum, right_sum, bands):
    rows, width = own.shape
    low = rows // 2
    piece = rows // bands

    def body(place, own, left_sum, right_sum, *outs):
        total = jnp.zeros((8, LANES), f32)
        for q in range(bands):
            relayed = left_sum if q * piece < low else right_sum
            part = slice(q * piece % low, q * piece % low + piece)
            value = own[q * piece : (q + 1) * piece] + relayed[part].astype(f32)
            step = lax.rem(q - place[2] + bands, bands)
            rounded = value.astype(bf16)
            for j in range(bands):

                @pl.when(step == j)
                def _():
                    outs[j][:, :width] = rounded

            by_row = jnp.sum((value * value).reshape(piece // 8, 8, width), axis=0)
            for c in range(width // LANES):
                total = total + by_row[:, c * LANES : (c + 1) * LANES]
        terms = [t.astype(f32) for t in split3(total)]
        terms.append(jnp.zeros((piece - 24, LANES), f32))
        terms = jnp.concatenate(terms, axis=0).astype(bf16)
        for out in outs:
            out[:, width:] = terms

    arrays = [place, own, left_sum, right_sum]
    out = [jax.ShapeDtypeStruct((piece, width + LANES), bf16)] * bands
    return local(body, arrays, out, "finish", 12 << 20)


def sum_over_replicas(place, grads, bands):
    size = lax.axis_size("dp")
    rows, columns = grads.shape
    width = columns // size
    half = (rows // 2, width)
    swap = [(d, d ^ 1) for d in range(size)]
    up = [(d, (d + 2) % size) for d in range(size)]
    down = [(d, (d - 2) % size) for d in range(size)]
    far_there, near_there, far_here, near_here = load(place, grads, width)
    other = lax.ppermute(far_there, "dp", swap)
    other, near_there = lax.optimization_barrier((other, near_there))
    others = lax.ppermute(near_there, "dp", swap)
    to_right, to_left = pair(far_body, place, far_here, other, [(half, bf16)] * 2, "pair_far")
    left_far = lax.ppermute(to_right, "dp", up)
    right_far = lax.ppermute(to_left, "dp", down)
    outs = [(half, bf16)] * 2 + [(half, f32)] * 2 + [((rows, width), f32)]
    to_right, to_left, keep_right, keep_left, own = pair(
        near_body, place, near_here, others, outs, "pair_near"
    )
    left_direct = lax.ppermute(to_right, "dp", up)
    right_direct = lax.ppermute(to_left, "dp", down)
    left_sum = lax.ppermute(relay(place, keep_right, left_far), "dp", up)
    right_sum = lax.ppermute(relay(place, keep_left, right_far), "dp", down)
    out = jax.ShapeDtypeStruct((rows, width), f32)
    own = local(direct_body, [place, own, left_direct, right_direct], out, "direct", cost=pl.CostEstimate(flops=2 * rows * width, bytes_accessed=12 * rows * width, transcendentals=0))
    return own, left_sum, right_sum


def exchange(arrays, steps):
    order = sorted(range(1, len(arrays)), key=lambda j: -min(j, len(arrays) - j))
    got = {0: arrays[0]}
    for j in order:
        got[j] = lax.ppermute(arrays[j], *steps[j - 1])
    return [got[j] for j in range(len(arrays))]


def assemble(pieces, slot, bands):
    per = pieces.shape[0] // bands
    return jnp.concatenate(
        [pieces[z * per + y, slot] for y in range(per) for z in range(bands)], axis=0
    )


def is_named(table, slot):
    named = table[0, 0] == slot
    for b in range(1, table.shape[1]):
        named = jnp.logical_or(named, table[0, b] == slot)
    return named


def clip_of(squares, entries):
    total = squares[0][...]
    for square in squares[1:]:
        total = total + square[...]
    total = jnp.sum(jnp.sum(total, axis=0, keepdims=True), axis=1, keepdims=True)
    return jnp.minimum(1.0, 1.0 / jnp.sqrt(total / entries + 1e-06))


def rotate(pieces, prepared, second, bands):
    slots, n, _ = second.shape

    def body(pieces, lt_src, l_src, r_src, rot_src, old_src, *refs):
        out, left, right, rot, old, lt, half, sems = refs
        pairs = ((lt_src, lt), (r_src, right), (rot_src, rot), (old_src, old), (l_src, left))
        copies = [
            pltpu.make_async_copy(src.at[s], dst.at[s], sems.at[s, i])
            for s in range(slots)
            for i, (src, dst) in enumerate(pairs)
        ]
        for c in copies:
            c.start()
        for s in range(slots):
            group = copies[s * len(pairs) : (s + 1) * len(pairs)]
            block = assemble(pieces, s, bands)
            group[0].wait()
            half[...] = mm(lt[s], block).astype(bf16)
            group[1].wait()
            out[s] = mm(half[...], right[s])
            for c in group[2:]:
                c.wait()

    whole = pl.BlockSpec(memory_space=VMEM)
    far = pl.BlockSpec(memory_space=HBM)
    return pl.pallas_call(
        body,
        in_specs=[whole] + [far] * 5,
        out_specs=[whole] * 5,
        out_shape=[
            VMEM((slots, n, n), f32),
            VMEM((slots, n, n), bf16),
            VMEM((slots, n, n), bf16),
            VMEM((slots, n, n), f32),
            VMEM((slots, n, n), f32),
        ],
        scratch_shapes=[
            pltpu.VMEM((slots, n, n), bf16),
            pltpu.VMEM((n, n), bf16),
            pltpu.SemaphoreType.DMA((slots, 5)),
        ],
        compiler_params=pltpu.CompilerParams(vmem_limit_bytes=12 << 20),
        name="rotate",
    )(pieces, *in_hbm(*prepared, second))


def direction(table, me, squares, rotated, bands, senders, entries):
    slots, n, _ = rotated[0].shape
    rows = n // senders
    per = senders // bands

    def body(table, me, *refs):
        squares, rest = refs[: len(refs) - 11], refs[len(refs) - 11 :]
        product, left, right, rot, old, out, second_out, new, step, half, sems = rest
        scale = clip_of(squares, entries)
        for s in range(slots):
            named = is_named(table, me[0] * slots + s)
            for r in tiles(n):
                turned = product[s, r] * scale
                before = old[s, r]
                value = 0.95 * before + 0.05 * turned * turned
                new[s, r] = jnp.where(named, value, before)
                ahead = rot[s, r] + 0.1 * turned
                step[r] = (ahead * pl.reciprocal(jnp.sqrt(value) + 1e-08, approx=True)).astype(bf16)
            pltpu.make_async_copy(new.at[s], second_out.at[s], sems.at[s]).start()
            half[...] = mm(left[s], step[...]).astype(bf16)
            update = mm(half[...], right[s], ((1,), (1,))).astype(bf16)
            for y in range(per):
                for z in range(bands):
                    row = (y * bands + z) * rows
                    out[z * per + y, s] = update[row : row + rows]
        for s in range(slots):
            pltpu.make_async_copy(new.at[s], second_out.at[s], sems.at[s]).wait()

    scalar = pl.BlockSpec(memory_space=SMEM)
    whole = pl.BlockSpec(memory_space=VMEM)
    return pl.pallas_call(
        body,
        in_specs=[scalar] * 2 + [whole] * (len(squares) + 5),
        out_specs=[whole, pl.BlockSpec(memory_space=HBM)],
        out_shape=[
            jax.ShapeDtypeStruct((senders, slots, rows, n), bf16),
            HBM((slots, n, n), f32),
        ],
        scratch_shapes=[
            pltpu.VMEM((slots, n, n), f32),
            pltpu.VMEM((n, n), bf16),
            pltpu.VMEM((n, n), bf16),
            pltpu.SemaphoreType.DMA((slots,)),
        ],
        compiler_params=pltpu.CompilerParams(vmem_limit_bytes=16 << 20),
        name="direction",
    )(table, me, *squares, *rotated)


def factors_body(bands, entries, table, me, *refs):
    *squares, pieces = refs[:-16]
    sources, outs, news, olds = (refs[i : i + 3] for i in range(-16, -4, 3))
    block, product, *sems = refs[-4:]
    slots, n, _ = news[0].shape
    copies = [
        [
            pltpu.make_async_copy(src.at[s], dst.at[s], sems[0].at[s, i])
            for i, (src, dst) in enumerate(zip(sources, olds))
        ]
        for s in range(slots)
    ]
    for group in copies:
        for c in group:
            c.start()
    scale = clip_of(squares, entries)
    square = 0.1 * scale * scale
    done = []
    for s in range(slots):
        named = is_named(table, me[0] * slots + s)
        block[...] = assemble(pieces, s, bands)
        for i in range(3):
            if i == 0:
                product[...] = mm(block[...], block[...], ((1,), (1,)))
            elif i == 1:
                product[...] = mm(block[...].T, block[...])
            copies[s][i].wait()
            for r in tiles(n):
                old = olds[i][s, r]
                more = square * product[r] if i < 2 else (0.1 * scale) * block[r].astype(f32)
                news[i][s, r] = jnp.where(named, 0.9 * old + more, old)
            done.append(pltpu.make_async_copy(news[i].at[s], outs[i].at[s], sems[1].at[s, i]))
            done[-1].start()
    for c in done:
        c.wait()


def factors(table, me, squares, pieces, left, right, first, bands, entries):
    slots, n, _ = left.shape
    scalar = pl.BlockSpec(memory_space=SMEM)
    whole = pl.BlockSpec(memory_space=VMEM)
    far = pl.BlockSpec(memory_space=HBM)

    def body(*refs):
        factors_body(bands, entries, *refs)

    return pl.pallas_call(
        body,
        in_specs=[scalar] * 2 + [whole] * (len(squares) + 1) + [far] * 3,
        out_specs=[far] * 3,
        out_shape=[HBM(left.shape, f32)] * 3,
        scratch_shapes=[pltpu.VMEM((slots, n, n), f32)] * 6
        + [pltpu.VMEM((n, n), bf16), pltpu.VMEM((n, n), f32)]
        + [pltpu.SemaphoreType.DMA((slots, 3))] * 2,
        compiler_params=pltpu.CompilerParams(vmem_limit_bytes=24 << 20),
        cost_estimate=pl.CostEstimate(
            flops=slots * 4 * n**3, bytes_accessed=slots * 26 * n * n, transcendentals=0
        ),
        name="factors",
    )(table, me, *squares, pieces, *in_hbm(left, right, first))


def per_device(
    replica_grads,
    owners,
    left_factor,
    right_factor,
    left_basis,
    right_basis,
    first_moment,
    second_moment,
):
    rows_dev = replica_grads.shape[1]
    shards = lax.axis_size("fsdp")
    slots, n = left_factor.shape[1:3]
    per_band = n // rows_dev
    bands = shards // per_band
    dp = lax.axis_size("dp")
    dp_me = lax.axis_index("dp").astype(jnp.int32)
    me = lax.axis_index("fsdp").astype(jnp.int32)
    place = jnp.stack([dp_me // 2, dp_me % 2, me // per_band])
    table = jnp.concatenate([owners, (me // per_band).reshape(1, 1)], axis=1)
    me = me.reshape(1)
    core = [("dp", [(d, d ^ 1) for d in range(dp)])]
    along_x = [("dp", [(d, (d + 2 * h) % dp) for d in range(dp)]) for h in range(1, dp // 2)]
    along_y = [
        ("fsdp", [(i, i // per_band * per_band + (i + h) % per_band) for i in range(shards)])
        for h in range(1, per_band)
    ]
    along_z = [
        ("fsdp", [(i, (i + h * per_band) % shards) for i in range(shards)])
        for h in range(1, bands)
    ]
    parts = sum_over_replicas(place, replica_grads[0], bands)
    prepared = prepare(left_basis[0], right_basis[0], first_moment[0])
    parts, prepared = lax.optimization_barrier((parts, prepared))
    sums = finish(place, *parts, bands)
    rows, width = sums[0].shape[0], sums[0].shape[1] - LANES
    cols = width // n
    entries = rows_dev * shards * replica_grads.shape[2]
    spread = exchange(sums, along_z)
    one = jax.ShapeDtypeStruct((8, LANES), f32)
    out = [jax.ShapeDtypeStruct((shards * slots, rows, n), bf16), one]
    sent, square = local(dispatch_body, [table, *spread], out, "dispatch")
    sent = sent.reshape(shards, slots, rows, n)
    pieces = lax.all_to_all(sent, "fsdp", split_axis=0, concat_axis=0, tiled=True)
    for steps in (core, along_x):
        arrived = [lax.ppermute(square, *step) for step in steps]
        square = local(plus_body, [place, square, *arrived], one, "plus")
    squares = [square] + [lax.ppermute(square, *step) for step in along_y]
    rotated = rotate(pieces, prepared, second_moment[0], bands)
    update, second_new = direction(owners, me, squares, rotated, bands, shards, entries)
    back = lax.all_to_all(update, "fsdp", split_axis=0, concat_axis=0, tiled=True)
    back, pieces = lax.optimization_barrier((back, pieces))
    new = factors(
        owners, me, squares, pieces, left_factor[0], right_factor[0], first_moment[0], bands, entries
    )
    left_new, right_new, first_new = new
    out = [jax.ShapeDtypeStruct((rows, width), bf16)] * bands
    mine = local(collect_body, [table, back.reshape(shards * slots, rows, n)], out, "collect")
    out = jax.ShapeDtypeStruct((bands, rows, width), bf16)
    result = local(put_body, [table, *exchange(mine, along_z)], out, "put").reshape(rows_dev, width)
    return (result, left_new[None], right_new[None], first_new[None], second_new[None])


def solution(mesh):
    state = P("dp", "fsdp", None, None)
    return jax.shard_map(
        per_device,
        mesh=mesh,
        in_specs=(P("dp", "fsdp", None), P("dp", None)) + (state,) * 6,
        out_specs=(P("fsdp", "dp"),) + (state,) * 4,
        check_vma=False,
    )
```

```python
import jax
import jax.numpy as jnp
from jax import lax
from jax.experimental import pallas as pl
from jax.experimental.pallas import tpu as pltpu
from jax.sharding import PartitionSpec as P

f32 = jnp.float32
bf16 = jnp.bfloat16
SMEM = pltpu.MemorySpace.SMEM
VMEM = pltpu.MemorySpace.VMEM
HBM = pltpu.MemorySpace.HBM
LANES = 128


def in_hbm(*arrays):
    return [pltpu.with_memory_space_constraint(a, HBM) for a in arrays]


def split3(value):
    head, rest = split(value)
    mid, tail = split(value - head.astype(f32))
    return head, mid, tail


def split(value):
    head = value.astype(bf16)
    return head, (value - head.astype(f32)).astype(bf16)


def mm(a, b, dims=((1,), (0,))):
    return lax.dot_general(a, b, (dims, ((), ())), preferred_element_type=f32)


def tiles(count, size=32):
    return [slice(r, r + size) for r in range(0, count, size)]


def prepare_body(
    left_src, right_src, first_src, lt_dst, l_dst, r_dst, rot_dst, *scratch
):
    left, right, first, lt, low, head, rot, lt_both, half, tail, product, sems, out_sems = scratch
    slots, n, _ = left.shape
    pairs = ((left_src, left), (first_src, first), (right_src, right))
    copies = [
        [
            pltpu.make_async_copy(src.at[s], dst.at[s], sems.at[s, i])
            for i, (src, dst) in enumerate(pairs)
        ]
        for s in range(slots)
    ]
    for group in copies:
        for c in group:
            c.start()
    pairs = ((lt, lt_dst), (low, l_dst), (head, r_dst), (rot, rot_dst))
    outs = [
        [
            pltpu.make_async_copy(src.at[s], dst.at[s], out_sems.at[s, i])
            for i, (src, dst) in enumerate(pairs)
        ]
        for s in range(slots)
    ]
    for s in range(slots):
        copies[s][0].wait()
        for rows in tiles(n, LANES):
            above, below = split(left[s, rows].T)
            lt[s, :, rows] = above
            lt_both[:n, rows] = above
            lt_both[n:, rows] = below
        outs[s][0].start()
        for rows in tiles(n):
            low[s, rows] = left[s, rows].astype(bf16)
        outs[s][1].start()
        copies[s][1].wait()
        for rows in tiles(n):
            half[rows] = first[s, rows].astype(bf16)
        product[...] = mm(lt_both[...], half[...])
        copies[s][2].wait()
        for rows, more in zip(tiles(n), tiles(2 * n)[n // 32 :]):
            half[rows] = (product[rows] + product[more]).astype(bf16)
            head[s, rows], tail[rows] = split(right[s, rows])
        outs[s][2].start()
        rot[s] = 0.9 * (mm(half[...], head[s]) + mm(half[...], tail[...]))
        outs[s][3].start()
    for group in outs:
        for c in group:
            c.wait()


def prepare(left_basis, right_basis, first_moment):
    slots, n, _ = left_basis.shape
    far = pl.BlockSpec(memory_space=HBM)
    return pl.pallas_call(
        prepare_body,
        in_specs=[far] * 3,
        out_specs=[far] * 4,
        out_shape=[HBM((slots, n, n), bf16)] * 3 + [HBM((slots, n, n), f32)],
        scratch_shapes=[pltpu.VMEM((slots, n, n), f32)] * 3
        + [pltpu.VMEM((slots, n, n), bf16)] * 3
        + [
            pltpu.VMEM((slots, n, n), f32),
            pltpu.VMEM((2 * n, n), bf16),
            pltpu.VMEM((n, n), bf16),
            pltpu.VMEM((n, n), bf16),
            pltpu.VMEM((2 * n, n), f32),
            pltpu.SemaphoreType.DMA((slots, 3)),
            pltpu.SemaphoreType.DMA((slots, 4)),
        ],
        compiler_params=pltpu.CompilerParams(vmem_limit_bytes=24 << 20),
        cost_estimate=pl.CostEstimate(
            flops=slots * 8 * n**3, bytes_accessed=slots * 22 * n * n, transcendentals=0
        ),
        name="prepare",
    )(*in_hbm(left_basis, right_basis, first_moment))


def local(body, arrays, out_shape, name, limit=8 << 20, cost=None):
    return pl.pallas_call(
        body,
        in_specs=[pl.BlockSpec(memory_space=SMEM)]
        + [pl.BlockSpec(memory_space=VMEM)] * (len(arrays) - 1),
        out_specs=jax.tree.map(
            lambda _: pl.BlockSpec(memory_space=VMEM), out_shape, is_leaf=lambda o: hasattr(o, "shape")
        ),
        out_shape=out_shape,
        compiler_params=pltpu.CompilerParams(vmem_limit_bytes=limit),
        cost_estimate=cost,
        name=name,
    )(*arrays)


def dispatch_body(table, *refs):
    *srcs, dst, square = refs
    n = dst.shape[2]
    bands = len(srcs)
    width = srcs[0].shape[1] - LANES
    cols = width // n
    z = table[0, bands * cols]
    total = jnp.zeros(square.shape, f32)
    for j, src in enumerate(srcs):
        band = lax.rem(z + bands - j, bands)
        for c in range(cols):
            dst[table[0, band * cols + c]] = src[:, c * n : (c + 1) * n]
        terms = src[:, width:].astype(f32)
        for t in range(3):
            total = total + terms[8 * t : 8 * t + 8]
    square[...] = total


def collect_body(table, src, *dsts):
    n = src.shape[2]
    bands = len(dsts)
    cols = dsts[0].shape[1] // n
    z = table[0, bands * cols]
    for j, dst in enumerate(dsts):
        band = lax.rem(z + j, bands)
        for c in range(cols):
            dst[:, c * n : (c + 1) * n] = src[table[0, band * cols + c]]


def put_body(table, *refs):
    *srcs, dst = refs
    bands = len(srcs)
    z = table[0, table.shape[1] - 1]
    for j, src in enumerate(srcs):
        dst[lax.rem(z + bands - j, bands)] = src[...]


def load(place, grads, width):
    rows, columns = grads.shape
    chips = columns // width // 2
    groups = ((2,), (1, 3, 0))

    def body(place, src, *refs):
        *dsts, sems = refs
        copies = []
        for i, dst in enumerate(dsts):
            core = 1 - place[1] if i < 2 else place[1]
            for k, j in enumerate(groups[i % 2]):
                slab = 2 * lax.rem(place[0] + j, chips) + core
                columns = pl.ds(pl.multiple_of(slab * width, width), width)
                copies.append(
                    pltpu.make_async_copy(src.at[:, columns], dst.at[k], sems.at[len(copies)])
                )
        for c in copies:
            c.start()
        for c in copies:
            c.wait()

    return pl.pallas_call(
        body,
        in_specs=[pl.BlockSpec(memory_space=SMEM), pl.BlockSpec(memory_space=HBM)],
        out_specs=[pl.BlockSpec(memory_space=VMEM)] * 4,
        out_shape=[VMEM((len(g), rows, width), bf16) for g in groups * 2],
        scratch_shapes=[pltpu.SemaphoreType.DMA((2 * chips,))],
        compiler_params=pltpu.CompilerParams(vmem_limit_bytes=2 << 20),
        name="load",
    )(place, *in_hbm(grads))


def pair(body, place, near, far, outs, name):
    low = near.shape[1] // 2

    def run(place, near, far, *outs):
        def total(i, a):
            part = slice(a * low, (a + 1) * low)
            return near[i, part].astype(f32) + far[i, part].astype(f32)

        body(total, low, *outs)

    out = [jax.ShapeDtypeStruct(shape, kind) for shape, kind in outs]
    return local(run, [place, near, far], out, name)


def far_body(total, low, to_right, to_left):
    to_right[...] = total(0, 0).astype(bf16)
    to_left[...] = total(0, 1).astype(bf16)


def near_body(total, low, to_right, to_left, keep_right, keep_left, own):
    keep_right[...] = total(0, 0)
    to_right[...] = total(0, 1).astype(bf16)
    to_left[...] = total(1, 0).astype(bf16)
    keep_left[...] = total(1, 1)
    for a in range(2):
        own[a * low : (a + 1) * low] = total(2, a)


def relay(place, kept, arrived):
    def body(place, kept, arrived, out):
        out[...] = (kept[...] + arrived[...].astype(f32)).astype(bf16)

    out = jax.ShapeDtypeStruct(kept.shape, bf16)
    return local(body, (place, kept, arrived), out, "relay")


def direct_body(place, own, left_direct, right_direct, out):
    low = left_direct.shape[0]
    out[:low] = own[:low] + right_direct[...].astype(f32)
    out[low:] = own[low:] + left_direct[...].astype(f32)


def finish(place, own, left_sum, right_sum, bands):
    rows, width = own.shape
    low = rows // 2
    piece = rows // bands

    def body(place, own, left_sum, right_sum, *outs):
        total = jnp.zeros((8, LANES), f32)
        for q in range(bands):
            relayed = left_sum if q * piece < low else right_sum
            part = slice(q * piece % low, q * piece % low + piece)
            value = own[q * piece : (q + 1) * piece] + relayed[part].astype(f32)
            step = lax.rem(q - place[2] + bands, bands)
            rounded = value.astype(bf16)
            for j in range(bands):

                @pl.when(step == j)
                def _():
                    outs[j][:, :width] = rounded

            by_row = jnp.sum((value * value).reshape(piece // 8, 8, width), axis=0)
            for c in range(width // LANES):
                total = total + by_row[:, c * LANES : (c + 1) * LANES]
        terms = [t.astype(f32) for t in split3(total)]
        terms.append(jnp.zeros((piece - 24, LANES), f32))
        terms = jnp.concatenate(terms, axis=0).astype(bf16)
        for out in outs:
            out[:, width:] = terms

    arrays = [place, own, left_sum, right_sum]
    out = [jax.ShapeDtypeStruct((piece, width + LANES), bf16)] * bands
    return local(body, arrays, out, "finish", 12 << 20)


def sum_over_replicas(place, grads, bands):
    size = lax.axis_size("dp")
    rows, columns = grads.shape
    width = columns // size
    half = (rows // 2, width)
    swap = [(d, d ^ 1) for d in range(size)]
    up = [(d, (d + 2) % size) for d in range(size)]
    down = [(d, (d - 2) % size) for d in range(size)]
    far_there, near_there, far_here, near_here = load(place, grads, width)
    other = lax.ppermute(far_there, "dp", swap)
    other, near_there = lax.optimization_barrier((other, near_there))
    others = lax.ppermute(near_there, "dp", swap)
    to_right, to_left = pair(far_body, place, far_here, other, [(half, bf16)] * 2, "pair_far")
    left_far = lax.ppermute(to_right, "dp", up)
    right_far = lax.ppermute(to_left, "dp", down)
    outs = [(half, bf16)] * 2 + [(half, f32)] * 2 + [((rows, width), f32)]
    to_right, to_left, keep_right, keep_left, own = pair(
        near_body, place, near_here, others, outs, "pair_near"
    )
    left_direct = lax.ppermute(to_right, "dp", up)
    right_direct = lax.ppermute(to_left, "dp", down)
    left_sum = lax.ppermute(relay(place, keep_right, left_far), "dp", up)
    right_sum = lax.ppermute(relay(place, keep_left, right_far), "dp", down)
    out = jax.ShapeDtypeStruct((rows, width), f32)
    own = local(direct_body, [place, own, left_direct, right_direct], out, "direct", cost=pl.CostEstimate(flops=2 * rows * width, bytes_accessed=12 * rows * width, transcendentals=0))
    return own, left_sum, right_sum


def exchange(arrays, steps):
    order = sorted(range(1, len(arrays)), key=lambda j: -min(j, len(arrays) - j))
    got = {0: arrays[0]}
    for j in order:
        got[j] = lax.ppermute(arrays[j], *steps[j - 1])
    return [got[j] for j in range(len(arrays))]


def assemble(pieces, slot, bands):
    per = pieces.shape[0] // bands
    return jnp.concatenate(
        [pieces[z * per + y, slot] for y in range(per) for z in range(bands)], axis=0
    )


def is_named(table, slot):
    named = table[0, 0] == slot
    for b in range(1, table.shape[1]):
        named = jnp.logical_or(named, table[0, b] == slot)
    return named


def clip_of(squares, entries):
    total = squares[0][...]
    for square in squares[1:]:
        total = total + square[...]
    total = jnp.sum(jnp.sum(total, axis=0, keepdims=True), axis=1, keepdims=True)
    return jnp.minimum(1.0, 1.0 / jnp.sqrt(total / entries + 1e-06))


def rotate(pieces, prepared, second, bands):
    slots, n, _ = second.shape

    def body(pieces, lt_src, l_src, r_src, rot_src, old_src, *refs):
        out, right, left, rot, old, lt, half, sems = refs
        pairs = [(src.at[s], dst.at[s]) for s in range(slots) for src, dst in ((lt_src, lt), (r_src, right))]
        pairs += [(src.at[0], dst.at[0]) for src, dst in ((rot_src, rot), (old_src, old), (l_src, left))]
        copies = [
            pltpu.make_async_copy(src, dst, sems.at[i]) for i, (src, dst) in enumerate(pairs)
        ]
        for c in copies:
            c.start()
        for s in range(slots):
            block = assemble(pieces, s, bands)
            copies[2 * s].wait()
            half[...] = mm(lt[s], block).astype(bf16)
            copies[2 * s + 1].wait()
            out[s] = mm(half[...], right[s])
        for c in copies[2 * slots :]:
            c.wait()

    whole = pl.BlockSpec(memory_space=VMEM)
    far = pl.BlockSpec(memory_space=HBM)
    return pl.pallas_call(
        body,
        in_specs=[whole] + [far] * 5,
        out_specs=[whole] * 5,
        out_shape=[
            VMEM((slots, n, n), f32),
            VMEM((slots, n, n), bf16),
            VMEM((1, n, n), bf16),
            VMEM((1, n, n), f32),
            VMEM((1, n, n), f32),
        ],
        scratch_shapes=[
            pltpu.VMEM((slots, n, n), bf16),
            pltpu.VMEM((n, n), bf16),
            pltpu.SemaphoreType.DMA((2 * slots + 3,)),
        ],
        compiler_params=pltpu.CompilerParams(vmem_limit_bytes=12 << 20),
        name="rotate",
    )(pieces, *in_hbm(*prepared, second))


def direction(table, me, squares, rotated, prepared, second, bands, senders, entries):
    slots, n, _ = rotated[0].shape
    rows = n // senders
    per = senders // bands

    def body(table, me, *refs):
        squares, rest = refs[: len(refs) - 18], refs[len(refs) - 18 :]
        product, right, left, rot, old, l_src, rot_src, old_src, out, second_out = rest[:10]
        left_more, rot_more, old_more, new, step, half, in_sems, sems = rest[10:]
        pairs = ((rot_src, rot_more), (old_src, old_more), (l_src, left_more))
        copies = [
            [
                pltpu.make_async_copy(src.at[s], dst.at[s - 1], in_sems.at[s, i])
                for i, (src, dst) in enumerate(pairs)
            ]
            for s in range(1, slots)
        ]
        for group in copies:
            for c in group:
                c.start()
        scale = clip_of(squares, entries)
        for s in range(slots):
            if s == 0:
                states = rot.at[0], old.at[0], left.at[0]
            else:
                states = rot_more.at[s - 1], old_more.at[s - 1], left_more.at[s - 1]
                for c in copies[s - 1]:
                    c.wait()
            named = is_named(table, me[0] * slots + s)
            for r in tiles(n):
                turned = product[s, r] * scale
                before = states[1][r]
                value = 0.95 * before + 0.05 * turned * turned
                new[s, r] = jnp.where(named, value, before)
                ahead = states[0][r] + 0.1 * turned
                step[r] = (ahead * pl.reciprocal(jnp.sqrt(value) + 1e-08, approx=True)).astype(bf16)
            pltpu.make_async_copy(new.at[s], second_out.at[s], sems.at[s]).start()
            half[...] = mm(states[2][...], step[...]).astype(bf16)
            update = mm(half[...], right[s], ((1,), (1,))).astype(bf16)
            for y in range(per):
                for z in range(bands):
                    row = (y * bands + z) * rows
                    out[z * per + y, s] = update[row : row + rows]
        for s in range(slots):
            pltpu.make_async_copy(new.at[s], second_out.at[s], sems.at[s]).wait()

    scalar = pl.BlockSpec(memory_space=SMEM)
    whole = pl.BlockSpec(memory_space=VMEM)
    far = pl.BlockSpec(memory_space=HBM)
    return pl.pallas_call(
        body,
        in_specs=[scalar] * 2 + [whole] * (len(squares) + 5) + [far] * 3,
        out_specs=[whole, far],
        out_shape=[
            jax.ShapeDtypeStruct((senders, slots, rows, n), bf16),
            HBM((slots, n, n), f32),
        ],
        scratch_shapes=[
            pltpu.VMEM((slots - 1, n, n), bf16),
            pltpu.VMEM((slots - 1, n, n), f32),
            pltpu.VMEM((slots - 1, n, n), f32),
            pltpu.VMEM((slots, n, n), f32),
            pltpu.VMEM((n, n), bf16),
            pltpu.VMEM((n, n), bf16),
            pltpu.SemaphoreType.DMA((slots, 3)),
            pltpu.SemaphoreType.DMA((slots,)),
        ],
        compiler_params=pltpu.CompilerParams(vmem_limit_bytes=16 << 20),
        name="direction",
    )(table, me, *squares, *rotated, *in_hbm(prepared[1], prepared[3], second))


def factors_body(bands, entries, table, me, *refs):
    *squares, pieces = refs[:-16]
    sources, outs, news, olds = (refs[i : i + 3] for i in range(-16, -4, 3))
    block, product, *sems = refs[-4:]
    slots, n, _ = news[0].shape
    copies = [
        [
            pltpu.make_async_copy(src.at[s], dst.at[s], sems[0].at[s, i])
            for i, (src, dst) in enumerate(zip(sources, olds))
        ]
        for s in range(slots)
    ]
    for group in copies:
        for c in group:
            c.start()
    scale = clip_of(squares, entries)
    square = 0.1 * scale * scale
    done = []
    for s in range(slots):
        named = is_named(table, me[0] * slots + s)
        block[...] = assemble(pieces, s, bands)
        for i in range(3):
            if i == 0:
                product[...] = mm(block[...], block[...], ((1,), (1,)))
            elif i == 1:
                product[...] = mm(block[...].T, block[...])
            copies[s][i].wait()
            for r in tiles(n):
                old = olds[i][s, r]
                more = square * product[r] if i < 2 else (0.1 * scale) * block[r].astype(f32)
                news[i][s, r] = jnp.where(named, 0.9 * old + more, old)
            done.append(pltpu.make_async_copy(news[i].at[s], outs[i].at[s], sems[1].at[s, i]))
            done[-1].start()
    for c in done:
        c.wait()


def factors(table, me, squares, pieces, left, right, first, bands, entries):
    slots, n, _ = left.shape
    scalar = pl.BlockSpec(memory_space=SMEM)
    whole = pl.BlockSpec(memory_space=VMEM)
    far = pl.BlockSpec(memory_space=HBM)

    def body(*refs):
        factors_body(bands, entries, *refs)

    return pl.pallas_call(
        body,
        in_specs=[scalar] * 2 + [whole] * (len(squares) + 1) + [far] * 3,
        out_specs=[far] * 3,
        out_shape=[HBM(left.shape, f32)] * 3,
        scratch_shapes=[pltpu.VMEM((slots, n, n), f32)] * 6
        + [pltpu.VMEM((n, n), bf16), pltpu.VMEM((n, n), f32)]
        + [pltpu.SemaphoreType.DMA((slots, 3))] * 2,
        compiler_params=pltpu.CompilerParams(vmem_limit_bytes=24 << 20),
        cost_estimate=pl.CostEstimate(
            flops=slots * 4 * n**3, bytes_accessed=slots * 26 * n * n, transcendentals=0
        ),
        name="factors",
    )(table, me, *squares, pieces, *in_hbm(left, right, first))


def per_device(
    replica_grads,
    owners,
    left_factor,
    right_factor,
    left_basis,
    right_basis,
    first_moment,
    second_moment,
):
    rows_dev = replica_grads.shape[1]
    shards = lax.axis_size("fsdp")
    slots, n = left_factor.shape[1:3]
    per_band = n // rows_dev
    bands = shards // per_band
    dp = lax.axis_size("dp")
    dp_me = lax.axis_index("dp").astype(jnp.int32)
    me = lax.axis_index("fsdp").astype(jnp.int32)
    place = jnp.stack([dp_me // 2, dp_me % 2, me // per_band])
    table = jnp.concatenate([owners, (me // per_band).reshape(1, 1)], axis=1)
    me = me.reshape(1)
    core = [("dp", [(d, d ^ 1) for d in range(dp)])]
    along_x = [("dp", [(d, (d + 2 * h) % dp) for d in range(dp)]) for h in range(1, dp // 2)]
    along_y = [
        ("fsdp", [(i, i // per_band * per_band + (i + h) % per_band) for i in range(shards)])
        for h in range(1, per_band)
    ]
    along_z = [
        ("fsdp", [(i, (i + h * per_band) % shards) for i in range(shards)])
        for h in range(1, bands)
    ]
    parts = sum_over_replicas(place, replica_grads[0], bands)
    prepared = prepare(left_basis[0], right_basis[0], first_moment[0])
    parts, prepared = lax.optimization_barrier((parts, prepared))
    sums = finish(place, *parts, bands)
    rows, width = sums[0].shape[0], sums[0].shape[1] - LANES
    cols = width // n
    entries = rows_dev * shards * replica_grads.shape[2]
    spread = exchange(sums, along_z)
    out = [
        jax.ShapeDtypeStruct((shards * slots, rows, n), bf16),
        jax.ShapeDtypeStruct((8, LANES), f32),
    ]
    sent, square = local(dispatch_body, [table, *spread], out, "dispatch")
    sent = sent.reshape(shards, slots, rows, n)
    pieces = lax.all_to_all(sent, "fsdp", split_axis=0, concat_axis=0, tiled=True)
    for steps in (core, along_x):
        square = sum([lax.ppermute(square, *step) for step in steps], square)
    squares = [square] + [lax.ppermute(square, *step) for step in along_y]
    rotated = rotate(pieces, prepared, second_moment[0], bands)
    update, second_new = direction(
        owners, me, squares, rotated, prepared, second_moment[0], bands, shards, entries
    )
    back = lax.all_to_all(update, "fsdp", split_axis=0, concat_axis=0, tiled=True)
    back, pieces = lax.optimization_barrier((back, pieces))
    new = factors(
        owners, me, squares, pieces, left_factor[0], right_factor[0], first_moment[0], bands, entries
    )
    left_new, right_new, first_new = new
    out = [jax.ShapeDtypeStruct((rows, width), bf16)] * bands
    mine = local(collect_body, [table, back.reshape(shards * slots, rows, n)], out, "collect")
    out = jax.ShapeDtypeStruct((bands, rows, width), bf16)
    result = local(put_body, [table, *exchange(mine, along_z)], out, "put").reshape(rows_dev, width)
    return (result, left_new[None], right_new[None], first_new[None], second_new[None])


def solution(mesh):
    state = P("dp", "fsdp", None, None)
    return jax.shard_map(
        per_device,
        mesh=mesh,
        in_specs=(P("dp", "fsdp", None), P("dp", None)) + (state,) * 6,
        out_specs=(P("fsdp", "dp"),) + (state,) * 4,
        check_vma=False,
    )
```

```python
import jax
import jax.numpy as jnp
from jax import lax
from jax.experimental import pallas as pl
from jax.experimental.pallas import tpu as pltpu
from jax.sharding import PartitionSpec as P

f32 = jnp.float32
bf16 = jnp.bfloat16
SMEM = pltpu.MemorySpace.SMEM
VMEM = pltpu.MemorySpace.VMEM
HBM = pltpu.MemorySpace.HBM
LANES = 128


def in_hbm(*arrays):
    return [pltpu.with_memory_space_constraint(a, HBM) for a in arrays]


def split3(value):
    head, rest = split(value)
    mid, tail = split(value - head.astype(f32))
    return head, mid, tail


def split(value):
    head = value.astype(bf16)
    return head, (value - head.astype(f32)).astype(bf16)


def mm(a, b, dims=((1,), (0,))):
    return lax.dot_general(a, b, (dims, ((), ())), preferred_element_type=f32)


def tiles(count, size=32):
    return [slice(r, r + size) for r in range(0, count, size)]


def prepare_body(
    left_src, right_src, first_src, lt_dst, l_dst, r_dst, rot_dst, *scratch
):
    left, right, first, lt, low, head, rot, lt_both, half, tail, product, sems, out_sems = scratch
    slots, n, _ = left.shape
    pairs = ((left_src, left), (first_src, first), (right_src, right))
    copies = [
        [
            pltpu.make_async_copy(src.at[s], dst.at[s], sems.at[s, i])
            for i, (src, dst) in enumerate(pairs)
        ]
        for s in range(slots)
    ]
    for group in copies:
        for c in group:
            c.start()
    pairs = ((lt, lt_dst), (low, l_dst), (head, r_dst), (rot, rot_dst))
    outs = [
        [
            pltpu.make_async_copy(src.at[s], dst.at[s], out_sems.at[s, i])
            for i, (src, dst) in enumerate(pairs)
        ]
        for s in range(slots)
    ]
    for s in range(slots):
        copies[s][0].wait()
        for rows in tiles(n, LANES):
            above, below = split(left[s, rows].T)
            lt[s, :, rows] = above
            lt_both[:n, rows] = above
            lt_both[n:, rows] = below
        outs[s][0].start()
        for rows in tiles(n):
            low[s, rows] = left[s, rows].astype(bf16)
        outs[s][1].start()
        copies[s][1].wait()
        for rows in tiles(n):
            half[rows] = first[s, rows].astype(bf16)
        product[...] = mm(lt_both[...], half[...])
        copies[s][2].wait()
        for rows, more in zip(tiles(n), tiles(2 * n)[n // 32 :]):
            half[rows] = (product[rows] + product[more]).astype(bf16)
            head[s, rows], tail[rows] = split(right[s, rows])
        outs[s][2].start()
        rot[s] = 0.9 * (mm(half[...], head[s]) + mm(half[...], tail[...]))
        outs[s][3].start()
    for group in outs:
        for c in group:
            c.wait()


def prepare(left_basis, right_basis, first_moment):
    slots, n, _ = left_basis.shape
    far = pl.BlockSpec(memory_space=HBM)
    return pl.pallas_call(
        prepare_body,
        in_specs=[far] * 3,
        out_specs=[far] * 4,
        out_shape=[HBM((slots, n, n), bf16)] * 3 + [HBM((slots, n, n), f32)],
        scratch_shapes=[pltpu.VMEM((slots, n, n), f32)] * 3
        + [pltpu.VMEM((slots, n, n), bf16)] * 3
        + [
            pltpu.VMEM((slots, n, n), f32),
            pltpu.VMEM((2 * n, n), bf16),
            pltpu.VMEM((n, n), bf16),
            pltpu.VMEM((n, n), bf16),
            pltpu.VMEM((2 * n, n), f32),
            pltpu.SemaphoreType.DMA((slots, 3)),
            pltpu.SemaphoreType.DMA((slots, 4)),
        ],
        compiler_params=pltpu.CompilerParams(vmem_limit_bytes=24 << 20),
        cost_estimate=pl.CostEstimate(
            flops=slots * 8 * n**3, bytes_accessed=slots * 22 * n * n, transcendentals=0
        ),
        name="prepare",
    )(*in_hbm(left_basis, right_basis, first_moment))


def local(body, arrays, out_shape, name, limit=8 << 20, cost=None):
    return pl.pallas_call(
        body,
        in_specs=[pl.BlockSpec(memory_space=SMEM)]
        + [pl.BlockSpec(memory_space=VMEM)] * (len(arrays) - 1),
        out_specs=jax.tree.map(
            lambda _: pl.BlockSpec(memory_space=VMEM), out_shape, is_leaf=lambda o: hasattr(o, "shape")
        ),
        out_shape=out_shape,
        compiler_params=pltpu.CompilerParams(vmem_limit_bytes=limit),
        cost_estimate=cost,
        name=name,
    )(*arrays)


def dispatch_body(table, *refs):
    *srcs, dst, square = refs
    n = dst.shape[2]
    bands = len(srcs)
    width = srcs[0].shape[1] - LANES
    cols = width // n
    z = table[0, bands * cols]
    total = jnp.zeros(square.shape, f32)
    for j, src in enumerate(srcs):
        band = lax.rem(z + bands - j, bands)
        for c in range(cols):
            dst[table[0, band * cols + c]] = src[:, c * n : (c + 1) * n]
        terms = src[:, width:].astype(f32)
        for t in range(3):
            total = total + terms[8 * t : 8 * t + 8]
    square[...] = total


def collect_body(table, src, *dsts):
    n = src.shape[2]
    bands = len(dsts)
    cols = dsts[0].shape[1] // n
    z = table[0, bands * cols]
    for j, dst in enumerate(dsts):
        band = lax.rem(z + j, bands)
        for c in range(cols):
            dst[:, c * n : (c + 1) * n] = src[table[0, band * cols + c]]


def put_body(table, *refs):
    *srcs, dst = refs
    bands = len(srcs)
    z = table[0, table.shape[1] - 1]
    for j, src in enumerate(srcs):
        dst[lax.rem(z + bands - j, bands)] = src[...]


def load(place, grads, width):
    rows, columns = grads.shape
    chips = columns // width // 2
    groups = ((2,), (1, 3, 0))

    def body(place, src, *refs):
        *dsts, sems = refs
        copies = []
        for i, dst in enumerate(dsts):
            core = 1 - place[1] if i < 2 else place[1]
            for k, j in enumerate(groups[i % 2]):
                slab = 2 * lax.rem(place[0] + j, chips) + core
                columns = pl.ds(pl.multiple_of(slab * width, width), width)
                copies.append(
                    pltpu.make_async_copy(src.at[:, columns], dst.at[k], sems.at[len(copies)])
                )
        for c in copies:
            c.start()
        for c in copies:
            c.wait()

    return pl.pallas_call(
        body,
        in_specs=[pl.BlockSpec(memory_space=SMEM), pl.BlockSpec(memory_space=HBM)],
        out_specs=[pl.BlockSpec(memory_space=VMEM)] * 4,
        out_shape=[VMEM((len(g), rows, width), bf16) for g in groups * 2],
        scratch_shapes=[pltpu.SemaphoreType.DMA((2 * chips,))],
        compiler_params=pltpu.CompilerParams(vmem_limit_bytes=2 << 20),
        name="load",
    )(place, *in_hbm(grads))


def pair(body, place, near, far, outs, name):
    low = near.shape[1] // 2

    def run(place, near, far, *outs):
        def total(i, a):
            part = slice(a * low, (a + 1) * low)
            return near[i, part].astype(f32) + far[i, part].astype(f32)

        body(total, low, *outs)

    out = [jax.ShapeDtypeStruct(shape, kind) for shape, kind in outs]
    return local(run, [place, near, far], out, name)


def far_body(total, low, to_right, to_left):
    to_right[...] = total(0, 0).astype(bf16)
    to_left[...] = total(0, 1).astype(bf16)


def near_body(total, low, to_right, to_left, keep_right, keep_left, own):
    keep_right[...] = total(0, 0)
    to_right[...] = total(0, 1).astype(bf16)
    to_left[...] = total(1, 0).astype(bf16)
    keep_left[...] = total(1, 1)
    for a in range(2):
        own[a * low : (a + 1) * low] = total(2, a)


def relay(place, kept, arrived):
    def body(place, kept, arrived, out):
        out[...] = (kept[...] + arrived[...].astype(f32)).astype(bf16)

    out = jax.ShapeDtypeStruct(kept.shape, bf16)
    return local(body, (place, kept, arrived), out, "relay")


def direct_body(place, own, left_direct, right_direct, out):
    low = left_direct.shape[0]
    out[:low] = own[:low] + right_direct[...].astype(f32)
    out[low:] = own[low:] + left_direct[...].astype(f32)


def finish(place, own, left_sum, right_sum, bands):
    rows, width = own.shape
    low = rows // 2
    piece = rows // bands

    def body(place, own, left_sum, right_sum, *outs):
        total = jnp.zeros((8, LANES), f32)
        for q in range(bands):
            relayed = left_sum if q * piece < low else right_sum
            part = slice(q * piece % low, q * piece % low + piece)
            value = own[q * piece : (q + 1) * piece] + relayed[part].astype(f32)
            step = lax.rem(q - place[2] + bands, bands)
            rounded = value.astype(bf16)
            for j in range(bands):

                @pl.when(step == j)
                def _():
                    outs[j][:, :width] = rounded

            by_row = jnp.sum((value * value).reshape(piece // 8, 8, width), axis=0)
            for c in range(width // LANES):
                total = total + by_row[:, c * LANES : (c + 1) * LANES]
        terms = [t.astype(f32) for t in split3(total)]
        terms.append(jnp.zeros((piece - 24, LANES), f32))
        terms = jnp.concatenate(terms, axis=0).astype(bf16)
        for out in outs:
            out[:, width:] = terms

    arrays = [place, own, left_sum, right_sum]
    out = [jax.ShapeDtypeStruct((piece, width + LANES), bf16)] * bands
    return local(body, arrays, out, "finish", 12 << 20)


def sum_over_replicas(place, grads, bands):
    size = lax.axis_size("dp")
    rows, columns = grads.shape
    width = columns // size
    half = (rows // 2, width)
    swap = [(d, d ^ 1) for d in range(size)]
    up = [(d, (d + 2) % size) for d in range(size)]
    down = [(d, (d - 2) % size) for d in range(size)]
    far_there, near_there, far_here, near_here = load(place, grads, width)
    other = lax.ppermute(far_there, "dp", swap)
    other, near_there = lax.optimization_barrier((other, near_there))
    others = lax.ppermute(near_there, "dp", swap)
    to_right, to_left = pair(far_body, place, far_here, other, [(half, bf16)] * 2, "pair_far")
    left_far = lax.ppermute(to_right, "dp", up)
    right_far = lax.ppermute(to_left, "dp", down)
    outs = [(half, bf16)] * 2 + [(half, f32)] * 2 + [((rows, width), f32)]
    to_right, to_left, keep_right, keep_left, own = pair(
        near_body, place, near_here, others, outs, "pair_near"
    )
    left_direct = lax.ppermute(to_right, "dp", up)
    right_direct = lax.ppermute(to_left, "dp", down)
    left_sum = lax.ppermute(relay(place, keep_right, left_far), "dp", up)
    right_sum = lax.ppermute(relay(place, keep_left, right_far), "dp", down)
    out = jax.ShapeDtypeStruct((rows, width), f32)
    own = local(direct_body, [place, own, left_direct, right_direct], out, "direct", cost=pl.CostEstimate(flops=2 * rows * width, bytes_accessed=12 * rows * width, transcendentals=0))
    return own, left_sum, right_sum


def exchange(arrays, steps):
    order = sorted(range(1, len(arrays)), key=lambda j: -min(j, len(arrays) - j))
    got = {0: arrays[0]}
    for j in order:
        got[j] = lax.ppermute(arrays[j], *steps[j - 1])
    return [got[j] for j in range(len(arrays))]


def assemble(pieces, slot, bands):
    per = pieces.shape[0] // bands
    return jnp.concatenate(
        [pieces[z * per + y, slot] for y in range(per) for z in range(bands)], axis=0
    )


def is_named(table, slot):
    named = table[0, 0] == slot
    for b in range(1, table.shape[1]):
        named = jnp.logical_or(named, table[0, b] == slot)
    return named


def clip_of(squares, entries):
    total = squares[0][...]
    for square in squares[1:]:
        total = total + square[...]
    total = jnp.sum(jnp.sum(total, axis=0, keepdims=True), axis=1, keepdims=True)
    return jnp.minimum(1.0, 1.0 / jnp.sqrt(total / entries + 1e-06))


def rotate(pieces, prepared, second, bands):
    slots, n, _ = second.shape

    def body(pieces, lt_src, l_src, r_src, rot_src, old_src, *refs):
        out, left, right, rot, old, lt, half, sems = refs
        pairs = ((lt_src, lt), (r_src, right), (rot_src, rot), (old_src, old), (l_src, left))
        copies = [
            pltpu.make_async_copy(src.at[s], dst.at[s], sems.at[s, i])
            for s in range(slots)
            for i, (src, dst) in enumerate(pairs)
        ]
        for c in copies:
            c.start()
        for s in range(slots):
            group = copies[s * len(pairs) : (s + 1) * len(pairs)]
            block = assemble(pieces, s, bands)
            group[0].wait()
            half[...] = mm(lt[s], block).astype(bf16)
            group[1].wait()
            out[s] = mm(half[...], right[s])
            for c in group[2:]:
                c.wait()

    whole = pl.BlockSpec(memory_space=VMEM)
    far = pl.BlockSpec(memory_space=HBM)
    return pl.pallas_call(
        body,
        in_specs=[whole] + [far] * 5,
        out_specs=[whole] * 5,
        out_shape=[
            VMEM((slots, n, n), f32),
            VMEM((slots, n, n), bf16),
            VMEM((slots, n, n), bf16),
            VMEM((slots, n, n), f32),
            VMEM((slots, n, n), f32),
        ],
        scratch_shapes=[
            pltpu.VMEM((slots, n, n), bf16),
            pltpu.VMEM((n, n), bf16),
            pltpu.SemaphoreType.DMA((slots, 5)),
        ],
        compiler_params=pltpu.CompilerParams(vmem_limit_bytes=12 << 20),
        name="rotate",
    )(pieces, *in_hbm(*prepared, second))


def direction(table, me, squares, rotated, bands, senders, entries):
    slots, n, _ = rotated[0].shape
    rows = n // senders
    per = senders // bands

    def body(table, me, *refs):
        squares, rest = refs[: len(refs) - 11], refs[len(refs) - 11 :]
        product, left, right, rot, old, out, second_out, new, step, half, sems = rest
        scale = clip_of(squares, entries)
        for s in range(slots):
            named = is_named(table, me[0] * slots + s)
            for r in tiles(n):
                turned = product[s, r] * scale
                before = old[s, r]
                value = 0.95 * before + 0.05 * turned * turned
                new[s, r] = jnp.where(named, value, before)
                ahead = rot[s, r] + 0.1 * turned
                step[r] = (ahead * pl.reciprocal(jnp.sqrt(value) + 1e-08, approx=True)).astype(bf16)
            pltpu.make_async_copy(new.at[s], second_out.at[s], sems.at[s]).start()
            half[...] = mm(left[s], step[...]).astype(bf16)
            update = mm(half[...], right[s], ((1,), (1,))).astype(bf16)
            for y in range(per):
                for z in range(bands):
                    row = (y * bands + z) * rows
                    out[z * per + y, s] = update[row : row + rows]
        for s in range(slots):
            pltpu.make_async_copy(new.at[s], second_out.at[s], sems.at[s]).wait()

    scalar = pl.BlockSpec(memory_space=SMEM)
    whole = pl.BlockSpec(memory_space=VMEM)
    return pl.pallas_call(
        body,
        in_specs=[scalar] * 2 + [whole] * (len(squares) + 5),
        out_specs=[whole, pl.BlockSpec(memory_space=HBM)],
        out_shape=[
            jax.ShapeDtypeStruct((senders, slots, rows, n), bf16),
            HBM((slots, n, n), f32),
        ],
        scratch_shapes=[
            pltpu.VMEM((slots, n, n), f32),
            pltpu.VMEM((n, n), bf16),
            pltpu.VMEM((n, n), bf16),
            pltpu.SemaphoreType.DMA((slots,)),
        ],
        compiler_params=pltpu.CompilerParams(vmem_limit_bytes=16 << 20),
        name="direction",
    )(table, me, *squares, *rotated)


def factors_body(bands, entries, table, me, *refs):
    *squares, pieces = refs[:-16]
    sources, outs, news, olds = (refs[i : i + 3] for i in range(-16, -4, 3))
    block, product, *sems = refs[-4:]
    slots, n, _ = news[0].shape
    copies = [
        [
            pltpu.make_async_copy(src.at[s], dst.at[s], sems[0].at[s, i])
            for i, (src, dst) in enumerate(zip(sources, olds))
        ]
        for s in range(slots)
    ]
    for group in copies:
        for c in group:
            c.start()
    scale = clip_of(squares, entries)
    square = 0.1 * scale * scale
    done = []
    for s in range(slots):
        named = is_named(table, me[0] * slots + s)
        block[...] = assemble(pieces, s, bands)
        for i in range(3):
            if i == 0:
                product[...] = mm(block[...], block[...], ((1,), (1,)))
            elif i == 1:
                product[...] = mm(block[...].T, block[...])
            copies[s][i].wait()
            for r in tiles(n):
                old = olds[i][s, r]
                more = square * product[r] if i < 2 else (0.1 * scale) * block[r].astype(f32)
                news[i][s, r] = jnp.where(named, 0.9 * old + more, old)
            done.append(pltpu.make_async_copy(news[i].at[s], outs[i].at[s], sems[1].at[s, i]))
            done[-1].start()
    for c in done:
        c.wait()


def factors(table, me, squares, pieces, left, right, first, bands, entries):
    slots, n, _ = left.shape
    scalar = pl.BlockSpec(memory_space=SMEM)
    whole = pl.BlockSpec(memory_space=VMEM)
    far = pl.BlockSpec(memory_space=HBM)

    def body(*refs):
        factors_body(bands, entries, *refs)

    return pl.pallas_call(
        body,
        in_specs=[scalar] * 2 + [whole] * (len(squares) + 1) + [far] * 3,
        out_specs=[far] * 3,
        out_shape=[HBM(left.shape, f32)] * 3,
        scratch_shapes=[pltpu.VMEM((slots, n, n), f32)] * 6
        + [pltpu.VMEM((n, n), bf16), pltpu.VMEM((n, n), f32)]
        + [pltpu.SemaphoreType.DMA((slots, 3))] * 2,
        compiler_params=pltpu.CompilerParams(vmem_limit_bytes=24 << 20),
        cost_estimate=pl.CostEstimate(
            flops=slots * 4 * n**3, bytes_accessed=slots * 26 * n * n, transcendentals=0
        ),
        name="factors",
    )(table, me, *squares, pieces, *in_hbm(left, right, first))


def per_device(
    replica_grads,
    owners,
    left_factor,
    right_factor,
    left_basis,
    right_basis,
    first_moment,
    second_moment,
):
    rows_dev = replica_grads.shape[1]
    shards = lax.axis_size("fsdp")
    slots, n = left_factor.shape[1:3]
    per_band = n // rows_dev
    bands = shards // per_band
    dp = lax.axis_size("dp")
    dp_me = lax.axis_index("dp").astype(jnp.int32)
    me = lax.axis_index("fsdp").astype(jnp.int32)
    place = jnp.stack([dp_me // 2, dp_me % 2, me // per_band])
    table = jnp.concatenate([owners, (me // per_band).reshape(1, 1)], axis=1)
    me = me.reshape(1)
    core = [("dp", [(d, d ^ 1) for d in range(dp)])]
    along_x = [("dp", [(d, (d + 2 * h) % dp) for d in range(dp)]) for h in range(1, dp // 2)]
    along_y = [
        ("fsdp", [(i, i // per_band * per_band + (i + h) % per_band) for i in range(shards)])
        for h in range(1, per_band)
    ]
    along_z = [
        ("fsdp", [(i, (i + h * per_band) % shards) for i in range(shards)])
        for h in range(1, bands)
    ]
    parts = sum_over_replicas(place, replica_grads[0], bands)
    prepared = prepare(left_basis[0], right_basis[0], first_moment[0])
    parts, prepared = lax.optimization_barrier((parts, prepared))
    sums = finish(place, *parts, bands)
    rows, width = sums[0].shape[0], sums[0].shape[1] - LANES
    cols = width // n
    entries = rows_dev * shards * replica_grads.shape[2]
    spread = exchange(sums, along_z)
    out = [
        jax.ShapeDtypeStruct((shards * slots, rows, n), bf16),
        jax.ShapeDtypeStruct((8, LANES), f32),
    ]
    sent, square = local(dispatch_body, [table, *spread], out, "dispatch")
    sent = sent.reshape(shards, slots, rows, n)
    pieces = lax.all_to_all(sent, "fsdp", split_axis=0, concat_axis=0, tiled=True)
    for steps in (core, along_x):
        square = sum([lax.ppermute(square, *step) for step in steps], square)
    squares = [square] + [lax.ppermute(square, *step) for step in along_y]
    rotated = rotate(pieces, prepared, second_moment[0], bands)
    update, second_new = direction(owners, me, squares, rotated, bands, shards, entries)
    back = lax.all_to_all(update, "fsdp", split_axis=0, concat_axis=0, tiled=True)
    back, pieces = lax.optimization_barrier((back, pieces))
    new = factors(
        owners, me, squares, pieces, left_factor[0], right_factor[0], first_moment[0], bands, entries
    )
    left_new, right_new, first_new = new
    out = [jax.ShapeDtypeStruct((rows, width), bf16)] * bands
    mine = local(collect_body, [table, back.reshape(shards * slots, rows, n)], out, "collect")
    out = jax.ShapeDtypeStruct((bands, rows, width), bf16)
    result = local(put_body, [table, *exchange(mine, along_z)], out, "put").reshape(rows_dev, width)
    return (result, left_new[None], right_new[None], first_new[None], second_new[None])


def solution(mesh):
    state = P("dp", "fsdp", None, None)
    return jax.shard_map(
        per_device,
        mesh=mesh,
        in_specs=(P("dp", "fsdp", None), P("dp", None)) + (state,) * 6,
        out_specs=(P("fsdp", "dp"),) + (state,) * 4,
        check_vma=False,
    )
```

```python
import jax
import jax.numpy as jnp
from jax import lax
from jax.experimental import pallas as pl
from jax.experimental.pallas import tpu as pltpu
from jax.sharding import PartitionSpec as P

f32 = jnp.float32
bf16 = jnp.bfloat16
SMEM = pltpu.MemorySpace.SMEM
VMEM = pltpu.MemorySpace.VMEM
HBM = pltpu.MemorySpace.HBM
LANES = 128


def in_hbm(*arrays):
    return [pltpu.with_memory_space_constraint(a, HBM) for a in arrays]


def split3(value):
    head, rest = split(value)
    mid, tail = split(value - head.astype(f32))
    return head, mid, tail


def split(value):
    head = value.astype(bf16)
    return head, (value - head.astype(f32)).astype(bf16)


def mm(a, b, dims=((1,), (0,))):
    return lax.dot_general(a, b, (dims, ((), ())), preferred_element_type=f32)


def tiles(count, size=32):
    return [slice(r, r + size) for r in range(0, count, size)]


def prepare_body(
    left_src, right_src, first_src, lt_dst, l_dst, r_dst, rot_dst, *scratch
):
    left, right, first, lt, low, head, rot, lt_both, half, tail, product, sems, out_sems = scratch
    slots, n, _ = left.shape
    pairs = ((left_src, left), (first_src, first), (right_src, right))
    copies = [
        [
            pltpu.make_async_copy(src.at[s], dst.at[s], sems.at[s, i])
            for i, (src, dst) in enumerate(pairs)
        ]
        for s in range(slots)
    ]
    for group in copies:
        for c in group:
            c.start()
    pairs = ((lt, lt_dst), (low, l_dst), (head, r_dst), (rot, rot_dst))
    outs = [
        [
            pltpu.make_async_copy(src.at[s], dst.at[s], out_sems.at[s, i])
            for i, (src, dst) in enumerate(pairs)
        ]
        for s in range(slots)
    ]
    for s in range(slots):
        copies[s][0].wait()
        for rows in tiles(n, LANES):
            above, below = split(left[s, rows].T)
            lt[s, :, rows] = above
            lt_both[:n, rows] = above
            lt_both[n:, rows] = below
        outs[s][0].start()
        for rows in tiles(n):
            low[s, rows] = left[s, rows].astype(bf16)
        outs[s][1].start()
        copies[s][1].wait()
        for rows in tiles(n):
            half[rows] = first[s, rows].astype(bf16)
        product[...] = mm(lt_both[...], half[...])
        copies[s][2].wait()
        for rows, more in zip(tiles(n), tiles(2 * n)[n // 32 :]):
            half[rows] = (product[rows] + product[more]).astype(bf16)
            head[s, rows], tail[rows] = split(right[s, rows])
        outs[s][2].start()
        rot[s] = 0.9 * (mm(half[...], head[s]) + mm(half[...], tail[...]))
        outs[s][3].start()
    for group in outs:
        for c in group:
            c.wait()


def prepare(left_basis, right_basis, first_moment):
    slots, n, _ = left_basis.shape
    far = pl.BlockSpec(memory_space=HBM)
    return pl.pallas_call(
        prepare_body,
        in_specs=[far] * 3,
        out_specs=[far] * 4,
        out_shape=[HBM((slots, n, n), bf16)] * 3 + [HBM((slots, n, n), f32)],
        scratch_shapes=[pltpu.VMEM((slots, n, n), f32)] * 3
        + [pltpu.VMEM((slots, n, n), bf16)] * 3
        + [
            pltpu.VMEM((slots, n, n), f32),
            pltpu.VMEM((2 * n, n), bf16),
            pltpu.VMEM((n, n), bf16),
            pltpu.VMEM((n, n), bf16),
            pltpu.VMEM((2 * n, n), f32),
            pltpu.SemaphoreType.DMA((slots, 3)),
            pltpu.SemaphoreType.DMA((slots, 4)),
        ],
        compiler_params=pltpu.CompilerParams(vmem_limit_bytes=24 << 20),
        cost_estimate=pl.CostEstimate(
            flops=slots * 8 * n**3, bytes_accessed=slots * 22 * n * n, transcendentals=0
        ),
        name="prepare",
    )(*in_hbm(left_basis, right_basis, first_moment))


def local(body, arrays, out_shape, name, limit=8 << 20, cost=None):
    return pl.pallas_call(
        body,
        in_specs=[pl.BlockSpec(memory_space=SMEM)]
        + [pl.BlockSpec(memory_space=VMEM)] * (len(arrays) - 1),
        out_specs=jax.tree.map(
            lambda _: pl.BlockSpec(memory_space=VMEM), out_shape, is_leaf=lambda o: hasattr(o, "shape")
        ),
        out_shape=out_shape,
        compiler_params=pltpu.CompilerParams(vmem_limit_bytes=limit),
        cost_estimate=cost,
        name=name,
    )(*arrays)


def dispatch_body(table, *refs):
    *srcs, dst, square = refs
    n = dst.shape[2]
    bands = len(srcs)
    width = srcs[0].shape[1] - LANES
    cols = width // n
    z = table[0, bands * cols]
    total = jnp.zeros(square.shape, f32)
    for j, src in enumerate(srcs):
        band = lax.rem(z + bands - j, bands)
        for c in range(cols):
            dst[table[0, band * cols + c]] = src[:, c * n : (c + 1) * n]
        terms = src[:, width:].astype(f32)
        for t in range(3):
            total = total + terms[8 * t : 8 * t + 8]
    square[...] = total


def collect_body(table, src, *dsts):
    n = src.shape[2]
    bands = len(dsts)
    cols = dsts[0].shape[1] // n
    z = table[0, bands * cols]
    for j, dst in enumerate(dsts):
        band = lax.rem(z + j, bands)
        for c in range(cols):
            dst[:, c * n : (c + 1) * n] = src[table[0, band * cols + c]]


def put_body(table, *refs):
    *srcs, dst = refs
    bands = len(srcs)
    z = table[0, table.shape[1] - 1]
    for j, src in enumerate(srcs):
        dst[lax.rem(z + bands - j, bands)] = src[...]


def load(place, grads, width):
    rows, columns = grads.shape
    chips = columns // width // 2
    groups = ((2,), (1, 3, 0))

    def body(place, src, *refs):
        *dsts, sems = refs
        copies = []
        for i, dst in enumerate(dsts):
            core = 1 - place[1] if i < 2 else place[1]
            for k, j in enumerate(groups[i % 2]):
                slab = 2 * lax.rem(place[0] + j, chips) + core
                columns = pl.ds(pl.multiple_of(slab * width, width), width)
                copies.append(
                    pltpu.make_async_copy(src.at[:, columns], dst.at[k], sems.at[len(copies)])
                )
        for c in copies:
            c.start()
        for c in copies:
            c.wait()

    return pl.pallas_call(
        body,
        in_specs=[pl.BlockSpec(memory_space=SMEM), pl.BlockSpec(memory_space=HBM)],
        out_specs=[pl.BlockSpec(memory_space=VMEM)] * 4,
        out_shape=[VMEM((len(g), rows, width), bf16) for g in groups * 2],
        scratch_shapes=[pltpu.SemaphoreType.DMA((2 * chips,))],
        compiler_params=pltpu.CompilerParams(vmem_limit_bytes=2 << 20),
        name="load",
    )(place, *in_hbm(grads))


def pair(body, place, near, far, outs, name):
    low = near.shape[1] // 2

    def run(place, near, far, *outs):
        def total(i, a):
            part = slice(a * low, (a + 1) * low)
            return near[i, part].astype(f32) + far[i, part].astype(f32)

        body(total, low, *outs)

    out = [jax.ShapeDtypeStruct(shape, kind) for shape, kind in outs]
    return local(run, [place, near, far], out, name)


def far_body(total, low, to_right, to_left):
    to_right[...] = total(0, 0).astype(bf16)
    to_left[...] = total(0, 1).astype(bf16)


def near_body(total, low, to_right, to_left, keep_right, keep_left, own):
    keep_right[...] = total(0, 0)
    to_right[...] = total(0, 1).astype(bf16)
    to_left[...] = total(1, 0).astype(bf16)
    keep_left[...] = total(1, 1)
    for a in range(2):
        own[a * low : (a + 1) * low] = total(2, a)


def relay(place, kept, arrived):
    def body(place, kept, arrived, out):
        out[...] = (kept[...] + arrived[...].astype(f32)).astype(bf16)

    out = jax.ShapeDtypeStruct(kept.shape, bf16)
    return local(body, (place, kept, arrived), out, "relay")


def direct_body(place, own, left_direct, right_direct, out):
    low = left_direct.shape[0]
    out[:low] = own[:low] + right_direct[...].astype(f32)
    out[low:] = own[low:] + left_direct[...].astype(f32)


def finish(place, own, left_sum, right_sum, bands):
    rows, width = own.shape
    low = rows // 2
    piece = rows // bands

    def body(place, own, left_sum, right_sum, *outs):
        total = jnp.zeros((8, LANES), f32)
        for q in range(bands):
            relayed = left_sum if q * piece < low else right_sum
            part = slice(q * piece % low, q * piece % low + piece)
            value = own[q * piece : (q + 1) * piece] + relayed[part].astype(f32)
            step = lax.rem(q - place[2] + bands, bands)
            rounded = value.astype(bf16)
            for j in range(bands):

                @pl.when(step == j)
                def _():
                    outs[j][:, :width] = rounded

            by_row = jnp.sum((value * value).reshape(piece // 8, 8, width), axis=0)
            for c in range(width // LANES):
                total = total + by_row[:, c * LANES : (c + 1) * LANES]
        terms = [t.astype(f32) for t in split3(total)]
        terms.append(jnp.zeros((piece - 24, LANES), f32))
        terms = jnp.concatenate(terms, axis=0).astype(bf16)
        for out in outs:
            out[:, width:] = terms

    arrays = [place, own, left_sum, right_sum]
    out = [jax.ShapeDtypeStruct((piece, width + LANES), bf16)] * bands
    return local(body, arrays, out, "finish", 12 << 20)


def sum_over_replicas(place, grads, bands):
    size = lax.axis_size("dp")
    rows, columns = grads.shape
    width = columns // size
    half = (rows // 2, width)
    swap = [(d, d ^ 1) for d in range(size)]
    up = [(d, (d + 2) % size) for d in range(size)]
    down = [(d, (d - 2) % size) for d in range(size)]
    far_there, near_there, far_here, near_here = load(place, grads, width)
    other = lax.ppermute(far_there, "dp", swap)
    other, near_there = lax.optimization_barrier((other, near_there))
    others = lax.ppermute(near_there, "dp", swap)
    to_right, to_left = pair(far_body, place, far_here, other, [(half, bf16)] * 2, "pair_far")
    left_far = lax.ppermute(to_right, "dp", up)
    right_far = lax.ppermute(to_left, "dp", down)
    outs = [(half, bf16)] * 2 + [(half, f32)] * 2 + [((rows, width), f32)]
    to_right, to_left, keep_right, keep_left, own = pair(
        near_body, place, near_here, others, outs, "pair_near"
    )
    left_direct = lax.ppermute(to_right, "dp", up)
    right_direct = lax.ppermute(to_left, "dp", down)
    left_sum = lax.ppermute(relay(place, keep_right, left_far), "dp", up)
    right_sum = lax.ppermute(relay(place, keep_left, right_far), "dp", down)
    out = jax.ShapeDtypeStruct((rows, width), f32)
    own = local(direct_body, [place, own, left_direct, right_direct], out, "direct", cost=pl.CostEstimate(flops=2 * rows * width, bytes_accessed=12 * rows * width, transcendentals=0))
    return own, left_sum, right_sum


def exchange(arrays, steps):
    order = sorted(range(1, len(arrays)), key=lambda j: -min(j, len(arrays) - j))
    got = {0: arrays[0]}
    for j in order:
        got[j] = lax.ppermute(arrays[j], *steps[j - 1])
    return [got[j] for j in range(len(arrays))]


def assemble(pieces, slot, bands):
    per = pieces.shape[0] // bands
    return jnp.concatenate(
        [pieces[z * per + y, slot] for y in range(per) for z in range(bands)], axis=0
    )


def is_named(table, slot):
    named = table[0, 0] == slot
    for b in range(1, table.shape[1]):
        named = jnp.logical_or(named, table[0, b] == slot)
    return named


def clip_of(squares, entries):
    total = squares[0][...]
    for square in squares[1:]:
        total = total + square[...]
    total = jnp.sum(jnp.sum(total, axis=0, keepdims=True), axis=1, keepdims=True)
    return jnp.minimum(1.0, 1.0 / jnp.sqrt(total / entries + 1e-06))


def rotate(pieces, prepared, second, bands):
    slots, n, _ = second.shape

    def body(pieces, lt_src, l_src, r_src, rot_src, old_src, *refs):
        out, right, left, rot, old, lt, half, sems = refs
        first = ((lt_src, lt), (r_src, right))
        pairs = [(src.at[s], dst.at[s]) for s in range(slots) for src, dst in first]
        pairs += [(src.at[0], dst.at[0]) for src, dst in ((rot_src, rot), (old_src, old))]
        pairs.append((l_src, left))
        copies = [
            pltpu.make_async_copy(src, dst, sems.at[i]) for i, (src, dst) in enumerate(pairs)
        ]
        for c in copies:
            c.start()
        for s in range(slots):
            block = assemble(pieces, s, bands)
            copies[2 * s].wait()
            half[...] = mm(lt[s], block).astype(bf16)
            copies[2 * s + 1].wait()
            out[s] = mm(half[...], right[s])
        for c in copies[2 * slots :]:
            c.wait()

    whole = pl.BlockSpec(memory_space=VMEM)
    far = pl.BlockSpec(memory_space=HBM)
    return pl.pallas_call(
        body,
        in_specs=[whole] + [far] * 5,
        out_specs=[whole] * 5,
        out_shape=[
            VMEM((slots, n, n), f32),
            VMEM((slots, n, n), bf16),
            VMEM((slots, n, n), bf16),
            VMEM((1, n, n), f32),
            VMEM((1, n, n), f32),
        ],
        scratch_shapes=[
            pltpu.VMEM((slots, n, n), bf16),
            pltpu.VMEM((n, n), bf16),
            pltpu.SemaphoreType.DMA((2 * slots + 3,)),
        ],
        compiler_params=pltpu.CompilerParams(vmem_limit_bytes=12 << 20),
        name="rotate",
    )(pieces, *in_hbm(*prepared, second))


def direction(table, me, squares, rotated, prepared, second, bands, senders, entries):
    slots, n, _ = rotated[0].shape
    rows = n // senders
    per = senders // bands

    def body(table, me, *refs):
        squares, rest = refs[: len(refs) - 16], refs[len(refs) - 16 :]
        product, right, left, rot, old, rot_src, old_src, out, second_out = rest[:9]
        rot_more, old_more, new, step, half, in_sems, sems = rest[9:]
        pairs = ((old_src, old_more), (rot_src, rot_more))
        copies = [
            [
                pltpu.make_async_copy(src.at[s], dst.at[s - 1], in_sems.at[s, i])
                for i, (src, dst) in enumerate(pairs)
            ]
            for s in range(1, slots)
        ]
        for group in copies:
            for c in group:
                c.start()
        scale = clip_of(squares, entries)
        for s in range(slots):
            if s == 0:
                states = rot.at[0], old.at[0]
            else:
                states = rot_more.at[s - 1], old_more.at[s - 1]
                for c in copies[s - 1]:
                    c.wait()
            named = is_named(table, me[0] * slots + s)
            for r in tiles(n):
                turned = product[s, r] * scale
                before = states[1][r]
                value = 0.95 * before + 0.05 * turned * turned
                new[s, r] = jnp.where(named, value, before)
                ahead = states[0][r] + 0.1 * turned
                step[r] = (ahead * pl.reciprocal(jnp.sqrt(value) + 1e-08, approx=True)).astype(bf16)
            pltpu.make_async_copy(new.at[s], second_out.at[s], sems.at[s]).start()
            half[...] = mm(left[s], step[...]).astype(bf16)
            update = mm(half[...], right[s], ((1,), (1,))).astype(bf16)
            for y in range(per):
                for z in range(bands):
                    row = (y * bands + z) * rows
                    out[z * per + y, s] = update[row : row + rows]
        for s in range(slots):
            pltpu.make_async_copy(new.at[s], second_out.at[s], sems.at[s]).wait()

    scalar = pl.BlockSpec(memory_space=SMEM)
    whole = pl.BlockSpec(memory_space=VMEM)
    far = pl.BlockSpec(memory_space=HBM)
    return pl.pallas_call(
        body,
        in_specs=[scalar] * 2 + [whole] * (len(squares) + 5) + [far] * 2,
        out_specs=[whole, far],
        out_shape=[
            jax.ShapeDtypeStruct((senders, slots, rows, n), bf16),
            HBM((slots, n, n), f32),
        ],
        scratch_shapes=[
            pltpu.VMEM((slots - 1, n, n), f32),
            pltpu.VMEM((slots - 1, n, n), f32),
            pltpu.VMEM((slots, n, n), f32),
            pltpu.VMEM((n, n), bf16),
            pltpu.VMEM((n, n), bf16),
            pltpu.SemaphoreType.DMA((slots, 2)),
            pltpu.SemaphoreType.DMA((slots,)),
        ],
        compiler_params=pltpu.CompilerParams(vmem_limit_bytes=16 << 20),
        name="direction",
    )(table, me, *squares, *rotated, *in_hbm(prepared[3], second))


def factors_body(bands, entries, table, me, *refs):
    *squares, pieces = refs[:-16]
    sources, outs, news, olds = (refs[i : i + 3] for i in range(-16, -4, 3))
    block, product, *sems = refs[-4:]
    slots, n, _ = news[0].shape
    copies = [
        [
            pltpu.make_async_copy(src.at[s], dst.at[s], sems[0].at[s, i])
            for i, (src, dst) in enumerate(zip(sources, olds))
        ]
        for s in range(slots)
    ]
    for group in copies:
        for c in group:
            c.start()
    scale = clip_of(squares, entries)
    square = 0.1 * scale * scale
    done = []
    for s in range(slots):
        named = is_named(table, me[0] * slots + s)
        block[...] = assemble(pieces, s, bands)
        for i in range(3):
            if i == 0:
                product[...] = mm(block[...], block[...], ((1,), (1,)))
            elif i == 1:
                product[...] = mm(block[...].T, block[...])
            copies[s][i].wait()
            for r in tiles(n):
                old = olds[i][s, r]
                more = square * product[r] if i < 2 else (0.1 * scale) * block[r].astype(f32)
                news[i][s, r] = jnp.where(named, 0.9 * old + more, old)
            done.append(pltpu.make_async_copy(news[i].at[s], outs[i].at[s], sems[1].at[s, i]))
            done[-1].start()
    for c in done:
        c.wait()


def factors(table, me, squares, pieces, left, right, first, bands, entries):
    slots, n, _ = left.shape
    scalar = pl.BlockSpec(memory_space=SMEM)
    whole = pl.BlockSpec(memory_space=VMEM)
    far = pl.BlockSpec(memory_space=HBM)

    def body(*refs):
        factors_body(bands, entries, *refs)

    return pl.pallas_call(
        body,
        in_specs=[scalar] * 2 + [whole] * (len(squares) + 1) + [far] * 3,
        out_specs=[far] * 3,
        out_shape=[HBM(left.shape, f32)] * 3,
        scratch_shapes=[pltpu.VMEM((slots, n, n), f32)] * 6
        + [pltpu.VMEM((n, n), bf16), pltpu.VMEM((n, n), f32)]
        + [pltpu.SemaphoreType.DMA((slots, 3))] * 2,
        compiler_params=pltpu.CompilerParams(vmem_limit_bytes=24 << 20),
        cost_estimate=pl.CostEstimate(
            flops=slots * 4 * n**3, bytes_accessed=slots * 26 * n * n, transcendentals=0
        ),
        name="factors",
    )(table, me, *squares, pieces, *in_hbm(left, right, first))


def per_device(
    replica_grads,
    owners,
    left_factor,
    right_factor,
    left_basis,
    right_basis,
    first_moment,
    second_moment,
):
    rows_dev = replica_grads.shape[1]
    shards = lax.axis_size("fsdp")
    slots, n = left_factor.shape[1:3]
    per_band = n // rows_dev
    bands = shards // per_band
    dp = lax.axis_size("dp")
    dp_me = lax.axis_index("dp").astype(jnp.int32)
    me = lax.axis_index("fsdp").astype(jnp.int32)
    place = jnp.stack([dp_me // 2, dp_me % 2, me // per_band])
    table = jnp.concatenate([owners, (me // per_band).reshape(1, 1)], axis=1)
    me = me.reshape(1)
    core = [("dp", [(d, d ^ 1) for d in range(dp)])]
    along_x = [("dp", [(d, (d + 2 * h) % dp) for d in range(dp)]) for h in range(1, dp // 2)]
    along_y = [
        ("fsdp", [(i, i // per_band * per_band + (i + h) % per_band) for i in range(shards)])
        for h in range(1, per_band)
    ]
    along_z = [
        ("fsdp", [(i, (i + h * per_band) % shards) for i in range(shards)])
        for h in range(1, bands)
    ]
    parts = sum_over_replicas(place, replica_grads[0], bands)
    prepared = prepare(left_basis[0], right_basis[0], first_moment[0])
    parts, prepared = lax.optimization_barrier((parts, prepared))
    sums = finish(place, *parts, bands)
    rows, width = sums[0].shape[0], sums[0].shape[1] - LANES
    cols = width // n
    entries = rows_dev * shards * replica_grads.shape[2]
    spread = exchange(sums, along_z)
    out = [
        jax.ShapeDtypeStruct((shards * slots, rows, n), bf16),
        jax.ShapeDtypeStruct((8, LANES), f32),
    ]
    sent, square = local(dispatch_body, [table, *spread], out, "dispatch")
    sent = sent.reshape(shards, slots, rows, n)
    pieces = lax.all_to_all(sent, "fsdp", split_axis=0, concat_axis=0, tiled=True)
    for steps in (core, along_x):
        square = sum([lax.ppermute(square, *step) for step in steps], square)
    squares = [square] + [lax.ppermute(square, *step) for step in along_y]
    rotated = rotate(pieces, prepared, second_moment[0], bands)
    update, second_new = direction(
        owners, me, squares, rotated, prepared, second_moment[0], bands, shards, entries
    )
    back = lax.all_to_all(update, "fsdp", split_axis=0, concat_axis=0, tiled=True)
    back, pieces = lax.optimization_barrier((back, pieces))
    new = factors(
        owners, me, squares, pieces, left_factor[0], right_factor[0], first_moment[0], bands, entries
    )
    left_new, right_new, first_new = new
    out = [jax.ShapeDtypeStruct((rows, width), bf16)] * bands
    mine = local(collect_body, [table, back.reshape(shards * slots, rows, n)], out, "collect")
    out = jax.ShapeDtypeStruct((bands, rows, width), bf16)
    result = local(put_body, [table, *exchange(mine, along_z)], out, "put").reshape(rows_dev, width)
    return (result, left_new[None], right_new[None], first_new[None], second_new[None])


def solution(mesh):
    state = P("dp", "fsdp", None, None)
    return jax.shard_map(
        per_device,
        mesh=mesh,
        in_specs=(P("dp", "fsdp", None), P("dp", None)) + (state,) * 6,
        out_specs=(P("fsdp", "dp"),) + (state,) * 4,
        check_vma=False,
    )
```

```python
import jax
import jax.numpy as jnp
from jax import lax
from jax.experimental import pallas as pl
from jax.experimental.pallas import tpu as pltpu
from jax.sharding import PartitionSpec as P

f32 = jnp.float32
bf16 = jnp.bfloat16
SMEM = pltpu.MemorySpace.SMEM
VMEM = pltpu.MemorySpace.VMEM
HBM = pltpu.MemorySpace.HBM
LANES = 128


def in_hbm(*arrays):
    return [pltpu.with_memory_space_constraint(a, HBM) for a in arrays]


def split3(value):
    head, rest = split(value)
    mid, tail = split(value - head.astype(f32))
    return head, mid, tail


def split(value):
    head = value.astype(bf16)
    return head, (value - head.astype(f32)).astype(bf16)


def mm(a, b, dims=((1,), (0,))):
    return lax.dot_general(a, b, (dims, ((), ())), preferred_element_type=f32)


def tiles(count, size=32):
    return [slice(r, r + size) for r in range(0, count, size)]


def prepare_body(
    left_src, right_src, first_src, lt_dst, l_dst, r_dst, rot_dst, *scratch
):
    left, right, first, lt, low, head, rot, lt_both, half, tail, product, sems, out_sems = scratch
    slots, n, _ = left.shape
    pairs = ((left_src, left), (first_src, first), (right_src, right))
    copies = [
        [
            pltpu.make_async_copy(src.at[s], dst.at[s], sems.at[s, i])
            for i, (src, dst) in enumerate(pairs)
        ]
        for s in range(slots)
    ]
    for group in copies:
        for c in group:
            c.start()
    pairs = ((lt, lt_dst), (low, l_dst), (head, r_dst), (rot, rot_dst))
    outs = [
        [
            pltpu.make_async_copy(src.at[s], dst.at[s], out_sems.at[s, i])
            for i, (src, dst) in enumerate(pairs)
        ]
        for s in range(slots)
    ]
    for s in range(slots):
        copies[s][0].wait()
        for rows in tiles(n, LANES):
            above, below = split(left[s, rows].T)
            lt[s, :, rows] = above
            lt_both[:n, rows] = above
            lt_both[n:, rows] = below
        outs[s][0].start()
        for rows in tiles(n):
            low[s, rows] = left[s, rows].astype(bf16)
        outs[s][1].start()
        copies[s][1].wait()
        for rows in tiles(n):
            half[rows] = first[s, rows].astype(bf16)
        product[...] = mm(lt_both[...], half[...])
        copies[s][2].wait()
        for rows, more in zip(tiles(n), tiles(2 * n)[n // 32 :]):
            half[rows] = (product[rows] + product[more]).astype(bf16)
            head[s, rows], tail[rows] = split(right[s, rows])
        outs[s][2].start()
        turned = mm(half[...], head[s]) + mm(half[...], tail[...])
        rot[s] = (0.9 * turned).astype(bf16)
        outs[s][3].start()
    for group in outs:
        for c in group:
            c.wait()


def prepare(left_basis, right_basis, first_moment):
    slots, n, _ = left_basis.shape
    far = pl.BlockSpec(memory_space=HBM)
    return pl.pallas_call(
        prepare_body,
        in_specs=[far] * 3,
        out_specs=[far] * 4,
        out_shape=[HBM((slots, n, n), bf16)] * 4,
        scratch_shapes=[pltpu.VMEM((slots, n, n), f32)] * 3
        + [pltpu.VMEM((slots, n, n), bf16)] * 4
        + [
            pltpu.VMEM((2 * n, n), bf16),
            pltpu.VMEM((n, n), bf16),
            pltpu.VMEM((n, n), bf16),
            pltpu.VMEM((2 * n, n), f32),
            pltpu.SemaphoreType.DMA((slots, 3)),
            pltpu.SemaphoreType.DMA((slots, 4)),
        ],
        compiler_params=pltpu.CompilerParams(vmem_limit_bytes=24 << 20),
        cost_estimate=pl.CostEstimate(
            flops=slots * 8 * n**3, bytes_accessed=slots * 22 * n * n, transcendentals=0
        ),
        name="prepare",
    )(*in_hbm(left_basis, right_basis, first_moment))


def local(body, arrays, out_shape, name, limit=8 << 20, cost=None):
    return pl.pallas_call(
        body,
        in_specs=[pl.BlockSpec(memory_space=SMEM)]
        + [pl.BlockSpec(memory_space=VMEM)] * (len(arrays) - 1),
        out_specs=jax.tree.map(
            lambda _: pl.BlockSpec(memory_space=VMEM), out_shape, is_leaf=lambda o: hasattr(o, "shape")
        ),
        out_shape=out_shape,
        compiler_params=pltpu.CompilerParams(vmem_limit_bytes=limit),
        cost_estimate=cost,
        name=name,
    )(*arrays)


def dispatch_body(table, *refs):
    *srcs, dst, square = refs
    n = dst.shape[2]
    bands = len(srcs)
    width = srcs[0].shape[1] - LANES
    cols = width // n
    z = table[0, bands * cols]
    total = jnp.zeros(square.shape, f32)
    for j, src in enumerate(srcs):
        band = lax.rem(z + bands - j, bands)
        for c in range(cols):
            dst[table[0, band * cols + c]] = src[:, c * n : (c + 1) * n]
        terms = src[:, width:].astype(f32)
        for t in range(3):
            total = total + terms[8 * t : 8 * t + 8]
    square[...] = total


def collect_body(table, src, *dsts):
    n = src.shape[2]
    bands = len(dsts)
    cols = dsts[0].shape[1] // n
    z = table[0, bands * cols]
    for j, dst in enumerate(dsts):
        band = lax.rem(z + j, bands)
        for c in range(cols):
            dst[:, c * n : (c + 1) * n] = src[table[0, band * cols + c]]


def put_body(table, *refs):
    *srcs, dst = refs
    bands = len(srcs)
    z = table[0, table.shape[1] - 1]
    for j, src in enumerate(srcs):
        dst[lax.rem(z + bands - j, bands)] = src[...]


def load(place, grads, width):
    rows, columns = grads.shape
    chips = columns // width // 2
    groups = ((2,), (1, 3, 0))

    def body(place, src, *refs):
        *dsts, sems = refs
        copies = []
        for i, dst in enumerate(dsts):
            core = 1 - place[1] if i < 2 else place[1]
            for k, j in enumerate(groups[i % 2]):
                slab = 2 * lax.rem(place[0] + j, chips) + core
                columns = pl.ds(pl.multiple_of(slab * width, width), width)
                copies.append(
                    pltpu.make_async_copy(src.at[:, columns], dst.at[k], sems.at[len(copies)])
                )
        for c in copies:
            c.start()
        for c in copies:
            c.wait()

    return pl.pallas_call(
        body,
        in_specs=[pl.BlockSpec(memory_space=SMEM), pl.BlockSpec(memory_space=HBM)],
        out_specs=[pl.BlockSpec(memory_space=VMEM)] * 4,
        out_shape=[VMEM((len(g), rows, width), bf16) for g in groups * 2],
        scratch_shapes=[pltpu.SemaphoreType.DMA((2 * chips,))],
        compiler_params=pltpu.CompilerParams(vmem_limit_bytes=2 << 20),
        name="load",
    )(place, *in_hbm(grads))


def pair(body, place, near, far, outs, name):
    low = near.shape[1] // 2

    def run(place, near, far, *outs):
        def total(i, a):
            part = slice(a * low, (a + 1) * low)
            return near[i, part].astype(f32) + far[i, part].astype(f32)

        body(total, low, *outs)

    out = [jax.ShapeDtypeStruct(shape, kind) for shape, kind in outs]
    return local(run, [place, near, far], out, name)


def far_body(total, low, to_right, to_left):
    to_right[...] = total(0, 0).astype(bf16)
    to_left[...] = total(0, 1).astype(bf16)


def near_body(total, low, to_right, to_left, keep_right, keep_left, own):
    keep_right[...] = total(0, 0)
    to_right[...] = total(0, 1).astype(bf16)
    to_left[...] = total(1, 0).astype(bf16)
    keep_left[...] = total(1, 1)
    for a in range(2):
        own[a * low : (a + 1) * low] = total(2, a)


def relay(place, kept, arrived):
    def body(place, kept, arrived, out):
        out[...] = (kept[...] + arrived[...].astype(f32)).astype(bf16)

    out = jax.ShapeDtypeStruct(kept.shape, bf16)
    return local(body, (place, kept, arrived), out, "relay")


def direct_body(place, own, left_direct, right_direct, out):
    low = left_direct.shape[0]
    out[:low] = own[:low] + right_direct[...].astype(f32)
    out[low:] = own[low:] + left_direct[...].astype(f32)


def finish(place, own, left_sum, right_sum, bands):
    rows, width = own.shape
    low = rows // 2
    piece = rows // bands

    def body(place, own, left_sum, right_sum, *outs):
        total = jnp.zeros((8, LANES), f32)
        for q in range(bands):
            relayed = left_sum if q * piece < low else right_sum
            part = slice(q * piece % low, q * piece % low + piece)
            value = own[q * piece : (q + 1) * piece] + relayed[part].astype(f32)
            step = lax.rem(q - place[2] + bands, bands)
            rounded = value.astype(bf16)
            for j in range(bands):

                @pl.when(step == j)
                def _():
                    outs[j][:, :width] = rounded

            by_row = jnp.sum((value * value).reshape(piece // 8, 8, width), axis=0)
            for c in range(width // LANES):
                total = total + by_row[:, c * LANES : (c + 1) * LANES]
        terms = [t.astype(f32) for t in split3(total)]
        terms.append(jnp.zeros((piece - 24, LANES), f32))
        terms = jnp.concatenate(terms, axis=0).astype(bf16)
        for out in outs:
            out[:, width:] = terms

    arrays = [place, own, left_sum, right_sum]
    out = [jax.ShapeDtypeStruct((piece, width + LANES), bf16)] * bands
    return local(body, arrays, out, "finish", 12 << 20)


def sum_over_replicas(place, grads, bands):
    size = lax.axis_size("dp")
    rows, columns = grads.shape
    width = columns // size
    half = (rows // 2, width)
    swap = [(d, d ^ 1) for d in range(size)]
    up = [(d, (d + 2) % size) for d in range(size)]
    down = [(d, (d - 2) % size) for d in range(size)]
    far_there, near_there, far_here, near_here = load(place, grads, width)
    other = lax.ppermute(far_there, "dp", swap)
    other, near_there = lax.optimization_barrier((other, near_there))
    others = lax.ppermute(near_there, "dp", swap)
    to_right, to_left = pair(far_body, place, far_here, other, [(half, bf16)] * 2, "pair_far")
    left_far = lax.ppermute(to_right, "dp", up)
    right_far = lax.ppermute(to_left, "dp", down)
    outs = [(half, bf16)] * 2 + [(half, f32)] * 2 + [((rows, width), f32)]
    to_right, to_left, keep_right, keep_left, own = pair(
        near_body, place, near_here, others, outs, "pair_near"
    )
    left_direct = lax.ppermute(to_right, "dp", up)
    right_direct = lax.ppermute(to_left, "dp", down)
    left_sum = lax.ppermute(relay(place, keep_right, left_far), "dp", up)
    right_sum = lax.ppermute(relay(place, keep_left, right_far), "dp", down)
    out = jax.ShapeDtypeStruct((rows, width), f32)
    own = local(direct_body, [place, own, left_direct, right_direct], out, "direct", cost=pl.CostEstimate(flops=2 * rows * width, bytes_accessed=12 * rows * width, transcendentals=0))
    return own, left_sum, right_sum


def exchange(arrays, steps):
    order = sorted(range(1, len(arrays)), key=lambda j: -min(j, len(arrays) - j))
    got = {0: arrays[0]}
    for j in order:
        got[j] = lax.ppermute(arrays[j], *steps[j - 1])
    return [got[j] for j in range(len(arrays))]


def assemble(pieces, slot, bands):
    per = pieces.shape[0] // bands
    return jnp.concatenate(
        [pieces[z * per + y, slot] for y in range(per) for z in range(bands)], axis=0
    )


def is_named(table, slot):
    named = table[0, 0] == slot
    for b in range(1, table.shape[1]):
        named = jnp.logical_or(named, table[0, b] == slot)
    return named


def clip_of(squares, entries):
    total = squares[0][...]
    for square in squares[1:]:
        total = total + square[...]
    total = jnp.sum(jnp.sum(total, axis=0, keepdims=True), axis=1, keepdims=True)
    return jnp.minimum(1.0, 1.0 / jnp.sqrt(total / entries + 1e-06))


def rotate(pieces, prepared, second, bands):
    slots, n, _ = second.shape

    def body(pieces, lt_src, l_src, r_src, rot_src, old_src, *refs):
        out, right, left, rot, old, lt, half, sems = refs
        pairs = [(src.at[s], dst.at[s]) for s in range(slots) for src, dst in ((lt_src, lt), (r_src, right))]
        pairs += [(src.at[0], dst.at[0]) for src, dst in ((rot_src, rot), (old_src, old), (l_src, left))]
        copies = [
            pltpu.make_async_copy(src, dst, sems.at[i]) for i, (src, dst) in enumerate(pairs)
        ]
        for c in copies:
            c.start()
        for s in range(slots):
            block = assemble(pieces, s, bands)
            copies[2 * s].wait()
            half[...] = mm(lt[s], block).astype(bf16)
            copies[2 * s + 1].wait()
            out[s] = mm(half[...], right[s])
        for c in copies[2 * slots :]:
            c.wait()

    whole = pl.BlockSpec(memory_space=VMEM)
    far = pl.BlockSpec(memory_space=HBM)
    return pl.pallas_call(
        body,
        in_specs=[whole] + [far] * 5,
        out_specs=[whole] * 5,
        out_shape=[
            VMEM((slots, n, n), f32),
            VMEM((slots, n, n), bf16),
            VMEM((1, n, n), bf16),
            VMEM((1, n, n), bf16),
            VMEM((1, n, n), f32),
        ],
        scratch_shapes=[
            pltpu.VMEM((slots, n, n), bf16),
            pltpu.VMEM((n, n), bf16),
            pltpu.SemaphoreType.DMA((2 * slots + 3,)),
        ],
        compiler_params=pltpu.CompilerParams(vmem_limit_bytes=12 << 20),
        name="rotate",
    )(pieces, *in_hbm(*prepared, second))


def direction(table, me, squares, rotated, prepared, second, bands, senders, entries):
    slots, n, _ = rotated[0].shape
    rows = n // senders
    per = senders // bands

    def body(table, me, *refs):
        squares, rest = refs[: len(refs) - 18], refs[len(refs) - 18 :]
        product, right, left, rot, old, l_src, rot_src, old_src, out, second_out = rest[:10]
        left_more, rot_more, old_more, new, step, half, in_sems, sems = rest[10:]
        pairs = ((rot_src, rot_more), (old_src, old_more), (l_src, left_more))
        copies = [
            [
                pltpu.make_async_copy(src.at[s], dst.at[s - 1], in_sems.at[s, i])
                for i, (src, dst) in enumerate(pairs)
            ]
            for s in range(1, slots)
        ]
        for group in copies:
            for c in group:
                c.start()
        scale = clip_of(squares, entries)
        for s in range(slots):
            if s == 0:
                states = rot.at[0], old.at[0], left.at[0]
            else:
                states = rot_more.at[s - 1], old_more.at[s - 1], left_more.at[s - 1]
                for c in copies[s - 1][:2]:
                    c.wait()
            named = is_named(table, me[0] * slots + s)
            for r in tiles(n):
                turned = product[s, r] * scale
                before = states[1][r]
                value = 0.95 * before + 0.05 * turned * turned
                new[s, r] = jnp.where(named, value, before)
                ahead = states[0][r].astype(f32) + 0.1 * turned
                step[r] = (ahead * pl.reciprocal(jnp.sqrt(value) + 1e-08, approx=True)).astype(bf16)
            pltpu.make_async_copy(new.at[s], second_out.at[s], sems.at[s]).start()
            if s > 0:
                copies[s - 1][2].wait()
            half[...] = mm(states[2][...], step[...]).astype(bf16)
            update = mm(half[...], right[s], ((1,), (1,))).astype(bf16)
            for y in range(per):
                for z in range(bands):
                    row = (y * bands + z) * rows
                    out[z * per + y, s] = update[row : row + rows]
        for s in range(slots):
            pltpu.make_async_copy(new.at[s], second_out.at[s], sems.at[s]).wait()

    scalar = pl.BlockSpec(memory_space=SMEM)
    whole = pl.BlockSpec(memory_space=VMEM)
    far = pl.BlockSpec(memory_space=HBM)
    return pl.pallas_call(
        body,
        in_specs=[scalar] * 2 + [whole] * (len(squares) + 5) + [far] * 3,
        out_specs=[whole, far],
        out_shape=[
            jax.ShapeDtypeStruct((senders, slots, rows, n), bf16),
            HBM((slots, n, n), f32),
        ],
        scratch_shapes=[
            pltpu.VMEM((slots - 1, n, n), bf16),
            pltpu.VMEM((slots - 1, n, n), bf16),
            pltpu.VMEM((slots - 1, n, n), f32),
            pltpu.VMEM((slots, n, n), f32),
            pltpu.VMEM((n, n), bf16),
            pltpu.VMEM((n, n), bf16),
            pltpu.SemaphoreType.DMA((slots, 3)),
            pltpu.SemaphoreType.DMA((slots,)),
        ],
        compiler_params=pltpu.CompilerParams(vmem_limit_bytes=16 << 20),
        name="direction",
    )(table, me, *squares, *rotated, *in_hbm(prepared[1], prepared[3], second))


def factors_body(bands, entries, table, me, *refs):
    *squares, pieces = refs[:-16]
    sources, outs, news, olds = (refs[i : i + 3] for i in range(-16, -4, 3))
    block, product, *sems = refs[-4:]
    slots, n, _ = news[0].shape
    copies = [
        [
            pltpu.make_async_copy(src.at[s], dst.at[s], sems[0].at[s, i])
            for i, (src, dst) in enumerate(zip(sources, olds))
        ]
        for s in range(slots)
    ]
    for group in copies:
        for i in (2, 0, 1):
            group[i].start()
    scale = clip_of(squares, entries)
    square = 0.1 * scale * scale
    done = []
    for s in range(slots):
        named = is_named(table, me[0] * slots + s)
        block[...] = assemble(pieces, s, bands)
        for i in (2, 0, 1):
            if i == 0:
                product[...] = mm(block[...], block[...], ((1,), (1,)))
            elif i == 1:
                product[...] = mm(block[...].T, block[...])
            copies[s][i].wait()
            for r in tiles(n):
                old = olds[i][s, r]
                more = square * product[r] if i < 2 else (0.1 * scale) * block[r].astype(f32)
                news[i][s, r] = jnp.where(named, 0.9 * old + more, old)
            done.append(pltpu.make_async_copy(news[i].at[s], outs[i].at[s], sems[1].at[s, i]))
            done[-1].start()
    for c in done:
        c.wait()


def factors(table, me, squares, pieces, left, right, first, bands, entries):
    slots, n, _ = left.shape
    scalar = pl.BlockSpec(memory_space=SMEM)
    whole = pl.BlockSpec(memory_space=VMEM)
    far = pl.BlockSpec(memory_space=HBM)

    def body(*refs):
        factors_body(bands, entries, *refs)

    return pl.pallas_call(
        body,
        in_specs=[scalar] * 2 + [whole] * (len(squares) + 1) + [far] * 3,
        out_specs=[far] * 3,
        out_shape=[HBM(left.shape, f32)] * 3,
        scratch_shapes=[pltpu.VMEM((slots, n, n), f32)] * 6
        + [pltpu.VMEM((n, n), bf16), pltpu.VMEM((n, n), f32)]
        + [pltpu.SemaphoreType.DMA((slots, 3))] * 2,
        compiler_params=pltpu.CompilerParams(vmem_limit_bytes=24 << 20),
        cost_estimate=pl.CostEstimate(
            flops=slots * 4 * n**3, bytes_accessed=slots * 26 * n * n, transcendentals=0
        ),
        name="factors",
    )(table, me, *squares, pieces, *in_hbm(left, right, first))


def per_device(
    replica_grads,
    owners,
    left_factor,
    right_factor,
    left_basis,
    right_basis,
    first_moment,
    second_moment,
):
    rows_dev = replica_grads.shape[1]
    shards = lax.axis_size("fsdp")
    slots, n = left_factor.shape[1:3]
    per_band = n // rows_dev
    bands = shards // per_band
    dp = lax.axis_size("dp")
    dp_me = lax.axis_index("dp").astype(jnp.int32)
    me = lax.axis_index("fsdp").astype(jnp.int32)
    place = jnp.stack([dp_me // 2, dp_me % 2, me // per_band])
    table = jnp.concatenate([owners, (me // per_band).reshape(1, 1)], axis=1)
    me = me.reshape(1)
    core = [("dp", [(d, d ^ 1) for d in range(dp)])]
    along_x = [("dp", [(d, (d + 2 * h) % dp) for d in range(dp)]) for h in range(1, dp // 2)]
    along_y = [
        ("fsdp", [(i, i // per_band * per_band + (i + h) % per_band) for i in range(shards)])
        for h in range(1, per_band)
    ]
    along_z = [
        ("fsdp", [(i, (i + h * per_band) % shards) for i in range(shards)])
        for h in range(1, bands)
    ]
    parts = sum_over_replicas(place, replica_grads[0], bands)
    prepared = prepare(left_basis[0], right_basis[0], first_moment[0])
    parts, prepared = lax.optimization_barrier((parts, prepared))
    sums = finish(place, *parts, bands)
    rows, width = sums[0].shape[0], sums[0].shape[1] - LANES
    cols = width // n
    entries = rows_dev * shards * replica_grads.shape[2]
    spread = exchange(sums, along_z)
    out = [
        jax.ShapeDtypeStruct((shards * slots, rows, n), bf16),
        jax.ShapeDtypeStruct((8, LANES), f32),
    ]
    sent, square = local(dispatch_body, [table, *spread], out, "dispatch")
    sent = sent.reshape(shards, slots, rows, n)
    pieces = lax.all_to_all(sent, "fsdp", split_axis=0, concat_axis=0, tiled=True)
    for steps in (core, along_x):
        square = sum([lax.ppermute(square, *step) for step in steps], square)
    squares = [square] + [lax.ppermute(square, *step) for step in along_y]
    rotated = rotate(pieces, prepared, second_moment[0], bands)
    update, second_new = direction(
        owners, me, squares, rotated, prepared, second_moment[0], bands, shards, entries
    )
    back = lax.all_to_all(update, "fsdp", split_axis=0, concat_axis=0, tiled=True)
    back, pieces = lax.optimization_barrier((back, pieces))
    new = factors(
        owners, me, squares, pieces, left_factor[0], right_factor[0], first_moment[0], bands, entries
    )
    left_new, right_new, first_new = new
    out = [jax.ShapeDtypeStruct((rows, width), bf16)] * bands
    mine = local(collect_body, [table, back.reshape(shards * slots, rows, n)], out, "collect")
    out = jax.ShapeDtypeStruct((bands, rows, width), bf16)
    result = local(put_body, [table, *exchange(mine, along_z)], out, "put").reshape(rows_dev, width)
    return (result, left_new[None], right_new[None], first_new[None], second_new[None])


def solution(mesh):
    state = P("dp", "fsdp", None, None)
    return jax.shard_map(
        per_device,
        mesh=mesh,
        in_specs=(P("dp", "fsdp", None), P("dp", None)) + (state,) * 6,
        out_specs=(P("fsdp", "dp"),) + (state,) * 4,
        check_vma=False,
    )
```

```python
import jax
import jax.numpy as jnp
from jax import lax
from jax.experimental import pallas as pl
from jax.experimental.pallas import tpu as pltpu
from jax.sharding import PartitionSpec as P

f32 = jnp.float32
bf16 = jnp.bfloat16
SMEM = pltpu.MemorySpace.SMEM
VMEM = pltpu.MemorySpace.VMEM
HBM = pltpu.MemorySpace.HBM
LANES = 128


def in_hbm(*arrays):
    return [pltpu.with_memory_space_constraint(a, HBM) for a in arrays]


def split3(value):
    head, rest = split(value)
    mid, tail = split(value - head.astype(f32))
    return head, mid, tail


def split(value):
    head = value.astype(bf16)
    return head, (value - head.astype(f32)).astype(bf16)


def mm(a, b, dims=((1,), (0,))):
    return lax.dot_general(a, b, (dims, ((), ())), preferred_element_type=f32)


def tiles(count, size=32):
    return [slice(r, r + size) for r in range(0, count, size)]


def prepare_body(
    left_src, right_src, first_src, lt_dst, l_dst, r_dst, rot_dst, *scratch
):
    left, right, first, lt, low, head, rot, lt_both, half, tail, product, sems, out_sems = scratch
    slots, n, _ = left.shape
    pairs = ((left_src, left), (first_src, first), (right_src, right))
    copies = [
        [
            pltpu.make_async_copy(src.at[s], dst.at[s], sems.at[s, i])
            for i, (src, dst) in enumerate(pairs)
        ]
        for s in range(slots)
    ]
    for group in copies:
        for c in group:
            c.start()
    pairs = ((lt, lt_dst), (low, l_dst), (head, r_dst), (rot, rot_dst))
    outs = [
        [
            pltpu.make_async_copy(src.at[s], dst.at[s], out_sems.at[s, i])
            for i, (src, dst) in enumerate(pairs)
        ]
        for s in range(slots)
    ]
    for s in range(slots):
        copies[s][0].wait()
        for rows in tiles(n, LANES):
            above, below = split(left[s, rows].T)
            lt[s, :, rows] = above
            lt_both[:n, rows] = above
            lt_both[n:, rows] = below
        outs[s][0].start()
        for rows in tiles(n):
            low[s, rows] = left[s, rows].astype(bf16)
        outs[s][1].start()
        copies[s][1].wait()
        for rows in tiles(n):
            half[rows] = first[s, rows].astype(bf16)
        product[...] = mm(lt_both[...], half[...])
        copies[s][2].wait()
        for rows, more in zip(tiles(n), tiles(2 * n)[n // 32 :]):
            half[rows] = (product[rows] + product[more]).astype(bf16)
            head[s, rows], tail[rows] = split(right[s, rows])
        outs[s][2].start()
        turned = mm(half[...], head[s]) + mm(half[...], tail[...])
        rot[s] = (0.9 * turned).astype(bf16)
        outs[s][3].start()
    for group in outs:
        for c in group:
            c.wait()


def prepare(left_basis, right_basis, first_moment):
    slots, n, _ = left_basis.shape
    far = pl.BlockSpec(memory_space=HBM)
    return pl.pallas_call(
        prepare_body,
        in_specs=[far] * 3,
        out_specs=[far] * 4,
        out_shape=[HBM((slots, n, n), bf16)] * 4,
        scratch_shapes=[pltpu.VMEM((slots, n, n), f32)] * 3
        + [pltpu.VMEM((slots, n, n), bf16)] * 4
        + [
            pltpu.VMEM((2 * n, n), bf16),
            pltpu.VMEM((n, n), bf16),
            pltpu.VMEM((n, n), bf16),
            pltpu.VMEM((2 * n, n), f32),
            pltpu.SemaphoreType.DMA((slots, 3)),
            pltpu.SemaphoreType.DMA((slots, 4)),
        ],
        compiler_params=pltpu.CompilerParams(vmem_limit_bytes=24 << 20),
        cost_estimate=pl.CostEstimate(
            flops=slots * 8 * n**3, bytes_accessed=slots * 22 * n * n, transcendentals=0
        ),
        name="prepare",
    )(*in_hbm(left_basis, right_basis, first_moment))


def local(body, arrays, out_shape, name, limit=8 << 20, cost=None):
    return pl.pallas_call(
        body,
        in_specs=[pl.BlockSpec(memory_space=SMEM)]
        + [pl.BlockSpec(memory_space=VMEM)] * (len(arrays) - 1),
        out_specs=jax.tree.map(
            lambda _: pl.BlockSpec(memory_space=VMEM), out_shape, is_leaf=lambda o: hasattr(o, "shape")
        ),
        out_shape=out_shape,
        compiler_params=pltpu.CompilerParams(vmem_limit_bytes=limit),
        cost_estimate=cost,
        name=name,
    )(*arrays)


def dispatch_body(table, *refs):
    *srcs, dst, square = refs
    n = dst.shape[2]
    bands = len(srcs)
    width = srcs[0].shape[1] - LANES
    cols = width // n
    z = table[0, bands * cols]
    total = jnp.zeros(square.shape, f32)
    for j, src in enumerate(srcs):
        band = lax.rem(z + bands - j, bands)
        for c in range(cols):
            dst[table[0, band * cols + c]] = src[:, c * n : (c + 1) * n]
        terms = src[:, width:].astype(f32)
        for t in range(3):
            total = total + terms[8 * t : 8 * t + 8]
    square[...] = total


def collect_body(table, src, *dsts):
    n = src.shape[2]
    bands = len(dsts)
    cols = dsts[0].shape[1] // n
    z = table[0, bands * cols]
    for j, dst in enumerate(dsts):
        band = lax.rem(z + j, bands)
        for c in range(cols):
            dst[:, c * n : (c + 1) * n] = src[table[0, band * cols + c]]


def put_body(table, *refs):
    *srcs, dst = refs
    bands = len(srcs)
    z = table[0, table.shape[1] - 1]
    for j, src in enumerate(srcs):
        dst[lax.rem(z + bands - j, bands)] = src[...]


def load(place, grads, width):
    rows, columns = grads.shape
    chips = columns // width // 2
    groups = ((2,), (1, 3, 0))

    def body(place, src, *refs):
        *dsts, sems = refs
        copies = []
        for i, dst in enumerate(dsts):
            core = 1 - place[1] if i < 2 else place[1]
            for k, j in enumerate(groups[i % 2]):
                slab = 2 * lax.rem(place[0] + j, chips) + core
                columns = pl.ds(pl.multiple_of(slab * width, width), width)
                copies.append(
                    pltpu.make_async_copy(src.at[:, columns], dst.at[k], sems.at[len(copies)])
                )
        for c in copies:
            c.start()
        for c in copies:
            c.wait()

    return pl.pallas_call(
        body,
        in_specs=[pl.BlockSpec(memory_space=SMEM), pl.BlockSpec(memory_space=HBM)],
        out_specs=[pl.BlockSpec(memory_space=VMEM)] * 4,
        out_shape=[VMEM((len(g), rows, width), bf16) for g in groups * 2],
        scratch_shapes=[pltpu.SemaphoreType.DMA((2 * chips,))],
        compiler_params=pltpu.CompilerParams(vmem_limit_bytes=2 << 20),
        name="load",
    )(place, *in_hbm(grads))


def pair(body, place, near, far, outs, name):
    low = near.shape[1] // 2

    def run(place, near, far, *outs):
        def total(i, a):
            part = slice(a * low, (a + 1) * low)
            return near[i, part].astype(f32) + far[i, part].astype(f32)

        body(total, low, *outs)

    out = [jax.ShapeDtypeStruct(shape, kind) for shape, kind in outs]
    return local(run, [place, near, far], out, name)


def far_body(total, low, to_right, to_left):
    to_right[...] = total(0, 0).astype(bf16)
    to_left[...] = total(0, 1).astype(bf16)


def near_body(total, low, to_right, to_left, keep_right, keep_left, own):
    keep_right[...] = total(0, 0)
    to_right[...] = total(0, 1).astype(bf16)
    to_left[...] = total(1, 0).astype(bf16)
    keep_left[...] = total(1, 1)
    for a in range(2):
        own[a * low : (a + 1) * low] = total(2, a)


def relay(place, kept, arrived):
    def body(place, kept, arrived, out):
        out[...] = (kept[...] + arrived[...].astype(f32)).astype(bf16)

    out = jax.ShapeDtypeStruct(kept.shape, bf16)
    return local(body, (place, kept, arrived), out, "relay")


def direct_body(place, own, left_direct, right_direct, out):
    low = left_direct.shape[0]
    out[:low] = own[:low] + right_direct[...].astype(f32)
    out[low:] = own[low:] + left_direct[...].astype(f32)


def finish(place, own, left_sum, right_sum, bands):
    rows, width = own.shape
    low = rows // 2
    piece = rows // bands

    def body(place, own, left_sum, right_sum, *outs):
        total = jnp.zeros((8, LANES), f32)
        for q in range(bands):
            relayed = left_sum if q * piece < low else right_sum
            part = slice(q * piece % low, q * piece % low + piece)
            value = own[q * piece : (q + 1) * piece] + relayed[part].astype(f32)
            step = lax.rem(q - place[2] + bands, bands)
            rounded = value.astype(bf16)
            for j in range(bands):

                @pl.when(step == j)
                def _():
                    outs[j][:, :width] = rounded

            by_row = jnp.sum((value * value).reshape(piece // 8, 8, width), axis=0)
            for c in range(width // LANES):
                total = total + by_row[:, c * LANES : (c + 1) * LANES]
        terms = [t.astype(f32) for t in split3(total)]
        terms.append(jnp.zeros((piece - 24, LANES), f32))
        terms = jnp.concatenate(terms, axis=0).astype(bf16)
        for out in outs:
            out[:, width:] = terms

    arrays = [place, own, left_sum, right_sum]
    out = [jax.ShapeDtypeStruct((piece, width + LANES), bf16)] * bands
    return local(body, arrays, out, "finish", 12 << 20)


def sum_over_replicas(place, grads, bands):
    size = lax.axis_size("dp")
    rows, columns = grads.shape
    width = columns // size
    half = (rows // 2, width)
    swap = [(d, d ^ 1) for d in range(size)]
    up = [(d, (d + 2) % size) for d in range(size)]
    down = [(d, (d - 2) % size) for d in range(size)]
    far_there, near_there, far_here, near_here = load(place, grads, width)
    other = lax.ppermute(far_there, "dp", swap)
    other, near_there = lax.optimization_barrier((other, near_there))
    others = lax.ppermute(near_there, "dp", swap)
    to_right, to_left = pair(far_body, place, far_here, other, [(half, bf16)] * 2, "pair_far")
    left_far = lax.ppermute(to_right, "dp", up)
    right_far = lax.ppermute(to_left, "dp", down)
    outs = [(half, bf16)] * 2 + [(half, f32)] * 2 + [((rows, width), f32)]
    to_right, to_left, keep_right, keep_left, own = pair(
        near_body, place, near_here, others, outs, "pair_near"
    )
    left_direct = lax.ppermute(to_right, "dp", up)
    right_direct = lax.ppermute(to_left, "dp", down)
    left_sum = lax.ppermute(relay(place, keep_right, left_far), "dp", up)
    right_sum = lax.ppermute(relay(place, keep_left, right_far), "dp", down)
    out = jax.ShapeDtypeStruct((rows, width), f32)
    own = local(direct_body, [place, own, left_direct, right_direct], out, "direct", cost=pl.CostEstimate(flops=2 * rows * width, bytes_accessed=12 * rows * width, transcendentals=0))
    return own, left_sum, right_sum


def exchange(arrays, steps):
    order = sorted(range(1, len(arrays)), key=lambda j: -min(j, len(arrays) - j))
    got = {0: arrays[0]}
    for j in order:
        got[j] = lax.ppermute(arrays[j], *steps[j - 1])
    return [got[j] for j in range(len(arrays))]


def assemble(pieces, slot, bands):
    per = pieces.shape[0] // bands
    return jnp.concatenate(
        [pieces[z * per + y, slot] for y in range(per) for z in range(bands)], axis=0
    )


def is_named(table, slot):
    named = table[0, 0] == slot
    for b in range(1, table.shape[1]):
        named = jnp.logical_or(named, table[0, b] == slot)
    return named


def clip_of(squares, entries):
    total = squares[0][...]
    for square in squares[1:]:
        total = total + square[...]
    total = jnp.sum(jnp.sum(total, axis=0, keepdims=True), axis=1, keepdims=True)
    return jnp.minimum(1.0, 1.0 / jnp.sqrt(total / entries + 1e-06))


def rotate(pieces, prepared, second, bands):
    slots, n, _ = second.shape

    def body(pieces, lt_src, l_src, r_src, rot_src, old_src, *refs):
        out, left, right, rot, old, lt, half, sems = refs
        pairs = ((lt_src, lt), (r_src, right), (rot_src, rot), (old_src, old), (l_src, left))
        copies = [
            pltpu.make_async_copy(src.at[s], dst.at[s], sems.at[s, i])
            for s in range(slots)
            for i, (src, dst) in enumerate(pairs)
        ]
        for c in copies:
            c.start()
        for s in range(slots):
            group = copies[s * len(pairs) : (s + 1) * len(pairs)]
            block = assemble(pieces, s, bands)
            group[0].wait()
            half[...] = mm(lt[s], block).astype(bf16)
            group[1].wait()
            out[s] = mm(half[...], right[s])
            for c in group[2:]:
                c.wait()

    whole = pl.BlockSpec(memory_space=VMEM)
    far = pl.BlockSpec(memory_space=HBM)
    return pl.pallas_call(
        body,
        in_specs=[whole] + [far] * 5,
        out_specs=[whole] * 5,
        out_shape=[
            VMEM((slots, n, n), f32),
            VMEM((slots, n, n), bf16),
            VMEM((slots, n, n), bf16),
            VMEM((slots, n, n), bf16),
            VMEM((slots, n, n), f32),
        ],
        scratch_shapes=[
            pltpu.VMEM((slots, n, n), bf16),
            pltpu.VMEM((n, n), bf16),
            pltpu.SemaphoreType.DMA((slots, 5)),
        ],
        compiler_params=pltpu.CompilerParams(vmem_limit_bytes=12 << 20),
        name="rotate",
    )(pieces, *in_hbm(*prepared, second))


def direction(table, me, squares, rotated, bands, senders, entries):
    slots, n, _ = rotated[0].shape
    rows = n // senders
    per = senders // bands

    def body(table, me, *refs):
        squares, rest = refs[: len(refs) - 11], refs[len(refs) - 11 :]
        product, left, right, rot, old, out, second_out, new, step, half, sems = rest
        scale = clip_of(squares, entries)
        for s in range(slots):
            named = is_named(table, me[0] * slots + s)
            for r in tiles(n):
                turned = product[s, r] * scale
                before = old[s, r]
                value = 0.95 * before + 0.05 * turned * turned
                new[s, r] = jnp.where(named, value, before)
                ahead = rot[s, r].astype(f32) + 0.1 * turned
                step[r] = (ahead * pl.reciprocal(jnp.sqrt(value) + 1e-08, approx=True)).astype(bf16)
            pltpu.make_async_copy(new.at[s], second_out.at[s], sems.at[s]).start()
            half[...] = mm(left[s], step[...]).astype(bf16)
            update = mm(half[...], right[s], ((1,), (1,))).astype(bf16)
            for y in range(per):
                for z in range(bands):
                    row = (y * bands + z) * rows
                    out[z * per + y, s] = update[row : row + rows]
        for s in range(slots):
            pltpu.make_async_copy(new.at[s], second_out.at[s], sems.at[s]).wait()

    scalar = pl.BlockSpec(memory_space=SMEM)
    whole = pl.BlockSpec(memory_space=VMEM)
    return pl.pallas_call(
        body,
        in_specs=[scalar] * 2 + [whole] * (len(squares) + 5),
        out_specs=[whole, pl.BlockSpec(memory_space=HBM)],
        out_shape=[
            jax.ShapeDtypeStruct((senders, slots, rows, n), bf16),
            HBM((slots, n, n), f32),
        ],
        scratch_shapes=[
            pltpu.VMEM((slots, n, n), f32),
            pltpu.VMEM((n, n), bf16),
            pltpu.VMEM((n, n), bf16),
            pltpu.SemaphoreType.DMA((slots,)),
        ],
        compiler_params=pltpu.CompilerParams(vmem_limit_bytes=16 << 20),
        name="direction",
    )(table, me, *squares, *rotated)


def factors_body(bands, entries, table, me, *refs):
    *squares, pieces = refs[:-16]
    sources, outs, news, olds = (refs[i : i + 3] for i in range(-16, -4, 3))
    block, product, *sems = refs[-4:]
    slots, n, _ = news[0].shape
    copies = [
        [
            pltpu.make_async_copy(src.at[s], dst.at[s], sems[0].at[s, i])
            for i, (src, dst) in enumerate(zip(sources, olds))
        ]
        for s in range(slots)
    ]
    for group in copies:
        for c in group:
            c.start()
    scale = clip_of(squares, entries)
    square = 0.1 * scale * scale
    done = []
    for s in range(slots):
        named = is_named(table, me[0] * slots + s)
        block[...] = assemble(pieces, s, bands)
        for i in range(3):
            if i == 0:
                product[...] = mm(block[...], block[...], ((1,), (1,)))
            elif i == 1:
                product[...] = mm(block[...].T, block[...])
            copies[s][i].wait()
            for r in tiles(n):
                old = olds[i][s, r]
                more = square * product[r] if i < 2 else (0.1 * scale) * block[r].astype(f32)
                news[i][s, r] = jnp.where(named, 0.9 * old + more, old)
            done.append(pltpu.make_async_copy(news[i].at[s], outs[i].at[s], sems[1].at[s, i]))
            done[-1].start()
    for c in done:
        c.wait()


def factors(table, me, squares, pieces, left, right, first, bands, entries):
    slots, n, _ = left.shape
    scalar = pl.BlockSpec(memory_space=SMEM)
    whole = pl.BlockSpec(memory_space=VMEM)
    far = pl.BlockSpec(memory_space=HBM)

    def body(*refs):
        factors_body(bands, entries, *refs)

    return pl.pallas_call(
        body,
        in_specs=[scalar] * 2 + [whole] * (len(squares) + 1) + [far] * 3,
        out_specs=[far] * 3,
        out_shape=[HBM(left.shape, f32)] * 3,
        scratch_shapes=[pltpu.VMEM((slots, n, n), f32)] * 6
        + [pltpu.VMEM((n, n), bf16), pltpu.VMEM((n, n), f32)]
        + [pltpu.SemaphoreType.DMA((slots, 3))] * 2,
        compiler_params=pltpu.CompilerParams(vmem_limit_bytes=24 << 20),
        cost_estimate=pl.CostEstimate(
            flops=slots * 4 * n**3, bytes_accessed=slots * 26 * n * n, transcendentals=0
        ),
        name="factors",
    )(table, me, *squares, pieces, *in_hbm(left, right, first))


def per_device(
    replica_grads,
    owners,
    left_factor,
    right_factor,
    left_basis,
    right_basis,
    first_moment,
    second_moment,
):
    rows_dev = replica_grads.shape[1]
    shards = lax.axis_size("fsdp")
    slots, n = left_factor.shape[1:3]
    per_band = n // rows_dev
    bands = shards // per_band
    dp = lax.axis_size("dp")
    dp_me = lax.axis_index("dp").astype(jnp.int32)
    me = lax.axis_index("fsdp").astype(jnp.int32)
    place = jnp.stack([dp_me // 2, dp_me % 2, me // per_band])
    table = jnp.concatenate([owners, (me // per_band).reshape(1, 1)], axis=1)
    me = me.reshape(1)
    core = [("dp", [(d, d ^ 1) for d in range(dp)])]
    along_x = [("dp", [(d, (d + 2 * h) % dp) for d in range(dp)]) for h in range(1, dp // 2)]
    along_y = [
        ("fsdp", [(i, i // per_band * per_band + (i + h) % per_band) for i in range(shards)])
        for h in range(1, per_band)
    ]
    along_z = [
        ("fsdp", [(i, (i + h * per_band) % shards) for i in range(shards)])
        for h in range(1, bands)
    ]
    parts = sum_over_replicas(place, replica_grads[0], bands)
    prepared = prepare(left_basis[0], right_basis[0], first_moment[0])
    parts, prepared = lax.optimization_barrier((parts, prepared))
    sums = finish(place, *parts, bands)
    rows, width = sums[0].shape[0], sums[0].shape[1] - LANES
    cols = width // n
    entries = rows_dev * shards * replica_grads.shape[2]
    spread = exchange(sums, along_z)
    out = [
        jax.ShapeDtypeStruct((shards * slots, rows, n), bf16),
        jax.ShapeDtypeStruct((8, LANES), f32),
    ]
    sent, square = local(dispatch_body, [table, *spread], out, "dispatch")
    sent = sent.reshape(shards, slots, rows, n)
    pieces = lax.all_to_all(sent, "fsdp", split_axis=0, concat_axis=0, tiled=True)
    for steps in (core, along_x):
        square = sum([lax.ppermute(square, *step) for step in steps], square)
    squares = [square] + [lax.ppermute(square, *step) for step in along_y]
    rotated = rotate(pieces, prepared, second_moment[0], bands)
    update, second_new = direction(owners, me, squares, rotated, bands, shards, entries)
    back = lax.all_to_all(update, "fsdp", split_axis=0, concat_axis=0, tiled=True)
    back, pieces = lax.optimization_barrier((back, pieces))
    new = factors(
        owners, me, squares, pieces, left_factor[0], right_factor[0], first_moment[0], bands, entries
    )
    left_new, right_new, first_new = new
    out = [jax.ShapeDtypeStruct((rows, width), bf16)] * bands
    mine = local(collect_body, [table, back.reshape(shards * slots, rows, n)], out, "collect")
    out = jax.ShapeDtypeStruct((bands, rows, width), bf16)
    result = local(put_body, [table, *exchange(mine, along_z)], out, "put").reshape(rows_dev, width)
    return (result, left_new[None], right_new[None], first_new[None], second_new[None])


def solution(mesh):
    state = P("dp", "fsdp", None, None)
    return jax.shard_map(
        per_device,
        mesh=mesh,
        in_specs=(P("dp", "fsdp", None), P("dp", None)) + (state,) * 6,
        out_specs=(P("fsdp", "dp"),) + (state,) * 4,
        check_vma=False,
    )
```
